512 devices in a mesh: vol: 128 (over x, z_hi, y, core), rep: 4 (over z_lo).
Axes of the slice: x: 4, y: 8, z: 8 (z_hi: 2, z_lo: 4; z = z_hi * 4 + z_lo), core: 2. Of those that a mesh axis runs over, the one named last changes fastest.
Arguments:
- displacement: float32 [3, 4, 512, 32, 128], P(None, None, 'vol', 'rep'), may hold values from -6 to 6
- body_force: float32 [3, 4, 512, 32, 128], P(None, None, 'vol', 'rep'), may hold values from -12 to 12
- stiffness: float32 [512, 32, 128], P('vol', 'rep'), may hold values from 0.5 to 4
- wet_cell: int32 [512, 128], P(('vol', 'rep')), may hold values from 0 to 4095, as said below
- wet_normal: float32 [3, 65536], P(None, ('vol', 'rep')), may hold values from -6 to 6
- route: int32 [65536, 1], P(('vol', 'rep')), may hold values from 0 to 127; in each aligned block of 128 rows (0 to 127, 128 to 255, ...) at most 2 rows name the same one
- tile_u: bfloat16 [16384, 32, 256], P(('vol', 'rep')), may hold values from -0.1875 to 0.1875
- tile_v: bfloat16 [16384, 32, 256], P(('vol', 'rep')), may hold values from -0.375 to 0.375
- tile_row: int32 [16384], P(('vol', 'rep')), may hold values from 0 to 3
- tile_col: int32 [16384], P(('vol', 'rep')), may hold values from 0 to 127
- tile_rank: int32 [16384], P(('vol', 'rep')), may hold values from 16 to 32
Outputs:
- updated: float32 [3, 4, 512, 32, 128], P(None, None, 'vol', 'rep')
- pressure: float32 [4, 131072], P(None, ('vol', 'rep'))
- wet_pressure: float32 [4, 65536], P(None, ('vol', 'rep'))
The draws below stay inside these ranges and needn't reach their ends.
Inputs may be any that keep to these rules, and one draw needn't show every extreme that they name: `wet_cell`: the cells in a row are distinct. `route`: no partition routes more than 2 of its unknowns to one owner; some partition routes exactly 2.
All inputs are finite; a program needn't handle non-finite values.
Results may differ from the reference program's by a relative error of at most 0.015.
Values may be sent and summed in bfloat16 or wider, within the bound.
A program may use at most 64 MiB of HBM per device.

```python
import math
import jax
import jax.numpy as jnp
import numpy as np
from jax import lax

K_INC = 4
CX = 4
CY = 8
CZ = 128
ITERS = 3
SLOTS = 128
BS = 256
RANK = 32
TILES_DEV = 32
NX = 512
NY = 32
CAP = 2
REGION = 256
BPR = 1
N_VOL = 128
N_REP = 4
DEVICES = 512


def draw_wet_cell(key, part):
    key = jax.random.fold_in(key, 11)
    streams = jax.random.split(key, DEVICES)
    listed = jax.vmap(lambda single: jax.random.permutation(single, CX * CY * CZ)[:SLOTS])(streams)
    return listed.astype(jnp.int32)


def draw_tile_rank(key, part):
    key = jax.random.fold_in(key, 23)
    levels = jax.random.randint(key, (DEVICES * TILES_DEV,), RANK // 2, RANK + 1)
    return levels.at[::TILES_DEV].set(RANK).astype(jnp.int32)


def set_ends(array, key, low, largest):
    longest = array.shape.index(max(array.shape))
    spots = []
    for shift in (0, 1):
        where = [jax.random.randint(jax.random.fold_in(key, axis), (), 0, length) for axis, length in enumerate(array.shape)]
        where[longest] = (where[longest] + shift) % array.shape[longest]
        spots.append(tuple(where))
    return array.at[spots[0]].set(low).at[spots[1]].set(largest)


def level_of(own_key, extent, pieces, least, high):
    factor_of = 1.0
    for axis_at, parts in pieces:
        heights = jax.random.uniform(jax.random.fold_in(jax.random.fold_in(own_key, 6), axis_at), (parts,), jnp.float32, least / len(pieces), high / len(pieces))
        factor_of = factor_of * jnp.repeat(jnp.exp(heights), extent[axis_at] // parts).reshape((-1,) + (1,) * (len(extent) - 1 - axis_at))
    return factor_of


def routed_block(rng, own, number, rows, amount, top, limit, lean):
    sequence = jax.random.permutation(rng, amount)
    heavy_load, usual = shares(amount, rows * top, limit, lean, True), shares(amount, rows * top, limit, lean, False)
    places = jnp.arange(amount)

    def named(sizes, offset_by):
        used = int((sizes > 0).sum())
        fixed = max(1, used // 4)
        passed = fixed + (places - fixed + offset_by * (used - fixed)) % max(1, amount - fixed)
        return jnp.zeros((amount,), jnp.int32).at[sequence[jnp.where(places < fixed, places, passed)]].set(jnp.asarray(sizes, jnp.int32))

    sizes = jnp.where(number % 4 == 0, named(heavy_load, number // 4), named(usual, number - number // 4 - 1))
    mixed = jax.random.permutation(jax.random.fold_in(own, 3), amount)
    source_of, receiver = mixed[0:amount // 2 * 2:2], mixed[1:amount // 2 * 2:2]
    margin = jnp.minimum(sizes[source_of] - 1, limit - sizes[receiver]) // 2
    margin = jnp.where((source_of == sequence[0]) | (receiver == sequence[0]) | (sizes[receiver] == 0), 0, jnp.maximum(margin, 0))
    passed = jax.random.randint(jax.random.fold_in(own, 4), (amount // 2,), 0, 1 << 20) % (margin + 1)
    sizes = sizes.at[source_of].add(-passed).at[receiver].add(passed)
    members = jnp.searchsorted(jnp.cumsum(sizes), jnp.arange(rows * top), side="right").astype(jnp.int32)
    listing = members.reshape(top, rows).T
    listing = listing[jax.random.permutation(jax.random.fold_in(own, 1), rows)]
    offset_by = jax.random.randint(jax.random.fold_in(own, 2), (rows, 1), 0, top)
    return jnp.take_along_axis(listing, (jnp.arange(top)[None, :] + offset_by) % top, axis=1)


def shares(count, total, most, lean, full):
    weights = [(1 << 20) // math.isqrt(rank ** lean) + 1 for rank in range(1, count + 1)]
    largest = most if full else min(most, max(-(-total // count), total * weights[0] // sum(weights)))
    least = 1 if total - largest >= count - 1 else 0
    holding, rest = [largest] + [least] * (count - 1), total - largest - least * (count - 1)
    while rest > 0:
        candidates = [i for i in range(1, count) if holding[i] < largest] or [i for i in range(1, count) if holding[i] < most]
        mass, budget = sum([weights[i] for i in candidates]), rest
        for i in candidates:
            extra = min(most - holding[i], max(1, budget * weights[i] // mass), rest)
            holding[i] = holding[i] + extra
            rest = rest - extra
    return np.array(holding)


def centred(key, extent, scale, most, cuts=(), kind=jnp.bfloat16):
    loudness = level_of(key, extent, cuts, -0.22, 0.18) if cuts else 1.0
    array = jax.random.normal(key, extent, jnp.float32) * scale * loudness
    return jnp.minimum(jnp.maximum(array, -most), most).astype(kind)


def setup_inputs(seed: int = 0) -> dict:
    arg_keys = jax.random.split(jax.random.key(seed), 12)
    displacement = centred(arg_keys[0], (3, K_INC, NX, NY, CZ), 1.0, 6.0, ((2, 128), (3, 4)), jnp.float32)
    body_force = centred(arg_keys[1], (3, K_INC, NX, NY, CZ), 2.0, 12.0, ((2, 128), (3, 4)), jnp.float32)
    stiffness = jnp.clip(jnp.exp(math.log(4.0) - 2.0794415 * jax.random.uniform(arg_keys[2], (NX, NY, CZ), jnp.float32) ** level_of(arg_keys[2], (NX, NY, CZ), ((0, 128), (1, 4)), -0.2, 0.2)), 0.5, 4.0)
    wet_cell = draw_wet_cell(jax.random.fold_in(arg_keys[11], 71), 0)
    wet_normal = centred(arg_keys[4], (3, DEVICES * SLOTS), 1.0, 6.0, ((1, 512),), jnp.float32)
    route_keys = jax.random.split(jax.random.fold_in(arg_keys[5], 1), (DEVICES * SLOTS) // SLOTS)
    route_turns = jax.random.permutation(jax.random.fold_in(arg_keys[5], 3), (DEVICES * SLOTS) // SLOTS)
    route = jax.vmap(lambda own, number: routed_block(jax.random.fold_in(arg_keys[5], 2), own, number, SLOTS, N_VOL, 1, CAP, 2))(route_keys, route_turns).reshape((DEVICES * SLOTS, 1))
    tile_u = centred(arg_keys[6], (DEVICES * TILES_DEV, RANK, BS), (RANK * max(1, TILES_DEV // BPR)) ** -0.5, 0.1875, ((0, 512),))
    tile_v = centred(arg_keys[7], (DEVICES * TILES_DEV, RANK, BS), BS ** -0.5, 0.375, ((0, 512),))
    tile_row = set_ends(jax.random.randint(arg_keys[8], (DEVICES * TILES_DEV,), 0, N_REP * BPR), jax.random.fold_in(arg_keys[8], 1), 0, (N_REP * BPR) - 1).astype(jnp.int32)
    tile_col = set_ends(jax.random.randint(arg_keys[9], (DEVICES * TILES_DEV,), 0, N_VOL * BPR), jax.random.fold_in(arg_keys[9], 1), 0, (N_VOL * BPR) - 1).astype(jnp.int32)
    tile_rank = draw_tile_rank(jax.random.fold_in(arg_keys[11], 71), 0)
    return dict(displacement=displacement, body_force=body_force, stiffness=stiffness, wet_cell=wet_cell, wet_normal=wet_normal, route=route, tile_u=tile_u, tile_v=tile_v, tile_row=tile_row, tile_col=tile_col, tile_rank=tile_rank)


relax_factor = 0.8
mass_shift = 1.0


def neighbour_sum(volume):
    padded = jnp.pad(volume, ((0, 0), (0, 0), (1, 1), (1, 1), (1, 1)))
    summed = padded[:, :, 2:, 1:-1, 1:-1] + padded[:, :, :-2, 1:-1, 1:-1]
    summed = summed + padded[:, :, 1:-1, 2:, 1:-1] + padded[:, :, 1:-1, :-2, 1:-1]
    return summed + padded[:, :, 1:-1, 1:-1, 2:] + padded[:, :, 1:-1, 1:-1, :-2]


def relax(volume, force, stiffness):
    diagonal = mass_shift + 6.0 * stiffness
    coupling = stiffness / diagonal
    return volume + relax_factor * (force / diagonal - volume + coupling * neighbour_sum(volume))


def to_blocks(volume):
    shaped = volume.reshape(3, K_INC, N_VOL, CX, N_REP, CY, CZ)
    return shaped.transpose(2, 4, 0, 1, 3, 5, 6).reshape(DEVICES, 3, K_INC, CX * CY * CZ)


def from_blocks(blocks):
    shaped = blocks.reshape(N_VOL, N_REP, 3, K_INC, CX, CY, CZ)
    return shaped.transpose(2, 3, 0, 4, 1, 5, 6).reshape(3, K_INC, N_VOL * CX, N_REP * CY, CZ)


def slot_order(destination, owner_count):
    indicator = (destination[:, None] == jnp.arange(owner_count, dtype=jnp.int32)[None, :]).astype(jnp.int32)
    earlier = jnp.cumsum(indicator, axis=0) - indicator
    return jnp.sum(earlier * indicator, axis=1).astype(jnp.int32)


def reference(displacement, body_force, stiffness, wet_cell, wet_normal, route, tile_u, tile_v, tile_row, tile_col, tile_rank):
    volume = displacement
    for iteration in range(ITERS):
        volume = relax(volume, body_force, stiffness)
    blocks = to_blocks(volume)
    picked = jnp.take_along_axis(blocks, wet_cell[:, None, None, :], axis=3)
    normals = wet_normal.reshape(3, DEVICES, SLOTS).transpose(1, 0, 2)
    traces = jnp.sum(normals[:, :, None, :] * picked, axis=1).astype(jnp.bfloat16)
    destination = route[:, 0].reshape(DEVICES, SLOTS)
    arrival = lax.map(lambda entries: slot_order(entries, N_VOL), destination)
    device = jnp.arange(DEVICES, dtype=jnp.int32)[:, None]
    target = (destination * N_REP + device % N_REP) * REGION + (device // N_REP) * CAP + arrival
    flat_target = target.reshape(-1).astype(jnp.int32)
    surface = jnp.zeros((K_INC, DEVICES * REGION), jnp.bfloat16)
    surface = surface.at[:, flat_target].set(traces.transpose(1, 0, 2).reshape(K_INC, DEVICES * SLOTS))
    x_blocks = surface.reshape(K_INC, DEVICES * BPR, BS)

    def one_device(carry, index):
        offset = index * TILES_DEV
        u_part = lax.dynamic_slice_in_dim(tile_u, offset, TILES_DEV, 0).astype(jnp.float32)
        v_part = lax.dynamic_slice_in_dim(tile_v, offset, TILES_DEV, 0).astype(jnp.float32)
        rows = lax.dynamic_slice_in_dim(tile_row, offset, TILES_DEV, 0)
        columns = lax.dynamic_slice_in_dim(tile_col, offset, TILES_DEV, 0)
        levels = lax.dynamic_slice_in_dim(tile_rank, offset, TILES_DEV, 0)
        owner = index // N_REP
        quarter = index % N_REP
        global_col = (((columns // BPR) * N_REP + quarter) * BPR + columns % BPR).astype(jnp.int32)
        chosen = jnp.take(x_blocks, global_col, axis=1).astype(jnp.float32)
        coefficient = jnp.einsum('ktb,trb->tkr', chosen, v_part, precision=lax.Precision.HIGHEST)
        retained = jnp.arange(RANK, dtype=jnp.int32)[None, :] < levels[:, None]
        coefficient = jnp.where(retained[:, None, :], coefficient, 0.0).astype(jnp.bfloat16)
        coefficient = lax.optimization_barrier(coefficient).astype(jnp.float32)
        contrib = jnp.einsum('tkr,trb->tkb', coefficient, u_part, precision=lax.Precision.HIGHEST)
        global_row = (owner * N_REP * BPR + rows).astype(jnp.int32)
        carry = carry.at[:, global_row, :].add(contrib.transpose(1, 0, 2))
        return carry, None

    start_sum = jnp.zeros((K_INC, DEVICES * BPR, BS), jnp.float32)
    summed_blocks, unused = lax.scan(one_device, start_sum, jnp.arange(DEVICES, dtype=jnp.int32))
    pressure = summed_blocks.reshape(K_INC, DEVICES * REGION)
    wet_pressure = pressure.astype(jnp.bfloat16)[:, flat_target].astype(jnp.float32)
    per_device = wet_pressure.reshape(K_INC, DEVICES, SLOTS).transpose(1, 0, 2)
    loads = -normals[:, :, None, :] * per_device[:, None, :, :]

    def place_load(cells, values):
        return jnp.zeros((3, K_INC, CX * CY * CZ), jnp.float32).at[:, :, cells].set(values)

    load_field = from_blocks(jax.vmap(place_load)(wet_cell, loads))
    updated = relax(volume, body_force + load_field, stiffness)
    return (updated, pressure, wet_pressure)
```

```python
import jax
import jax.numpy as jnp
from jax import lax
from jax.experimental import pallas as pl
from jax.experimental.pallas import tpu as pltpu
from jax.sharding import PartitionSpec as P

MESH = pl.DeviceIdType.MESH
relax_factor = 0.8
mass_shift = 1.0

F32 = jnp.float32
BF16 = jnp.bfloat16
I32 = jnp.int32

NX, NZH, NY, NC = 4, 2, 8, 2
NR = 4
NHI = NX * NZH
NLO = NY * NC
NV = NHI * NLO
SLOTS = 128
COMP = 12
TILES, RANK = 32, 32
TQ = TILES * RANK

NT = (((1,), (1,)), ((), ()))


def dot(a, b):
    return jnp.dot(a, b, preferred_element_type=F32)


def dot_nt(a, b):
    return lax.dot_general(a, b, NT, preferred_element_type=F32)


def iota(shape, dim):
    return lax.broadcasted_iota(I32, shape, dim)


def onehot(condition, dtype=BF16):
    return jnp.where(condition, 1.0, 0.0).astype(F32).astype(dtype)


def pairs(tiles):
    lead = 1
    for size in tiles.shape[:-2]:
        lead *= size
    return tiles.reshape(lead // 2, 16, 128).astype(BF16)


def unpairs(tiles, lead):
    return tiles.astype(F32).reshape(*lead, 8, 128)


def neighbours(inner, low, high):
    rows = inner.shape[1]
    lane = iota(inner.shape, 2)
    total = low + high
    total = total + pltpu.roll(inner, 1, 1) + pltpu.roll(inner, rows - 1, 1)
    total = total + jnp.where(lane == 0, 0.0, pltpu.roll(inner, 1, 2))
    return total + jnp.where(lane == 127, 0.0, pltpu.roll(inner, 127, 2))


def body(
    disp, force, stiff, wcell, wnorm, route, tu_any, tv_any, trow, tcol, trank,
    out_u, out_p, out_w,
    tu, tv, vol_s, vol_r, rep_s, rep_r, cor_s, cor_r, fvol_s, fvol_r, frep_s, frep_r,
    w_ext, f_ext, c_ext, field, base, scale,
    vdt, ud, ol, rowhot, armask, place, sel_t, diag_m, row_m, sel_lo, lo_hot, ha_hot,
    ra, g, zs, zr, xb, ws, wr,
    load_sem, halo_ss, halo_rs, fhalo_ss, fhalo_rs, ph_ss, ph_rs,
):
    v = lax.axis_index("vol")
    r = lax.axis_index("rep")
    hi, lo = v // NLO, lax.rem(v, NLO)
    x, zh = hi // NZH, lax.rem(hi, NZH)
    y, c = lo // NC, lax.rem(lo, NC)

    def vol_of(x_, zh_, y_, c_):
        return ((x_ * NZH + zh_) * NY + y_) * NC + c_

    hi_peers = [(lax.rem(hi + j, NHI) * NLO + lo, r) for j in range(1, NHI)]
    y_peers = [(vol_of(x, zh, lax.rem(y + j, NY), c), r) for j in range(1, NY)]
    core_peer = (vol_of(x, zh, y, 1 - c), r)
    lo_at = [lax.rem(lo + j, NLO) for j in range(1, NLO)]
    lo_peers = [(hi * NLO + at, r) for at in lo_at]
    x_peers = [(vol_of(lax.rem(x + j, NX), zh, y, c), r) for j in range(1, NX)]
    z_at = [(zh, lax.rem(r + j, NR)) for j in range(1, NR)] + [(1 - zh, lax.rem(r + j, NR)) for j in range(NR)]
    z_peers = [(vol_of(x, zh_, y, c), r_) for zh_, r_ in z_at]
    up_v, down_v = lax.rem(v + 1, NV), lax.rem(v + NV - 1, NV)
    up_r, down_r = lax.rem(r + 1, NR), lax.rem(r + NR - 1, NR)
    halo_peers = [(up_v, r), (down_v, r)] + [(a, b) for a in (up_v, down_v) for b in (up_r, down_r)]

    barrier = pltpu.get_barrier_semaphore()
    greeted = hi_peers + lo_peers + z_peers + halo_peers
    for peer in greeted:
        pl.semaphore_signal(barrier, inc=1, device_id=peer, device_id_type=MESH)

    load_u = pltpu.make_async_copy(tu_any, tu, load_sem.at[0])
    load_v = pltpu.make_async_copy(tv_any, tv, load_sem.at[1])
    load_u.start()
    load_v.start()

    row3 = iota((COMP, 4, 8, 128), 2)
    row_c = iota((COMP, 8, 128), 1)
    for side in (0, 1):
        first = 1 - side
        vol_s[side, 0:18] = pairs(disp[:, first:first + 3])
        vol_s[side, 18:30] = pairs(force[:, 2 - 2 * side:4 - 2 * side])
        vol_s[side, 30:31] = pairs(stiff[2 - 2 * side:4 - 2 * side])
    force_up = pltpu.roll(force[...].reshape(COMP * 4, 8, 128), 4, 1).reshape(COMP, 4, 8, 128)
    rep_s[0, 0:24] = pairs(jnp.where(row3 >= 5, disp[...], force_up))
    rep_s[1, 0:24] = pairs(jnp.where(row3 <= 2, disp[...], force_up))
    for side in (0, 1):
        rep_s[side, 24:26] = pairs(stiff[...])
        edge, second = (3, 2) if side == 0 else (0, 1)
        w_e, w_2, f_e = disp[:, edge], disp[:, second], force[:, edge]
        s_e = jnp.broadcast_to(stiff[edge:edge + 1], (COMP, 8, 128))
        w_2 = pltpu.roll(w_2, 4, 1)
        up = jnp.where(row_c >= 6, w_e, jnp.where(row_c == 3, w_2, jnp.where(row_c == 1, pltpu.roll(f_e, 2, 1), pltpu.roll(s_e, 1, 1))))
        down = jnp.where(row_c <= 1, w_e, jnp.where(row_c == 4, w_2, jnp.where(row_c == 6, pltpu.roll(f_e, 6, 1), pltpu.roll(s_e, 7, 1))))
        cor_s[side, 0] = pairs(up)
        cor_s[side, 1] = pairs(down)

    vol_to = [v < NV - 1, v > 0]
    vol_from = [v > 0, v < NV - 1]
    rep_to = [r < NR - 1, r > 0]
    rep_from = [r > 0, r < NR - 1]
    vol_dev, rep_dev = [up_v, down_v], [up_r, down_r]

    moves = []
    for s in (0, 1):
        moves.append((vol_s.at[s], vol_r.at[s], s, (vol_dev[s], r), vol_to[s], vol_from[s]))
    for s in (0, 1):
        for t in (0, 1):
            moves.append((cor_s.at[s, t], cor_r.at[s, t], 4 + 2 * s + t, (vol_dev[s], rep_dev[t]),
                          jnp.logical_and(vol_to[s], rep_to[t]), jnp.logical_and(vol_from[s], rep_from[t])))
    for t in (0, 1):
        moves.append((rep_s.at[t], rep_r.at[t], 2 + t, (v, rep_dev[t]), rep_to[t], rep_from[t]))

    def remote(src, dst, ss, rs, dev):
        return pltpu.make_async_remote_copy(src_ref=src, dst_ref=dst, send_sem=ss, recv_sem=rs, device_id=dev, device_id_type=MESH)

    for src, dst, at, dev, sends, comes in moves:
        @pl.when(jnp.logical_not(comes))
        def _():
            dst[...] = jnp.zeros(dst.shape, BF16)

    pl.semaphore_wait(barrier, len(greeted))

    for src, dst, at, dev, sends, comes in moves:
        @pl.when(sends)
        def _():
            remote(src, dst, halo_ss.at[at], halo_rs.at[at], dev).start()

    route_row = route[...]
    route_sq = jnp.broadcast_to(route_row, (SLOTS, SLOTS))
    route_col = jnp.transpose(route_sq.astype(F32)).astype(I32)
    sub = iota((SLOTS, SLOTS), 0)
    lane = iota((SLOTS, SLOTS), 1)
    earlier = jnp.where(jnp.logical_and(route_col == route_sq, sub < lane), 1.0, 0.0)
    arrival = jnp.sum(earlier, axis=0, keepdims=True).astype(I32)
    place[...] = onehot(sub == route_sq)
    armask[...] = jnp.where(iota((8, SLOTS), 0) // 4 == jnp.broadcast_to(arrival, (8, SLOTS)), 1.0, 0.0)
    cell = wcell[...]
    z_one = onehot(sub == jnp.broadcast_to(lax.rem(cell, 128), (SLOTS, SLOTS)))
    ol[0:128] = z_one
    ol[128:256] = z_one
    rowhot[...] = jnp.where(iota((32, SLOTS), 0) == jnp.broadcast_to(cell // 128, (32, SLOTS)), 1.0, 0.0)
    lo_t = jnp.where(sub == jnp.broadcast_to(lax.rem(route_row, NLO), (SLOTS, SLOTS)), 1.0, 0.0)
    lo_hot[...] = jnp.transpose(lo_t).astype(BF16)
    ha = route_row // NLO * 2 + arrival
    ha_t = jnp.where(sub // 4 == jnp.broadcast_to(ha, (SLOTS, SLOTS)), 1.0, 0.0)
    ha_hot[...] = jnp.transpose(ha_t)
    sel_lo[...] = onehot(iota((NLO, NV), 1) == iota((NLO, NV), 0) + hi * NLO)

    spread = onehot(iota((TILES, TQ), 1) // RANK == iota((TILES, TQ), 0))
    lists = jnp.concatenate([jnp.broadcast_to(trank[...], (4, TILES)), jnp.broadcast_to(trow[...], (4, TILES))], axis=0)
    over = dot(lists.astype(F32).astype(BF16), spread)
    rank_l, row_l = over[0:1], over[4:5]
    lane_q = lax.rem(iota((TILES, TQ), 1), RANK).astype(F32)
    diag_m[...] = jnp.where(lane_q < jnp.broadcast_to(rank_l, (TILES, TQ)), spread.astype(F32), 0.0)
    row_m[...] = jnp.where(iota((32, TQ), 0) // 8 == jnp.broadcast_to(row_l, (32, TQ)).astype(I32), 1.0, 0.0)
    col_t = jnp.where(iota((128, TILES), 0) == jnp.broadcast_to(tcol[...], (128, TILES)), 1.0, 0.0)
    col_t = jnp.concatenate([col_t, jnp.zeros((128, 96), F32)], axis=1)
    sel_t[...] = jnp.transpose(col_t)[0:TILES].astype(BF16)

    load_v.wait()
    load_u.wait()
    at_b, at_g = iota((256, 256), 0), iota((256, 256), 1)
    source = lax.rem(at_b // 2, 8) * 32 + lax.rem(at_b // 16, 8) * 4 + at_b // 128 * 2 + lax.rem(at_b, 2)
    perm_v = onehot(at_g == source)
    vdt[...] = dot_nt(perm_v, tv[...].reshape(TQ, 256)).astype(BF16)
    split = at_b == lax.rem(at_g, 128) * 2 + at_g // 128
    ud[...] = dot(tu[...].reshape(TQ, 256), onehot(split)).astype(BF16)

    w_ext[:, 3:7, 0:8] = disp[...]
    w_ext[:, 0:1, 8:16] = jnp.zeros((COMP, 1, 8, 128), F32)
    w_ext[:, 9:10, 8:16] = jnp.zeros((COMP, 1, 8, 128), F32)
    s_own = stiff[...]
    own_inv = relax_factor / (mass_shift + 6.0 * s_own)
    scale[...] = own_inv
    c_ext[2:6, 0:8] = own_inv * s_own
    f_ext[:, 2:6, 0:8] = force[...] * own_inv[None]

    for src, dst, at, dev, sends, comes in moves:
        @pl.when(comes)
        def _():
            remote(src, dst, halo_ss.at[at], halo_rs.at[at], dev).wait_recv()

    for s in (0, 1):
        w_ext[:, 7 * s:7 * s + 3, 0:8] = unpairs(vol_r[s, 0:18], (COMP, 3))
        s_v = unpairs(vol_r[s, 30:31], (2,))
        inv = relax_factor / (mass_shift + 6.0 * s_v)
        c_ext[6 * s:6 * s + 2, 0:8] = inv * s_v
        f_ext[:, 6 * s:6 * s + 2, 0:8] = unpairs(vol_r[s, 18:30], (COMP, 2)) * inv[None]
    low_r, high_r = unpairs(rep_r[0, 0:24], (COMP, 4)), unpairs(rep_r[1, 0:24], (COMP, 4))
    w_ext[:, 3:7, 8:16] = jnp.where(row3 <= 2, high_r, low_r)
    s_b = jnp.where(iota((4, 8, 128), 1) <= 3, unpairs(rep_r[1, 24:26], (4,)), unpairs(rep_r[0, 24:26], (4,)))
    inv = relax_factor / (mass_shift + 6.0 * s_b)
    c_ext[2:6, 8:16] = inv * s_b
    f_b = pltpu.roll(jnp.where(row3 >= 4, high_r, low_r).reshape(COMP * 4, 8, 128), 4, 1).reshape(COMP, 4, 8, 128)
    f_ext[:, 2:6, 8:16] = f_b * inv[None]
    zero_plane = jnp.zeros((1, 8, 128), F32)
    for s in (0, 1):
        low_c, high_c = unpairs(cor_r[s, 0], (COMP,)), unpairs(cor_r[s, 1], (COMP,))
        near, far = (2, 1) if s == 0 else (7, 8)
        w_ext[:, near, 8:16] = jnp.where(row_c <= 3, high_c, low_c)
        w_ext[:, far, 8:16] = jnp.where(row_c <= 3, pltpu.roll(high_c, 4, 1), pltpu.roll(low_c, 4, 1))
        s_c = jnp.where(row_c[0] <= 3, pltpu.roll(high_c[0], 1, 0), pltpu.roll(low_c[0], 7, 0))
        s_c = jnp.where(jnp.logical_or(row_c[0] == 0, row_c[0] == 7), s_c, 0.0)
        f_c = jnp.where(row_c <= 3, pltpu.roll(high_c, 2, 1), pltpu.roll(low_c, 6, 1))
        inv = relax_factor / (mass_shift + 6.0 * s_c)
        c_near, c_far = (1, 0) if s == 0 else (6, 7)
        c_ext[c_near, 8:16] = inv * s_c
        f_ext[:, c_near, 8:16] = f_c * inv[None]
        c_ext[c_far:c_far + 1, 8:16] = zero_plane
        f_ext[:, c_far, 8:16] = jnp.zeros((COMP, 8, 128), F32)

    keep = 1.0 - relax_factor

    def sweeps(i, carry):
        w = w_ext[i]
        f, cc = f_ext[i], c_ext[...]
        w = keep * w[1:9] + f + cc * neighbours(w[1:9], w[0:8], w[2:10])
        w = keep * w[1:7] + f[1:7] + cc[1:7] * neighbours(w[1:7], w[0:6], w[2:8])
        w = keep * w[1:5] + f[2:6] + cc[2:6] * neighbours(w[1:5], w[0:4], w[2:6])
        field[i] = w[:, 0:8]
        return carry

    lax.fori_loop(0, COMP, sweeps, 0)

    flat = field[...].reshape(COMP * 32, 128)
    upper = flat.astype(BF16)
    lower = (flat - upper.astype(F32)).astype(BF16)
    picked = dot(jnp.concatenate([upper, lower], axis=1), ol[...]).reshape(COMP, 32, SLOTS)
    normal = wnorm[...]
    picked = jnp.sum(picked * rowhot[...][None], axis=1)
    traces = normal[0:1] * picked[0:4] + normal[1:2] * picked[4:8] + normal[2:3] * picked[8:12]
    traces = jnp.concatenate([traces, traces], axis=0) * armask[...]
    message = dot_nt(traces.astype(BF16), place[...])

    ra[hi] = message
    for peer in hi_peers:
        remote(ra.at[hi], ra.at[hi], ph_ss.at[0], ph_rs.at[0], peer).start()

    row_f = iota((COMP, 8, 128), 1)
    fvol_s[0] = pairs(field[:, 3])
    fvol_s[1] = pairs(field[:, 0])
    for t in (0, 1):
        acc = jnp.zeros((COMP, 8, 128), F32)
        for p in range(4):
            shift = p + 1 if t == 0 else p
            rolled = field[:, p] if shift == 0 else pltpu.roll(field[:, p], shift, 1)
            acc = jnp.where(row_f == p, rolled, acc)
        frep_s[t] = pairs(acc)
    fmoves = []
    for s in (0, 1):
        fmoves.append((fvol_s.at[s], fvol_r.at[s], s, (vol_dev[s], r), vol_to[s], vol_from[s]))
        fmoves.append((frep_s.at[s], frep_r.at[s], 2 + s, (v, rep_dev[s]), rep_to[s], rep_from[s]))
    for src, dst, at, dev, sends, comes in fmoves:
        @pl.when(sends)
        def _():
            remote(src, dst, fhalo_ss.at[at], fhalo_rs.at[at], dev).start()

        @pl.when(jnp.logical_not(comes))
        def _():
            dst[...] = jnp.zeros(dst.shape, BF16)

    to_row, from_row = iota((64, 64), 0), iota((64, 64), 1)
    wanted = lax.rem(to_row, 16) // 2 * 8 + lax.rem(to_row, 2) * 4 + to_row // 16
    reorder = onehot(from_row == wanted)

    def wait_all(region, at, peer):
        remote(region, region, ph_ss.at[at], ph_rs.at[at], peer).wait_recv()

    wait_all(ra.at[pl.ds(0, NHI - 1)], 0, hi_peers[0])
    mine = dot(reorder, ra[...].reshape(64, 128).astype(BF16)).astype(BF16).reshape(4, 16, 128)
    g[c, y] = mine
    for peer in y_peers:
        remote(g.at[c, y], g.at[c, y], ph_ss.at[1], ph_rs.at[1], peer).start()
    wait_all(g.at[c, pl.ds(0, NY - 1)], 1, y_peers[0])
    remote(g.at[c], g.at[c], ph_ss.at[2], ph_rs.at[2], core_peer).start()

    for src, dst, at, dev, sends, comes in fmoves:
        @pl.when(comes)
        def _():
            remote(src, dst, fhalo_ss.at[at], fhalo_rs.at[at], dev).wait_recv()

    wait_all(g.at[c], 2, core_peer)

    pick = sel_t[...]
    chosen = jnp.concatenate([dot_nt(pick, g[:, :, k].reshape(256, 128)) for k in range(4)], axis=0).astype(BF16)
    every = dot(chosen, vdt[...])
    coef = jnp.sum(every.reshape(4, TILES, TQ) * diag_m[...][None], axis=1)
    coef = jnp.concatenate([coef, coef], axis=0)
    spread_c = (jnp.concatenate([coef] * 4, axis=0) * row_m[...]).astype(BF16)
    parts = dot(spread_c, ud[...])
    take = lax.rem(iota((32, 128), 0), 8) < 4
    parts = jnp.where(take, parts[:, 0:128], parts[:, 128:256])
    zs[...] = parts.reshape(4, 8, 128)

    mine_at = zh * NR + r
    for (zh_, r_), peer in zip(z_at, z_peers):
        remote(zs.at[r_], zr.at[mine_at], ph_ss.at[3], ph_rs.at[3], peer).start()
    zr[mine_at] = zs[r]

    low_f, high_f = unpairs(fvol_r[0], (COMP,)), unpairs(fvol_r[1], (COMP,))
    low_y, high_y = unpairs(frep_r[0], (COMP,)), unpairs(frep_r[1], (COMP,))
    for p in range(4):
        w = field[:, p]
        total = (field[:, p - 1] if p > 0 else low_f) + (field[:, p + 1] if p < 3 else high_f)
        before = pltpu.roll(low_y, 8 - p, 1) if p > 0 else low_y
        after = pltpu.roll(high_y, 7 - p, 1)
        total = total + jnp.where(row_f == 0, before, pltpu.roll(w, 1, 1))
        total = total + jnp.where(row_f == 7, after, pltpu.roll(w, 7, 1))
        lane_f = iota((COMP, 8, 128), 2)
        total = total + jnp.where(lane_f == 0, 0.0, pltpu.roll(w, 1, 2))
        total = total + jnp.where(lane_f == 127, 0.0, pltpu.roll(w, 127, 2))
        base[:, p] = keep * w + f_ext[:, 2 + p, 0:8] + c_ext[2 + p, 0:8][None] * total

    wait_all(zr.at[pl.ds(0, 2 * NR - 1)], 3, z_peers[0])
    sums = jnp.sum(zr[...].reshape(NZH, NR, 8, 128), axis=1)
    xb[x] = sums.reshape(16, 128).astype(BF16)
    for peer in x_peers:
        remote(xb.at[x], xb.at[x], ph_ss.at[4], ph_rs.at[4], peer).start()
    own = jnp.where(zh == 0, sums[0], sums[1])
    wide = jnp.concatenate([own[0:4], own[4:8]], axis=1)
    join = jnp.where(at_g == lax.rem(at_b, 128) * 2 + at_b // 128, 1.0, 0.0)
    out_p[...] = jnp.dot(wide, join, precision=lax.Precision.HIGHEST, preferred_element_type=F32)

    wait_all(xb.at[pl.ds(0, NX - 1)], 4, x_peers[0])
    gathered = xb[...].reshape(64, 128)
    gathered = jnp.concatenate([gathered, jnp.zeros((64, 128), BF16)], axis=0)
    ws[...] = dot_nt(sel_lo[...], gathered).reshape(NLO, 1, 128)
    for at, peer in zip(lo_at, lo_peers):
        remote(ws.at[at], wr.at[lo], ph_ss.at[5], ph_rs.at[5], peer).start()
    wr[lo] = ws[lo]
    wait_all(wr.at[pl.ds(0, NLO - 1)], 5, lo_peers[0])

    got = wr[...].reshape(NLO, 128).astype(BF16)
    got = jnp.concatenate([got, jnp.zeros((128 - NLO, 128), BF16)], axis=0)
    per_slot = (dot(lo_hot[...], got) * ha_hot[...]).astype(BF16)
    wave = onehot(lax.rem(iota((8, 128), 1), 4) == iota((8, 128), 0))
    wet = dot_nt(wave, per_slot)[0:4]
    out_w[...] = wet

    normal = -wnorm[...]
    load = jnp.concatenate([normal[i:i + 1] * wet for i in range(3)], axis=0)
    rows = (load[:, None, :] * rowhot[...][None]).reshape(COMP * 32, SLOTS)
    upper = rows.astype(BF16)
    lower = (rows - upper.astype(F32)).astype(BF16)
    z_one = ol[0:128]
    placed = dot_nt(jnp.concatenate([upper, lower], axis=1), jnp.concatenate([z_one, z_one], axis=1))
    out_u[...] = base[...] + scale[...][None] * placed.reshape(COMP, 4, 8, 128)

    for src, dst, at, dev, sends, comes in moves:
        @pl.when(sends)
        def _():
            remote(src, dst, halo_ss.at[at], halo_rs.at[at], dev).wait_send()
    for src, dst, at, dev, sends, comes in fmoves:
        @pl.when(sends)
        def _():
            remote(src, dst, fhalo_ss.at[at], fhalo_rs.at[at], dev).wait_send()

    def sent(region, at, peer):
        remote(region, region, ph_ss.at[at], ph_rs.at[at], peer).wait_send()

    sent(ra.at[pl.ds(0, NHI - 1)], 0, hi_peers[0])
    sent(g.at[c, pl.ds(0, NY - 1)], 1, y_peers[0])
    sent(g.at[c], 2, core_peer)
    sent(zr.at[pl.ds(0, 2 * NR - 1)], 3, z_peers[0])
    sent(xb.at[pl.ds(0, NX - 1)], 4, x_peers[0])
    sent(wr.at[pl.ds(0, NLO - 1)], 5, lo_peers[0])


def shards(displacement, body_force, stiffness, wet_cell, wet_normal, route, tile_u, tile_v, tile_row, tile_col, tile_rank):
    vmem = pl.BlockSpec(memory_space=pltpu.VMEM)
    anywhere = pl.BlockSpec(memory_space=pl.ANY)
    V = pltpu.VMEM
    updated, pressure, wet = pl.pallas_call(
        body,
        out_shape=(
            jax.ShapeDtypeStruct((COMP, 4, 8, 128), F32),
            jax.ShapeDtypeStruct((4, 256), F32),
            jax.ShapeDtypeStruct((4, SLOTS), F32),
        ),
        in_specs=[vmem] * 6 + [anywhere] * 2 + [vmem] * 3,
        out_specs=(vmem, vmem, vmem),
        scratch_shapes=[
            V((TILES, RANK, 256), BF16), V((TILES, RANK, 256), BF16),
            V((2, 31, 16, 128), BF16), V((2, 31, 16, 128), BF16),
            V((2, 26, 16, 128), BF16), V((2, 26, 16, 128), BF16),
            V((2, 2, 6, 16, 128), BF16), V((2, 2, 6, 16, 128), BF16),
            V((2, 6, 16, 128), BF16), V((2, 6, 16, 128), BF16),
            V((2, 6, 16, 128), BF16), V((2, 6, 16, 128), BF16),
            V((COMP, 10, 16, 128), F32), V((COMP, 8, 16, 128), F32), V((8, 16, 128), F32),
            V((COMP, 4, 8, 128), F32), V((COMP, 4, 8, 128), F32), V((4, 8, 128), F32),
            V((256, TQ), BF16), V((TQ, 256), BF16), V((256, SLOTS), BF16), V((32, SLOTS), F32),
            V((8, SLOTS), F32), V((128, SLOTS), BF16), V((TILES, 128), BF16), V((TILES, TQ), F32),
            V((32, TQ), F32), V((NLO, NV), BF16), V((SLOTS, 128), BF16), V((SLOTS, 128), F32),
            V((NHI, 8, 128), F32), V((NC, NY, 4, 16, 128), BF16),
            V((NR, 8, 128), F32), V((NZH * NR, 8, 128), F32), V((NX, 16, 128), BF16),
            V((NLO, 1, 128), F32), V((NLO, 1, 128), F32),
            pltpu.SemaphoreType.DMA((2,)),
            pltpu.SemaphoreType.DMA((8,)), pltpu.SemaphoreType.DMA((8,)),
            pltpu.SemaphoreType.DMA((4,)), pltpu.SemaphoreType.DMA((4,)),
            pltpu.SemaphoreType.DMA((6,)), pltpu.SemaphoreType.DMA((6,)),
        ],
        compiler_params=pltpu.CompilerParams(collective_id=0, has_side_effects=True, vmem_limit_bytes=40 << 20),
    )(
        displacement.reshape(COMP, 4, 8, 128),
        body_force.reshape(COMP, 4, 8, 128),
        stiffness,
        wet_cell,
        wet_normal,
        route.reshape(1, SLOTS),
        tile_u,
        tile_v,
        tile_row.reshape(1, TILES),
        tile_col.reshape(1, TILES),
        tile_rank.reshape(1, TILES),
    )
    return updated.reshape(displacement.shape), pressure, wet


def solution(mesh):
    return jax.shard_map(
        shards,
        mesh=mesh,
        in_specs=(
            P(None, None, "vol", "rep", None),
            P(None, None, "vol", "rep", None),
            P("vol", "rep", None),
            P(("vol", "rep"), None),
            P(None, ("vol", "rep")),
            P(("vol", "rep"), None),
            P(("vol", "rep"), None, None),
            P(("vol", "rep"), None, None),
            P(("vol", "rep")),
            P(("vol", "rep")),
            P(("vol", "rep")),
        ),
        out_specs=(
            P(None, None, "vol", "rep", None),
            P(None, ("vol", "rep")),
            P(None, ("vol", "rep")),
        ),
        check_vma=False,
    )
```

```python
import jax
import jax.numpy as jnp
from jax import lax
from jax.experimental import pallas as pl
from jax.experimental.pallas import tpu as pltpu
from jax.sharding import PartitionSpec as P

MESH = pl.DeviceIdType.MESH
relax_factor = 0.8
mass_shift = 1.0

F32 = jnp.float32
BF16 = jnp.bfloat16
I32 = jnp.int32

NX, NZH, NY, NC = 4, 2, 8, 2
NR = 4
NHI = NX * NZH
NLO = NY * NC
NV = NHI * NLO
NXY = NX * NLO
SLOTS = 128
COMP = 12
TILES, RANK = 32, 32
TQ = TILES * RANK

NT = (((1,), (1,)), ((), ()))


def dot(a, b):
    return jnp.dot(a, b, preferred_element_type=F32)


def dot_nt(a, b):
    return lax.dot_general(a, b, NT, preferred_element_type=F32)


def iota(shape, dim):
    return lax.broadcasted_iota(I32, shape, dim)


def onehot(condition, dtype=BF16):
    return jnp.where(condition, 1.0, 0.0).astype(F32).astype(dtype)


def pairs(tiles):
    lead = 1
    for size in tiles.shape[:-2]:
        lead *= size
    return tiles.reshape(lead // 2, 16, 128).astype(BF16)


def unpairs(tiles, lead):
    return tiles.astype(F32).reshape(*lead, 8, 128)


def neighbours(inner, low, high):
    rows = inner.shape[1]
    lane = iota(inner.shape, 2)
    total = low + high
    total = total + pltpu.roll(inner, 1, 1) + pltpu.roll(inner, rows - 1, 1)
    total = total + jnp.where(lane == 0, 0.0, pltpu.roll(inner, 1, 2))
    return total + jnp.where(lane == 127, 0.0, pltpu.roll(inner, 127, 2))


def body(
    disp_h, force_h, stiff_h, wcell_h, wnorm_h, route_h, tu_h, tv_h, trow_h, tcol_h, trank_h,
    out_u, out_p, out_w,
    disp, force, stiff, wcell, wnorm, route, tu, tv, trow, tcol, trank,
    vol_s, vol_r, rep_s, rep_r, cor_s, cor_r, fvol_s, fvol_r, frep_s, frep_r,
    w_ext, f_ext, c_ext, field, base, scale,
    vdt, ud, ol, rowhot, armask, place, sel_t, diag_m, row_m, sel_at, at_hot, za_hot,
    ra, g, zs, zr, ws, wr,
    load_sem, halo_ss, halo_rs, fhalo_ss, fhalo_rs, ph_ss, ph_rs,
):
    v = lax.axis_index("vol")
    r = lax.axis_index("rep")
    hi, lo = v // NLO, lax.rem(v, NLO)
    x, zh = hi // NZH, lax.rem(hi, NZH)
    y, c = lo // NC, lax.rem(lo, NC)

    def vol_of(x_, zh_, y_, c_):
        return ((x_ * NZH + zh_) * NY + y_) * NC + c_

    hi_peers = [(lax.rem(hi + j, NHI) * NLO + lo, r) for j in range(1, NHI)]
    y_peers = [(vol_of(x, zh, lax.rem(y + j, NY), c), r) for j in range(1, NY)]
    core_peer = (vol_of(x, zh, y, 1 - c), r)
    here = x * NLO + lo

    def plane_peer(j):
        at = lax.rem(here + j, NXY)
        return at, (at // NLO * (NZH * NLO) + zh * NLO + lax.rem(at, NLO), r)

    z_at = [(zh, lax.rem(r + j, NR)) for j in range(1, NR)] + [(1 - zh, lax.rem(r + j, NR)) for j in range(NR)]
    z_peers = [(vol_of(x, zh_, y, c), r_) for zh_, r_ in z_at]
    up_v, down_v = lax.rem(v + 1, NV), lax.rem(v + NV - 1, NV)
    up_r, down_r = lax.rem(r + 1, NR), lax.rem(r + NR - 1, NR)
    halo_peers = [(up_v, r), (down_v, r)] + [(a, b) for a in (up_v, down_v) for b in (up_r, down_r)]

    barrier = pltpu.get_barrier_semaphore()
    greeted = halo_peers + z_peers + hi_peers + y_peers + [core_peer]
    for peer in greeted:
        pl.semaphore_signal(barrier, inc=1, device_id=peer, device_id_type=MESH)

    sources = (disp_h, force_h, stiff_h, wcell_h, wnorm_h, route_h, trow_h, tcol_h, trank_h, tv_h, tu_h)
    targets = (disp, force, stiff, wcell, wnorm, route, trow, tcol, trank, tv, tu)
    loads = [pltpu.make_async_copy(a, b, load_sem.at[i]) for i, (a, b) in enumerate(zip(sources, targets))]
    for load in loads:
        load.start()
    for load in loads[:3]:
        load.wait()

    row3 = iota((COMP, 4, 8, 128), 2)
    row_c = iota((COMP, 8, 128), 1)
    for side in (0, 1):
        first = 1 - side
        vol_s[side, 0:18] = pairs(disp[:, first:first + 3])
        vol_s[side, 18:30] = pairs(force[:, 2 - 2 * side:4 - 2 * side])
        vol_s[side, 30:31] = pairs(stiff[2 - 2 * side:4 - 2 * side])
    force_up = pltpu.roll(force[...].reshape(COMP * 4, 8, 128), 4, 1).reshape(COMP, 4, 8, 128)
    rep_s[0, 0:24] = pairs(jnp.where(row3 >= 5, disp[...], force_up))
    rep_s[1, 0:24] = pairs(jnp.where(row3 <= 2, disp[...], force_up))
    for side in (0, 1):
        rep_s[side, 24:26] = pairs(stiff[...])
        edge, second = (3, 2) if side == 0 else (0, 1)
        w_e, w_2, f_e = disp[:, edge], disp[:, second], force[:, edge]
        s_e = jnp.broadcast_to(stiff[edge:edge + 1], (COMP, 8, 128))
        w_2 = pltpu.roll(w_2, 4, 1)
        up = jnp.where(row_c >= 6, w_e, jnp.where(row_c == 3, w_2, jnp.where(row_c == 1, pltpu.roll(f_e, 2, 1), pltpu.roll(s_e, 1, 1))))
        down = jnp.where(row_c <= 1, w_e, jnp.where(row_c == 4, w_2, jnp.where(row_c == 6, pltpu.roll(f_e, 6, 1), pltpu.roll(s_e, 7, 1))))
        cor_s[side, 0] = pairs(up)
        cor_s[side, 1] = pairs(down)

    vol_to = [v < NV - 1, v > 0]
    vol_from = [v > 0, v < NV - 1]
    rep_to = [r < NR - 1, r > 0]
    rep_from = [r > 0, r < NR - 1]
    vol_dev, rep_dev = [up_v, down_v], [up_r, down_r]

    moves = []
    for s in (0, 1):
        moves.append((vol_s.at[s], vol_r.at[s], s, (vol_dev[s], r), vol_to[s], vol_from[s]))
    for s in (0, 1):
        for t in (0, 1):
            moves.append((cor_s.at[s, t], cor_r.at[s, t], 4 + 2 * s + t, (vol_dev[s], rep_dev[t]),
                          jnp.logical_and(vol_to[s], rep_to[t]), jnp.logical_and(vol_from[s], rep_from[t])))
    for t in (0, 1):
        moves.append((rep_s.at[t], rep_r.at[t], 2 + t, (v, rep_dev[t]), rep_to[t], rep_from[t]))

    def remote(src, dst, ss, rs, dev):
        return pltpu.make_async_remote_copy(src_ref=src, dst_ref=dst, send_sem=ss, recv_sem=rs, device_id=dev, device_id_type=MESH)

    for src, dst, at, dev, sends, comes in moves:
        @pl.when(jnp.logical_not(comes))
        def _():
            dst[...] = jnp.zeros(dst.shape, BF16)

    pl.semaphore_wait(barrier, len(greeted))

    for src, dst, at, dev, sends, comes in moves:
        @pl.when(sends)
        def _():
            remote(src, dst, halo_ss.at[at], halo_rs.at[at], dev).start()

    for load in loads[3:]:
        load.wait()
    route_row = route[...]
    route_sq = jnp.broadcast_to(route_row, (SLOTS, SLOTS))
    route_col = jnp.transpose(route_sq.astype(F32)).astype(I32)
    sub = iota((SLOTS, SLOTS), 0)
    lane = iota((SLOTS, SLOTS), 1)
    earlier = jnp.where(jnp.logical_and(route_col == route_sq, sub < lane), 1.0, 0.0)
    arrival = jnp.sum(earlier, axis=0, keepdims=True).astype(I32)
    place[...] = onehot(sub == route_sq)
    armask[...] = jnp.where(iota((8, SLOTS), 0) // 4 == jnp.broadcast_to(arrival, (8, SLOTS)), 1.0, 0.0)
    cell = wcell[...]
    z_one = onehot(sub == jnp.broadcast_to(lax.rem(cell, 128), (SLOTS, SLOTS)))
    ol[0:128] = z_one
    ol[128:256] = z_one
    rowhot[...] = jnp.where(iota((32, SLOTS), 0) == jnp.broadcast_to(cell // 128, (32, SLOTS)), 1.0, 0.0)
    owner_at = route_row // (NZH * NLO) * NLO + lax.rem(route_row, NLO)
    at_t = jnp.where(sub == jnp.broadcast_to(owner_at, (SLOTS, SLOTS)), 1.0, 0.0)
    at_hot[...] = jnp.transpose(at_t).astype(BF16)
    za = lax.rem(route_row // NLO, NZH) * 2 + arrival
    za_t = jnp.where(sub // 4 == jnp.broadcast_to(za, (SLOTS, SLOTS)), 1.0, 0.0)
    za_hot[...] = jnp.transpose(za_t)
    at_row = iota((NXY, NV), 0)
    sel_at[...] = onehot(iota((NXY, NV), 1) == at_row // NLO * (NZH * NLO) + zh * NLO + lax.rem(at_row, NLO))

    spread = onehot(iota((TILES, TQ), 1) // RANK == iota((TILES, TQ), 0))
    lists = jnp.concatenate([jnp.broadcast_to(trank[...], (4, TILES)), jnp.broadcast_to(trow[...], (4, TILES))], axis=0)
    over = dot(lists.astype(F32).astype(BF16), spread)
    rank_l, row_l = over[0:1], over[4:5]
    lane_q = lax.rem(iota((TILES, TQ), 1), RANK).astype(F32)
    diag_m[...] = jnp.where(lane_q < jnp.broadcast_to(rank_l, (TILES, TQ)), spread.astype(F32), 0.0)
    row_m[...] = jnp.where(iota((32, TQ), 0) // 8 == jnp.broadcast_to(row_l, (32, TQ)).astype(I32), 1.0, 0.0)
    col_t = jnp.where(iota((128, TILES), 0) == jnp.broadcast_to(tcol[...], (128, TILES)), 1.0, 0.0)
    col_t = jnp.concatenate([col_t, jnp.zeros((128, 96), F32)], axis=1)
    sel_t[...] = jnp.transpose(col_t)[0:TILES].astype(BF16)

    at_b, at_g = iota((256, 256), 0), iota((256, 256), 1)
    source = lax.rem(at_b // 2, 8) * 32 + lax.rem(at_b // 16, 8) * 4 + at_b // 128 * 2 + lax.rem(at_b, 2)
    perm_v = onehot(at_g == source)
    vdt[...] = dot_nt(perm_v, tv[...].reshape(TQ, 256)).astype(BF16)
    split = at_b == lax.rem(at_g, 128) * 2 + at_g // 128
    ud[...] = dot(tu[...].reshape(TQ, 256), onehot(split)).astype(BF16)

    w_ext[:, 3:7, 0:8] = disp[...]
    w_ext[:, 0:1, 8:16] = jnp.zeros((COMP, 1, 8, 128), F32)
    w_ext[:, 9:10, 8:16] = jnp.zeros((COMP, 1, 8, 128), F32)
    s_own = stiff[...]
    own_inv = relax_factor / (mass_shift + 6.0 * s_own)
    scale[...] = own_inv
    c_ext[2:6, 0:8] = own_inv * s_own
    f_ext[:, 2:6, 0:8] = force[...] * own_inv[None]

    for src, dst, at, dev, sends, comes in moves:
        @pl.when(comes)
        def _():
            remote(src, dst, halo_ss.at[at], halo_rs.at[at], dev).wait_recv()

    for s in (0, 1):
        w_ext[:, 7 * s:7 * s + 3, 0:8] = unpairs(vol_r[s, 0:18], (COMP, 3))
        s_v = unpairs(vol_r[s, 30:31], (2,))
        inv = relax_factor / (mass_shift + 6.0 * s_v)
        c_ext[6 * s:6 * s + 2, 0:8] = inv * s_v
        f_ext[:, 6 * s:6 * s + 2, 0:8] = unpairs(vol_r[s, 18:30], (COMP, 2)) * inv[None]
    low_r, high_r = unpairs(rep_r[0, 0:24], (COMP, 4)), unpairs(rep_r[1, 0:24], (COMP, 4))
    w_ext[:, 3:7, 8:16] = jnp.where(row3 <= 2, high_r, low_r)
    s_b = jnp.where(iota((4, 8, 128), 1) <= 3, unpairs(rep_r[1, 24:26], (4,)), unpairs(rep_r[0, 24:26], (4,)))
    inv = relax_factor / (mass_shift + 6.0 * s_b)
    c_ext[2:6, 8:16] = inv * s_b
    f_b = pltpu.roll(jnp.where(row3 >= 4, high_r, low_r).reshape(COMP * 4, 8, 128), 4, 1).reshape(COMP, 4, 8, 128)
    f_ext[:, 2:6, 8:16] = f_b * inv[None]
    zero_plane = jnp.zeros((1, 8, 128), F32)
    for s in (0, 1):
        low_c, high_c = unpairs(cor_r[s, 0], (COMP,)), unpairs(cor_r[s, 1], (COMP,))
        near, far = (2, 1) if s == 0 else (7, 8)
        w_ext[:, near, 8:16] = jnp.where(row_c <= 3, high_c, low_c)
        w_ext[:, far, 8:16] = jnp.where(row_c <= 3, pltpu.roll(high_c, 4, 1), pltpu.roll(low_c, 4, 1))
        s_c = jnp.where(row_c[0] <= 3, pltpu.roll(high_c[0], 1, 0), pltpu.roll(low_c[0], 7, 0))
        s_c = jnp.where(jnp.logical_or(row_c[0] == 0, row_c[0] == 7), s_c, 0.0)
        f_c = jnp.where(row_c <= 3, pltpu.roll(high_c, 2, 1), pltpu.roll(low_c, 6, 1))
        inv = relax_factor / (mass_shift + 6.0 * s_c)
        c_near, c_far = (1, 0) if s == 0 else (6, 7)
        c_ext[c_near, 8:16] = inv * s_c
        f_ext[:, c_near, 8:16] = f_c * inv[None]
        c_ext[c_far:c_far + 1, 8:16] = zero_plane
        f_ext[:, c_far, 8:16] = jnp.zeros((COMP, 8, 128), F32)

    keep = 1.0 - relax_factor

    def sweeps(i, carry):
        w = w_ext[i]
        f, cc = f_ext[i], c_ext[...]
        w = keep * w[1:9] + f + cc * neighbours(w[1:9], w[0:8], w[2:10])
        w = keep * w[1:7] + f[1:7] + cc[1:7] * neighbours(w[1:7], w[0:6], w[2:8])
        w = keep * w[1:5] + f[2:6] + cc[2:6] * neighbours(w[1:5], w[0:4], w[2:6])
        field[i] = w[:, 0:8]
        return carry

    lax.fori_loop(0, COMP, sweeps, 0, unroll=12)

    flat = field[...].reshape(COMP * 32, 128)
    upper = flat.astype(BF16)
    lower = (flat - upper.astype(F32)).astype(BF16)
    picked = dot(jnp.concatenate([upper, lower], axis=1), ol[...]).reshape(COMP, 32, SLOTS)
    normal = wnorm[...]
    picked = jnp.sum(picked * rowhot[...][None], axis=1)
    traces = normal[0:1] * picked[0:4] + normal[1:2] * picked[4:8] + normal[2:3] * picked[8:12]
    traces = jnp.concatenate([traces, traces], axis=0) * armask[...]
    message = dot_nt(traces.astype(BF16), place[...])

    ra[hi] = message
    for peer in hi_peers:
        remote(ra.at[hi], ra.at[hi], ph_ss.at[0], ph_rs.at[0], peer).start()

    to_row, from_row = iota((64, 64), 0), iota((64, 64), 1)
    wanted = lax.rem(to_row, 16) // 2 * 8 + lax.rem(to_row, 2) * 4 + to_row // 16
    reorder = onehot(from_row == wanted)

    def wait_all(region, at, peer):
        remote(region, region, ph_ss.at[at], ph_rs.at[at], peer).wait_recv()

    wait_all(ra.at[pl.ds(0, NHI - 1)], 0, hi_peers[0])
    mine = dot(reorder, ra[...].reshape(64, 128).astype(BF16)).astype(BF16).reshape(4, 16, 128)
    g[c, y] = mine
    for peer in y_peers:
        remote(g.at[c, y], g.at[c, y], ph_ss.at[1], ph_rs.at[1], peer).start()
    wait_all(g.at[c, pl.ds(0, NY - 1)], 1, y_peers[0])
    remote(g.at[c], g.at[c], ph_ss.at[2], ph_rs.at[2], core_peer).start()

    row_f = iota((COMP, 8, 128), 1)
    fvol_s[0] = pairs(field[:, 3])
    fvol_s[1] = pairs(field[:, 0])
    for t in (0, 1):
        acc = jnp.zeros((COMP, 8, 128), F32)
        for p in range(4):
            shift = p + 1 if t == 0 else p
            rolled = field[:, p] if shift == 0 else pltpu.roll(field[:, p], shift, 1)
            acc = jnp.where(row_f == p, rolled, acc)
        frep_s[t] = pairs(acc)
    fmoves = []
    for s in (0, 1):
        fmoves.append((fvol_s.at[s], fvol_r.at[s], s, (vol_dev[s], r), vol_to[s], vol_from[s]))
        fmoves.append((frep_s.at[s], frep_r.at[s], 2 + s, (v, rep_dev[s]), rep_to[s], rep_from[s]))
    for src, dst, at, dev, sends, comes in fmoves:
        @pl.when(sends)
        def _():
            remote(src, dst, fhalo_ss.at[at], fhalo_rs.at[at], dev).start()

        @pl.when(jnp.logical_not(comes))
        def _():
            dst[...] = jnp.zeros(dst.shape, BF16)


    wait_all(g.at[c], 2, core_peer)

    pick = sel_t[...]
    chosen = jnp.concatenate([dot_nt(pick, g[:, :, k].reshape(256, 128)) for k in range(4)], axis=0).astype(BF16)
    every = dot(chosen, vdt[...])
    coef = jnp.sum(every.reshape(4, TILES, TQ) * diag_m[...][None], axis=1)
    coef = jnp.concatenate([coef, coef], axis=0)
    spread_c = (jnp.concatenate([coef] * 4, axis=0) * row_m[...]).astype(BF16)
    parts = dot(spread_c, ud[...])
    take = lax.rem(iota((32, 128), 0), 8) < 4
    parts = jnp.where(take, parts[:, 0:128], parts[:, 128:256])
    zs[...] = parts.reshape(4, 8, 128)

    mine_at = zh * NR + r
    for (zh_, r_), peer in zip(z_at, z_peers):
        remote(zs.at[r_], zr.at[mine_at], ph_ss.at[3], ph_rs.at[3], peer).start()
    zr[mine_at] = zs[r]

    wait_all(zr.at[pl.ds(0, 2 * NR - 1)], 3, z_peers[0])
    sums = jnp.sum(zr[...].reshape(NZH, NR, 8, 128), axis=1)
    back = jnp.concatenate([sums.reshape(16, 128), jnp.zeros((112, 128), F32)], axis=0).astype(BF16)
    ws[...] = dot_nt(sel_at[...], back).reshape(NXY, 1, 128)

    def give_back(j, carry):
        at, peer = plane_peer(j)
        remote(ws.at[at], wr.at[here], ph_ss.at[4], ph_rs.at[4], peer).start()
        return carry

    lax.fori_loop(1, NXY, give_back, 0)
    wr[here] = ws[here]
    own = jnp.where(zh == 0, sums[0], sums[1])
    wide = jnp.concatenate([own[0:4], own[4:8]], axis=1)
    join = jnp.where(at_g == lax.rem(at_b, 128) * 2 + at_b // 128, 1.0, 0.0)
    out_p[...] = jnp.dot(wide, join, precision=lax.Precision.HIGHEST, preferred_element_type=F32)

    for src, dst, at, dev, sends, comes in fmoves:
        @pl.when(comes)
        def _():
            remote(src, dst, fhalo_ss.at[at], fhalo_rs.at[at], dev).wait_recv()

    low_f, high_f = unpairs(fvol_r[0], (COMP,)), unpairs(fvol_r[1], (COMP,))
    low_y, high_y = unpairs(frep_r[0], (COMP,)), unpairs(frep_r[1], (COMP,))
    for p in range(4):
        w = field[:, p]
        total = (field[:, p - 1] if p > 0 else low_f) + (field[:, p + 1] if p < 3 else high_f)
        before = pltpu.roll(low_y, 8 - p, 1) if p > 0 else low_y
        after = pltpu.roll(high_y, 7 - p, 1)
        total = total + jnp.where(row_f == 0, before, pltpu.roll(w, 1, 1))
        total = total + jnp.where(row_f == 7, after, pltpu.roll(w, 7, 1))
        lane_f = iota((COMP, 8, 128), 2)
        total = total + jnp.where(lane_f == 0, 0.0, pltpu.roll(w, 1, 2))
        total = total + jnp.where(lane_f == 127, 0.0, pltpu.roll(w, 127, 2))
        base[:, p] = keep * w + f_ext[:, 2 + p, 0:8] + c_ext[2 + p, 0:8][None] * total

    wait_all(wr.at[pl.ds(0, NXY - 1)], 4, core_peer)

    got = wr[...].reshape(NXY, 128).astype(BF16)
    got = jnp.concatenate([got, jnp.zeros((128 - NXY, 128), BF16)], axis=0)
    per_slot = (dot(at_hot[...], got) * za_hot[...]).astype(BF16)
    wave = onehot(lax.rem(iota((8, 128), 1), 4) == iota((8, 128), 0))
    wet = dot_nt(wave, per_slot)[0:4]
    out_w[...] = wet

    normal = -wnorm[...]
    load = jnp.concatenate([normal[i:i + 1] * wet for i in range(3)], axis=0)
    rows = (load[:, None, :] * rowhot[...][None]).reshape(COMP * 32, SLOTS)
    upper = rows.astype(BF16)
    lower = (rows - upper.astype(F32)).astype(BF16)
    z_one = ol[0:128]
    placed = dot_nt(jnp.concatenate([upper, lower], axis=1), jnp.concatenate([z_one, z_one], axis=1))
    out_u[...] = base[...] + scale[...][None] * placed.reshape(COMP, 4, 8, 128)

    for src, dst, at, dev, sends, comes in moves:
        @pl.when(sends)
        def _():
            remote(src, dst, halo_ss.at[at], halo_rs.at[at], dev).wait_send()
    for src, dst, at, dev, sends, comes in fmoves:
        @pl.when(sends)
        def _():
            remote(src, dst, fhalo_ss.at[at], fhalo_rs.at[at], dev).wait_send()

    def sent(region, at, peer):
        remote(region, region, ph_ss.at[at], ph_rs.at[at], peer).wait_send()

    sent(ra.at[pl.ds(0, NHI - 1)], 0, hi_peers[0])
    sent(g.at[c, pl.ds(0, NY - 1)], 1, y_peers[0])
    sent(g.at[c], 2, core_peer)
    sent(zr.at[pl.ds(0, 2 * NR - 1)], 3, z_peers[0])
    sent(wr.at[pl.ds(0, NXY - 1)], 4, core_peer)


def shards(displacement, body_force, stiffness, wet_cell, wet_normal, route, tile_u, tile_v, tile_row, tile_col, tile_rank):
    vmem = pl.BlockSpec(memory_space=pltpu.VMEM)
    hbm = pl.BlockSpec(memory_space=pltpu.HBM)
    V = pltpu.VMEM
    updated, pressure, wet = pl.pallas_call(
        body,
        out_shape=(
            jax.ShapeDtypeStruct((COMP, 4, 8, 128), F32),
            jax.ShapeDtypeStruct((4, 256), F32),
            jax.ShapeDtypeStruct((4, SLOTS), F32),
        ),
        in_specs=[hbm] * 11,
        out_specs=(vmem, vmem, vmem),
        scratch_shapes=[
            V((COMP, 4, 8, 128), F32), V((COMP, 4, 8, 128), F32), V((4, 8, 128), F32),
            V((1, SLOTS), I32), V((3, SLOTS), F32), V((1, SLOTS), I32),
            V((TILES, RANK, 256), BF16), V((TILES, RANK, 256), BF16),
            V((1, TILES), I32), V((1, TILES), I32), V((1, TILES), I32),
            V((2, 31, 16, 128), BF16), V((2, 31, 16, 128), BF16),
            V((2, 26, 16, 128), BF16), V((2, 26, 16, 128), BF16),
            V((2, 2, 6, 16, 128), BF16), V((2, 2, 6, 16, 128), BF16),
            V((2, 6, 16, 128), BF16), V((2, 6, 16, 128), BF16),
            V((2, 6, 16, 128), BF16), V((2, 6, 16, 128), BF16),
            V((COMP, 10, 16, 128), F32), V((COMP, 8, 16, 128), F32), V((8, 16, 128), F32),
            V((COMP, 4, 8, 128), F32), V((COMP, 4, 8, 128), F32), V((4, 8, 128), F32),
            V((256, TQ), BF16), V((TQ, 256), BF16), V((256, SLOTS), BF16), V((32, SLOTS), F32),
            V((8, SLOTS), F32), V((128, SLOTS), BF16), V((TILES, 128), BF16), V((TILES, TQ), F32),
            V((32, TQ), F32), V((NXY, NV), BF16), V((SLOTS, 128), BF16), V((SLOTS, 128), F32),
            V((NHI, 8, 128), F32), V((NC, NY, 4, 16, 128), BF16),
            V((NR, 8, 128), F32), V((NZH * NR, 8, 128), F32),
            V((NXY, 1, 128), F32), V((NXY, 1, 128), F32),
            pltpu.SemaphoreType.DMA((11,)),
            pltpu.SemaphoreType.DMA((8,)), pltpu.SemaphoreType.DMA((8,)),
            pltpu.SemaphoreType.DMA((4,)), pltpu.SemaphoreType.DMA((4,)),
            pltpu.SemaphoreType.DMA((5,)), pltpu.SemaphoreType.DMA((5,)),
        ],
        compiler_params=pltpu.CompilerParams(collective_id=0, has_side_effects=True, vmem_limit_bytes=56 << 20),
    )(
        displacement.reshape(COMP, 4, 8, 128),
        body_force.reshape(COMP, 4, 8, 128),
        stiffness,
        wet_cell,
        wet_normal,
        route.reshape(1, SLOTS),
        tile_u,
        tile_v,
        tile_row.reshape(1, TILES),
        tile_col.reshape(1, TILES),
        tile_rank.reshape(1, TILES),
    )
    return updated.reshape(displacement.shape), pressure, wet


def solution(mesh):
    return jax.shard_map(
        shards,
        mesh=mesh,
        in_specs=(
            P(None, None, "vol", "rep", None),
            P(None, None, "vol", "rep", None),
            P("vol", "rep", None),
            P(("vol", "rep"), None),
            P(None, ("vol", "rep")),
            P(("vol", "rep"), None),
            P(("vol", "rep"), None, None),
            P(("vol", "rep"), None, None),
            P(("vol", "rep")),
            P(("vol", "rep")),
            P(("vol", "rep")),
        ),
        out_specs=(
            P(None, None, "vol", "rep", None),
            P(None, ("vol", "rep")),
            P(None, ("vol", "rep")),
        ),
        check_vma=False,
    )
```

```python
import jax
import jax.numpy as jnp
from jax import lax
from jax.experimental import pallas as pl
from jax.experimental.pallas import tpu as pltpu
from jax.sharding import PartitionSpec as P

MESH = pl.DeviceIdType.MESH
relax_factor = 0.8
mass_shift = 1.0

F32 = jnp.float32
BF16 = jnp.bfloat16
I32 = jnp.int32

NX, NZH, NY, NC = 4, 2, 8, 2
NR = 4
NHI = NX * NZH
NLO = NY * NC
NV = NHI * NLO
NXY = NX * NLO
SLOTS = 128
COMP = 12
TILES, RANK = 32, 32
TQ = TILES * RANK

NT = (((1,), (1,)), ((), ()))


def dot(a, b):
    return jnp.dot(a, b, preferred_element_type=F32)


def dot_nt(a, b):
    return lax.dot_general(a, b, NT, preferred_element_type=F32)


def iota(shape, dim):
    return lax.broadcasted_iota(I32, shape, dim)


def onehot(condition, dtype=BF16):
    return jnp.where(condition, 1.0, 0.0).astype(F32).astype(dtype)


def pairs(tiles):
    lead = 1
    for size in tiles.shape[:-2]:
        lead *= size
    return tiles.reshape(lead // 2, 16, 128).astype(BF16)


def unpairs(tiles, lead):
    return tiles.astype(F32).reshape(*lead, 8, 128)


def body(
    disp_h, force_h, stiff_h, wcell_h, wnorm_h, route_h, tu_h, tv_h, trow_h, tcol_h, trank_h,
    out_u, out_p, out_w,
    disp, force, stiff, wcell, wnorm, route, tu, tv, trow, tcol, trank,
    vol_s, vol_r, rep_s, rep_r, cor_s, cor_r, fvol_s, fvol_r, frep_s, frep_r,
    w_ext, f_ext, c_ext, once_ext, twice_ext, field, base, scale,
    vdt, ud, ol, rowhot, armask, place, sel_t, diag_m, row_m, sel_at, at_hot, za_hot,
    ra, g, zs, zr, ws, wr,
    load_sem, halo_ss, halo_rs, fhalo_ss, fhalo_rs, ph_ss, ph_rs,
):
    v = lax.axis_index("vol")
    r = lax.axis_index("rep")
    hi, lo = v // NLO, lax.rem(v, NLO)
    x, zh = hi // NZH, lax.rem(hi, NZH)
    y, c = lo // NC, lax.rem(lo, NC)

    def vol_of(x_, zh_, y_, c_):
        return ((x_ * NZH + zh_) * NY + y_) * NC + c_

    hi_peers = [(lax.rem(hi + j, NHI) * NLO + lo, r) for j in range(1, NHI)]
    y_peers = [(vol_of(x, zh, lax.rem(y + j, NY), c), r) for j in range(1, NY)]
    core_peer = (vol_of(x, zh, y, 1 - c), r)
    here = x * NLO + lo

    def plane_peer(j):
        at = lax.rem(here + j, NXY)
        return at, (at // NLO * (NZH * NLO) + zh * NLO + lax.rem(at, NLO), r)

    z_at = [(zh, lax.rem(r + j, NR)) for j in range(1, NR)] + [(1 - zh, lax.rem(r + j, NR)) for j in range(NR)]
    z_peers = [(vol_of(x, zh_, y, c), r_) for zh_, r_ in z_at]
    up_v, down_v = lax.rem(v + 1, NV), lax.rem(v + NV - 1, NV)
    up_r, down_r = lax.rem(r + 1, NR), lax.rem(r + NR - 1, NR)
    halo_peers = [(up_v, r), (down_v, r)] + [(a, b) for a in (up_v, down_v) for b in (up_r, down_r)]

    barrier = pltpu.get_barrier_semaphore()
    greeted = halo_peers + z_peers + hi_peers + y_peers + [core_peer]
    for peer in greeted:
        pl.semaphore_signal(barrier, inc=1, device_id=peer, device_id_type=MESH)

    sources = (disp_h, force_h, stiff_h, wcell_h, wnorm_h, route_h, trow_h, tcol_h, trank_h, tv_h, tu_h)
    targets = (disp, force, stiff, wcell, wnorm, route, trow, tcol, trank, tv, tu)
    loads = [pltpu.make_async_copy(a, b, load_sem.at[i]) for i, (a, b) in enumerate(zip(sources, targets))]
    for load in loads:
        load.start()
    for load in loads[:3]:
        load.wait()

    keep = 1.0 - relax_factor
    row3 = iota((COMP, 4, 8, 128), 2)
    row_c = iota((COMP, 8, 128), 1)
    lane_c = iota((COMP, 8, 128), 2)

    def inside(w):
        total = jnp.where(row_c == 0, 0.0, pltpu.roll(w, 1, 1)) + jnp.where(row_c == 7, 0.0, pltpu.roll(w, 7, 1))
        return total + jnp.where(lane_c == 0, 0.0, pltpu.roll(w, 1, 2)) + jnp.where(lane_c == 127, 0.0, pltpu.roll(w, 127, 2))

    own_inv = relax_factor / (mass_shift + 6.0 * stiff[...])
    own_c = own_inv * stiff[...]
    scale[...] = own_inv
    c_ext[1:5, 0:8] = own_c
    f_ext[:, :, 0:8] = force[...] * own_inv[None]
    for side in (0, 1):
        edge, second, third = (3, 2, 1) if side == 0 else (0, 1, 2)
        w_e, w_2, f_e = disp[:, edge], disp[:, second], f_ext[:, edge, 0:8]
        c_e, c_2 = own_c[edge], own_c[second]
        once = keep * w_e + f_e + c_e[None] * (w_2 + inside(w_e))
        once_2 = keep * w_2 + f_ext[:, second, 0:8] + c_2[None] * (w_e + disp[:, third] + inside(w_2))
        twice = f_e + c_e[None] * once_2
        vol_s[side, 0:6] = pairs(w_e)
        vol_s[side, 6:12] = pairs(once)
        vol_s[side, 12:18] = pairs(twice)
        vol_s[side, 18:19] = pairs(jnp.stack([c_e, c_e * c_2]))
        up = jnp.where(row_c >= 6, w_e, jnp.where(row_c == 5, pltpu.roll(once, 6, 1), pltpu.roll(w_2, 5, 1)))
        down = jnp.where(row_c <= 1, w_e, jnp.where(row_c == 2, pltpu.roll(once, 2, 1), pltpu.roll(w_2, 3, 1)))
        half = row_c[0:6] >= 4
        cor_s[side, 0, 0:3] = pairs(jnp.where(half, up[6:12], pltpu.roll(up[0:6], 4, 1)))
        cor_s[side, 1, 0:3] = pairs(jnp.where(half, pltpu.roll(down[6:12], 4, 1), down[0:6]))
        for t in (0, 1):
            cor_s[side, t, 3:4] = pairs(jnp.stack([c_e, c_e]))
    force_up = pltpu.roll(f_ext[:, :, 0:8].reshape(COMP * 4, 8, 128), 4, 1).reshape(COMP, 4, 8, 128)
    rep_s[0, 0:24] = pairs(jnp.where(row3 >= 5, disp[...], force_up))
    rep_s[1, 0:24] = pairs(jnp.where(row3 <= 2, disp[...], force_up))
    for side in (0, 1):
        rep_s[side, 24:26] = pairs(own_c)

    vol_to = [v < NV - 1, v > 0]
    vol_from = [v > 0, v < NV - 1]
    rep_to = [r < NR - 1, r > 0]
    rep_from = [r > 0, r < NR - 1]
    vol_dev, rep_dev = [up_v, down_v], [up_r, down_r]

    moves = []
    for s in (0, 1):
        moves.append((vol_s.at[s], vol_r.at[s], s, (vol_dev[s], r), vol_to[s], vol_from[s]))
    for s in (0, 1):
        for t in (0, 1):
            moves.append((cor_s.at[s, t], cor_r.at[s, t], 4 + 2 * s + t, (vol_dev[s], rep_dev[t]),
                          jnp.logical_and(vol_to[s], rep_to[t]), jnp.logical_and(vol_from[s], rep_from[t])))
    for t in (0, 1):
        moves.append((rep_s.at[t], rep_r.at[t], 2 + t, (v, rep_dev[t]), rep_to[t], rep_from[t]))

    def remote(src, dst, ss, rs, dev):
        return pltpu.make_async_remote_copy(src_ref=src, dst_ref=dst, send_sem=ss, recv_sem=rs, device_id=dev, device_id_type=MESH)

    for src, dst, at, dev, sends, comes in moves:
        @pl.when(jnp.logical_not(comes))
        def _():
            dst[...] = jnp.zeros(dst.shape, BF16)

    pl.semaphore_wait(barrier, len(greeted))

    for src, dst, at, dev, sends, comes in moves:
        @pl.when(sends)
        def _():
            remote(src, dst, halo_ss.at[at], halo_rs.at[at], dev).start()

    for load in loads[3:]:
        load.wait()
    route_row = route[...]
    route_sq = jnp.broadcast_to(route_row, (SLOTS, SLOTS))
    route_col = jnp.transpose(route_sq.astype(F32)).astype(I32)
    sub = iota((SLOTS, SLOTS), 0)
    lane = iota((SLOTS, SLOTS), 1)
    earlier = jnp.where(jnp.logical_and(route_col == route_sq, sub < lane), 1.0, 0.0)
    arrival = jnp.sum(earlier, axis=0, keepdims=True).astype(I32)
    place[...] = onehot(sub == route_sq)
    armask[...] = jnp.where(iota((8, SLOTS), 0) // 4 == jnp.broadcast_to(arrival, (8, SLOTS)), 1.0, 0.0)
    cell = wcell[...]
    z_one = onehot(sub == jnp.broadcast_to(lax.rem(cell, 128), (SLOTS, SLOTS)))
    ol[0:128] = z_one
    ol[128:256] = z_one
    rowhot[...] = jnp.where(iota((32, SLOTS), 0) == jnp.broadcast_to(cell // 128, (32, SLOTS)), 1.0, 0.0)
    owner_at = route_row // (NZH * NLO) * NLO + lax.rem(route_row, NLO)
    at_t = jnp.where(sub == jnp.broadcast_to(owner_at, (SLOTS, SLOTS)), 1.0, 0.0)
    at_hot[...] = jnp.transpose(at_t).astype(BF16)
    za = lax.rem(route_row // NLO, NZH) * 2 + arrival
    za_t = jnp.where(sub // 4 == jnp.broadcast_to(za, (SLOTS, SLOTS)), 1.0, 0.0)
    za_hot[...] = jnp.transpose(za_t)
    at_row = iota((NXY, NV), 0)
    sel_at[...] = onehot(iota((NXY, NV), 1) == at_row // NLO * (NZH * NLO) + zh * NLO + lax.rem(at_row, NLO))

    spread = onehot(iota((TILES, TQ), 1) // RANK == iota((TILES, TQ), 0))
    lists = jnp.concatenate([jnp.broadcast_to(trank[...], (4, TILES)), jnp.broadcast_to(trow[...], (4, TILES))], axis=0)
    over = dot(lists.astype(F32).astype(BF16), spread)
    rank_l, row_l = over[0:1], over[4:5]
    lane_q = lax.rem(iota((TILES, TQ), 1), RANK).astype(F32)
    diag_m[...] = jnp.where(lane_q < jnp.broadcast_to(rank_l, (TILES, TQ)), spread.astype(F32), 0.0)
    row_m[...] = jnp.where(iota((32, TQ), 0) // 8 == jnp.broadcast_to(row_l, (32, TQ)).astype(I32), 1.0, 0.0)
    col_t = jnp.where(iota((128, TILES), 0) == jnp.broadcast_to(tcol[...], (128, TILES)), 1.0, 0.0)
    col_t = jnp.concatenate([col_t, jnp.zeros((128, 96), F32)], axis=1)
    sel_t[...] = jnp.transpose(col_t)[0:TILES].astype(BF16)

    at_b, at_g = iota((256, 256), 0), iota((256, 256), 1)
    source = lax.rem(at_b // 2, 8) * 32 + lax.rem(at_b // 16, 8) * 4 + at_b // 128 * 2 + lax.rem(at_b, 2)
    perm_v = onehot(at_g == source)
    vdt[...] = dot_nt(perm_v, tv[...].reshape(TQ, 256)).astype(BF16)
    split = at_b == lax.rem(at_g, 128) * 2 + at_g // 128
    ud[...] = dot(tu[...].reshape(TQ, 256), onehot(split)).astype(BF16)

    w_ext[:, 1:5, 0:8] = disp[...]

    for src, dst, at, dev, sends, comes in moves:
        @pl.when(comes)
        def _():
            remote(src, dst, halo_ss.at[at], halo_rs.at[at], dev).wait_recv()

    low_r, high_r = unpairs(rep_r[0, 0:24], (COMP, 4)), unpairs(rep_r[1, 0:24], (COMP, 4))
    w_ext[:, 1:5, 8:16] = jnp.where(row3 <= 2, high_r, low_r)
    f_ext[:, :, 8:16] = pltpu.roll(jnp.where(row3 >= 4, high_r, low_r).reshape(COMP * 4, 8, 128), 4, 1).reshape(COMP, 4, 8, 128)
    c_ext[1:5, 8:16] = jnp.where(iota((4, 8, 128), 1) <= 3, unpairs(rep_r[1, 24:26], (4,)), unpairs(rep_r[0, 24:26], (4,)))
    for s in (0, 1):
        at = 5 * s
        w_ext[:, at, 0:8] = unpairs(vol_r[s, 0:6], (COMP,))
        once_ext[:, s, 0:8] = unpairs(vol_r[s, 6:12], (COMP,))
        c_s = unpairs(vol_r[s, 18:19], (2,))
        c_ext[at, 0:8] = c_s[0]
        low_t, high_t = unpairs(cor_r[s, 0, 0:3], (6,)), unpairs(cor_r[s, 1, 0:3], (6,))
        low_c = jnp.concatenate([pltpu.roll(low_t, 4, 1), low_t], axis=0)
        high_c = jnp.concatenate([high_t, pltpu.roll(high_t, 4, 1)], axis=0)
        upper_half = row_c <= 3
        w_ext[:, at, 8:16] = jnp.where(upper_half, high_c, low_c)
        once_ext[:, s, 8:16] = jnp.where(upper_half, pltpu.roll(high_c, 6, 1), pltpu.roll(low_c, 2, 1))
        c_low, c_high = unpairs(cor_r[s, 0, 3:4], (2,)), unpairs(cor_r[s, 1, 3:4], (2,))
        c_ext[at, 8:16] = jnp.where(upper_half[0], c_high[0], c_low[0])
        beside = jnp.where(row_c == 0, pltpu.roll(low_c, 4, 1), jnp.where(row_c == 7, pltpu.roll(high_c, 4, 1), 0.0))
        twice_ext[:, s] = unpairs(vol_r[s, 12:18], (COMP,)) + c_s[1][None] * beside

    row_p = iota((1, 16, 128), 1)
    first_row = jnp.logical_or(row_p == 0, row_p == 8)
    last_row = jnp.logical_or(row_p == 7, row_p == 15)

    def across(w):
        return jnp.where(first_row, pltpu.roll(w, 1, 1), 0.0) + jnp.where(last_row, pltpu.roll(w, 15, 1), 0.0)

    def beside_in_plane(w):
        lane = iota(w.shape, 2)
        total = pltpu.roll(w, 1, 1) + pltpu.roll(w, 15, 1)
        total = total + jnp.where(lane == 0, 0.0, pltpu.roll(w, 1, 2))
        return total + jnp.where(lane == 127, 0.0, pltpu.roll(w, 127, 2))

    def sweeps(i, carry):
        w, f, cc = w_ext[i], f_ext[i], c_ext[...]
        once, twice = once_ext[i], twice_ext[i]
        low, high, own = w[0:1], w[5:6], w[1:5]
        next_own = keep * own + f + cc[1:5] * (w[0:4] + w[2:6] + beside_in_plane(own))
        low = once[0:1] + cc[0:1] * (own[0:1] + across(low))
        high = once[1:2] + cc[5:6] * (own[3:4] + across(high))
        own = next_own
        w = jnp.concatenate([low, own, high], axis=0)
        next_own = keep * own + f + cc[1:5] * (w[0:4] + w[2:6] + beside_in_plane(own))
        low = twice[0:1] + (keep * low + cc[0:1] * (own[0:1] + beside_in_plane(low)))[:, 0:8]
        high = twice[1:2] + (keep * high + cc[5:6] * (own[3:4] + beside_in_plane(high)))[:, 0:8]
        own = next_own[:, 0:8]
        w = jnp.concatenate([low, own, high], axis=0)
        field[i] = keep * own + f[:, 0:8] + cc[1:5, 0:8] * (w[0:4] + w[2:6] + beside_in_plane(next_own)[:, 0:8])
        return carry

    lax.fori_loop(0, COMP, sweeps, 0, unroll=12)

    flat = field[...].reshape(COMP * 32, 128)
    upper = flat.astype(BF16)
    lower = (flat - upper.astype(F32)).astype(BF16)
    picked = dot(jnp.concatenate([upper, lower], axis=1), ol[...]).reshape(COMP, 32, SLOTS)
    normal = wnorm[...]
    picked = jnp.sum(picked * rowhot[...][None], axis=1)
    traces = normal[0:1] * picked[0:4] + normal[1:2] * picked[4:8] + normal[2:3] * picked[8:12]
    traces = jnp.concatenate([traces, traces], axis=0) * armask[...]
    message = dot_nt(traces.astype(BF16), place[...])

    ra[hi] = message
    for peer in hi_peers:
        remote(ra.at[hi], ra.at[hi], ph_ss.at[0], ph_rs.at[0], peer).start()

    to_row, from_row = iota((64, 64), 0), iota((64, 64), 1)
    wanted = lax.rem(to_row, 16) // 2 * 8 + lax.rem(to_row, 2) * 4 + to_row // 16
    reorder = onehot(from_row == wanted)

    def wait_all(region, at, peer):
        remote(region, region, ph_ss.at[at], ph_rs.at[at], peer).wait_recv()

    wait_all(ra.at[pl.ds(0, NHI - 1)], 0, hi_peers[0])
    mine = dot(reorder, ra[...].reshape(64, 128).astype(BF16)).astype(BF16).reshape(4, 16, 128)
    g[c, y] = mine
    for peer in y_peers:
        remote(g.at[c, y], g.at[c, y], ph_ss.at[1], ph_rs.at[1], peer).start()
    wait_all(g.at[c, pl.ds(0, NY - 1)], 1, y_peers[0])
    remote(g.at[c], g.at[c], ph_ss.at[2], ph_rs.at[2], core_peer).start()

    row_f = iota((COMP, 8, 128), 1)
    fvol_s[0] = pairs(field[:, 3])
    fvol_s[1] = pairs(field[:, 0])
    for t in (0, 1):
        acc = jnp.zeros((COMP, 8, 128), F32)
        for p in range(4):
            shift = p + 1 if t == 0 else p
            rolled = field[:, p] if shift == 0 else pltpu.roll(field[:, p], shift, 1)
            acc = jnp.where(row_f == p, rolled, acc)
        frep_s[t] = pairs(acc)
    fmoves = []
    for s in (0, 1):
        fmoves.append((fvol_s.at[s], fvol_r.at[s], s, (vol_dev[s], r), vol_to[s], vol_from[s]))
        fmoves.append((frep_s.at[s], frep_r.at[s], 2 + s, (v, rep_dev[s]), rep_to[s], rep_from[s]))
    for src, dst, at, dev, sends, comes in fmoves:
        @pl.when(sends)
        def _():
            remote(src, dst, fhalo_ss.at[at], fhalo_rs.at[at], dev).start()

        @pl.when(jnp.logical_not(comes))
        def _():
            dst[...] = jnp.zeros(dst.shape, BF16)


    wait_all(g.at[c], 2, core_peer)

    pick = sel_t[...]
    chosen = jnp.concatenate([dot_nt(pick, g[:, :, k].reshape(256, 128)) for k in range(4)], axis=0).astype(BF16)
    every = dot(chosen, vdt[...])
    coef = jnp.sum(every.reshape(4, TILES, TQ) * diag_m[...][None], axis=1)
    coef = jnp.concatenate([coef, coef], axis=0)
    spread_c = (jnp.concatenate([coef] * 4, axis=0) * row_m[...]).astype(BF16)
    parts = dot(spread_c, ud[...])
    take = lax.rem(iota((32, 128), 0), 8) < 4
    parts = jnp.where(take, parts[:, 0:128], parts[:, 128:256])
    zs[...] = parts.reshape(4, 8, 128)

    mine_at = zh * NR + r
    for (zh_, r_), peer in zip(z_at, z_peers):
        remote(zs.at[r_], zr.at[mine_at], ph_ss.at[3], ph_rs.at[3], peer).start()
    zr[mine_at] = zs[r]

    wait_all(zr.at[pl.ds(0, 2 * NR - 1)], 3, z_peers[0])
    sums = jnp.sum(zr[...].reshape(NZH, NR, 8, 128), axis=1)
    back = jnp.concatenate([sums.reshape(16, 128), jnp.zeros((112, 128), F32)], axis=0).astype(BF16)
    ws[...] = dot_nt(sel_at[...], back).reshape(NXY, 1, 128)

    def give_back(j, carry):
        at, peer = plane_peer(j)
        remote(ws.at[at], wr.at[here], ph_ss.at[4], ph_rs.at[4], peer).start()
        return carry

    lax.fori_loop(1, NXY, give_back, 0)
    wr[here] = ws[here]
    own = jnp.where(zh == 0, sums[0], sums[1])
    wide = jnp.concatenate([own[0:4], own[4:8]], axis=1)
    join = jnp.where(at_g == lax.rem(at_b, 128) * 2 + at_b // 128, 1.0, 0.0)
    out_p[...] = jnp.dot(wide, join, precision=lax.Precision.HIGHEST, preferred_element_type=F32)

    for src, dst, at, dev, sends, comes in fmoves:
        @pl.when(comes)
        def _():
            remote(src, dst, fhalo_ss.at[at], fhalo_rs.at[at], dev).wait_recv()

    low_f, high_f = unpairs(fvol_r[0], (COMP,)), unpairs(fvol_r[1], (COMP,))
    low_y, high_y = unpairs(frep_r[0], (COMP,)), unpairs(frep_r[1], (COMP,))
    for p in range(4):
        w = field[:, p]
        total = (field[:, p - 1] if p > 0 else low_f) + (field[:, p + 1] if p < 3 else high_f)
        before = pltpu.roll(low_y, 8 - p, 1) if p > 0 else low_y
        after = pltpu.roll(high_y, 7 - p, 1)
        total = total + jnp.where(row_f == 0, before, pltpu.roll(w, 1, 1))
        total = total + jnp.where(row_f == 7, after, pltpu.roll(w, 7, 1))
        lane_f = iota((COMP, 8, 128), 2)
        total = total + jnp.where(lane_f == 0, 0.0, pltpu.roll(w, 1, 2))
        total = total + jnp.where(lane_f == 127, 0.0, pltpu.roll(w, 127, 2))
        base[:, p] = keep * w + f_ext[:, p, 0:8] + c_ext[1 + p, 0:8][None] * total

    wait_all(wr.at[pl.ds(0, NXY - 1)], 4, core_peer)

    got = wr[...].reshape(NXY, 128).astype(BF16)
    got = jnp.concatenate([got, jnp.zeros((128 - NXY, 128), BF16)], axis=0)
    per_slot = (dot(at_hot[...], got) * za_hot[...]).astype(BF16)
    wave = onehot(lax.rem(iota((8, 128), 1), 4) == iota((8, 128), 0))
    wet = dot_nt(wave, per_slot)[0:4]
    out_w[...] = wet

    normal = -wnorm[...]
    load = jnp.concatenate([normal[i:i + 1] * wet for i in range(3)], axis=0)
    rows = (load[:, None, :] * rowhot[...][None]).reshape(COMP * 32, SLOTS)
    upper = rows.astype(BF16)
    lower = (rows - upper.astype(F32)).astype(BF16)
    z_one = ol[0:128]
    placed = dot_nt(jnp.concatenate([upper, lower], axis=1), jnp.concatenate([z_one, z_one], axis=1))
    out_u[...] = base[...] + scale[...][None] * placed.reshape(COMP, 4, 8, 128)

    for src, dst, at, dev, sends, comes in moves:
        @pl.when(sends)
        def _():
            remote(src, dst, halo_ss.at[at], halo_rs.at[at], dev).wait_send()
    for src, dst, at, dev, sends, comes in fmoves:
        @pl.when(sends)
        def _():
            remote(src, dst, fhalo_ss.at[at], fhalo_rs.at[at], dev).wait_send()

    def sent(region, at, peer):
        remote(region, region, ph_ss.at[at], ph_rs.at[at], peer).wait_send()

    sent(ra.at[pl.ds(0, NHI - 1)], 0, hi_peers[0])
    sent(g.at[c, pl.ds(0, NY - 1)], 1, y_peers[0])
    sent(g.at[c], 2, core_peer)
    sent(zr.at[pl.ds(0, 2 * NR - 1)], 3, z_peers[0])
    sent(wr.at[pl.ds(0, NXY - 1)], 4, core_peer)


def hand_out(u, p, w, out_u, out_p, out_w):
    out_u[...] = u[...]
    out_p[...] = p[...]
    out_w[...] = w[...]


def shards(displacement, body_force, stiffness, wet_cell, wet_normal, route, tile_u, tile_v, tile_row, tile_col, tile_rank):
    vmem = pl.BlockSpec(memory_space=pltpu.VMEM)
    hbm = pl.BlockSpec(memory_space=pltpu.HBM)
    V = pltpu.VMEM
    updated, pressure, wet = pl.pallas_call(
        body,
        out_shape=(
            jax.ShapeDtypeStruct((COMP, 4, 8, 128), F32),
            jax.ShapeDtypeStruct((4, 256), F32),
            jax.ShapeDtypeStruct((4, SLOTS), F32),
        ),
        in_specs=[hbm] * 11,
        out_specs=(vmem, vmem, vmem),
        scratch_shapes=[
            V((COMP, 4, 8, 128), F32), V((COMP, 4, 8, 128), F32), V((4, 8, 128), F32),
            V((1, SLOTS), I32), V((3, SLOTS), F32), V((1, SLOTS), I32),
            V((TILES, RANK, 256), BF16), V((TILES, RANK, 256), BF16),
            V((1, TILES), I32), V((1, TILES), I32), V((1, TILES), I32),
            V((2, 19, 16, 128), BF16), V((2, 19, 16, 128), BF16),
            V((2, 26, 16, 128), BF16), V((2, 26, 16, 128), BF16),
            V((2, 2, 4, 16, 128), BF16), V((2, 2, 4, 16, 128), BF16),
            V((2, 6, 16, 128), BF16), V((2, 6, 16, 128), BF16),
            V((2, 6, 16, 128), BF16), V((2, 6, 16, 128), BF16),
            V((COMP, 6, 16, 128), F32), V((COMP, 4, 16, 128), F32), V((6, 16, 128), F32),
            V((COMP, 2, 16, 128), F32), V((COMP, 2, 8, 128), F32),
            V((COMP, 4, 8, 128), F32), V((COMP, 4, 8, 128), F32), V((4, 8, 128), F32),
            V((256, TQ), BF16), V((TQ, 256), BF16), V((256, SLOTS), BF16), V((32, SLOTS), F32),
            V((8, SLOTS), F32), V((128, SLOTS), BF16), V((TILES, 128), BF16), V((TILES, TQ), F32),
            V((32, TQ), F32), V((NXY, NV), BF16), V((SLOTS, 128), BF16), V((SLOTS, 128), F32),
            V((NHI, 8, 128), F32), V((NC, NY, 4, 16, 128), BF16),
            V((NR, 8, 128), F32), V((NZH * NR, 8, 128), F32),
            V((NXY, 1, 128), F32), V((NXY, 1, 128), F32),
            pltpu.SemaphoreType.DMA((11,)),
            pltpu.SemaphoreType.DMA((8,)), pltpu.SemaphoreType.DMA((8,)),
            pltpu.SemaphoreType.DMA((4,)), pltpu.SemaphoreType.DMA((4,)),
            pltpu.SemaphoreType.DMA((5,)), pltpu.SemaphoreType.DMA((5,)),
        ],
        compiler_params=pltpu.CompilerParams(collective_id=0, has_side_effects=True, vmem_limit_bytes=56 << 20),
    )(
        displacement.reshape(COMP, 4, 8, 128),
        body_force.reshape(COMP, 4, 8, 128),
        stiffness,
        wet_cell,
        wet_normal,
        route.reshape(1, SLOTS),
        tile_u,
        tile_v,
        tile_row.reshape(1, TILES),
        tile_col.reshape(1, TILES),
        tile_rank.reshape(1, TILES),
    )
    updated, pressure, wet = pl.pallas_call(
        hand_out,
        out_shape=(
            jax.ShapeDtypeStruct((COMP, 4, 8, 128), F32),
            jax.ShapeDtypeStruct((4, 256), F32),
            jax.ShapeDtypeStruct((4, SLOTS), F32),
        ),
        in_specs=[vmem] * 3,
        out_specs=(vmem, vmem, vmem),
        compiler_params=pltpu.CompilerParams(vmem_limit_bytes=56 << 20),
    )(updated, pressure, wet)
    return updated.reshape(displacement.shape), pressure, wet


def solution(mesh):
    return jax.shard_map(
        shards,
        mesh=mesh,
        in_specs=(
            P(None, None, "vol", "rep", None),
            P(None, None, "vol", "rep", None),
            P("vol", "rep", None),
            P(("vol", "rep"), None),
            P(None, ("vol", "rep")),
            P(("vol", "rep"), None),
            P(("vol", "rep"), None, None),
            P(("vol", "rep"), None, None),
            P(("vol", "rep")),
            P(("vol", "rep")),
            P(("vol", "rep")),
        ),
        out_specs=(
            P(None, None, "vol", "rep", None),
            P(None, ("vol", "rep")),
            P(None, ("vol", "rep")),
        ),
        check_vma=False,
    )
```

```python
import jax
import jax.numpy as jnp
from jax import lax
from jax.experimental import pallas as pl
from jax.experimental.pallas import tpu as pltpu
from jax.sharding import PartitionSpec as P

MESH = pl.DeviceIdType.MESH
relax_factor = 0.8
mass_shift = 1.0

F32 = jnp.float32
BF16 = jnp.bfloat16
I32 = jnp.int32

NX, NZH, NY, NC = 4, 2, 8, 2
NR = 4
NHI = NX * NZH
NLO = NY * NC
NV = NHI * NLO
NXY = NX * NLO
SLOTS = 128
COMP = 12
TILES, RANK = 32, 32
TQ = TILES * RANK

NT = (((1,), (1,)), ((), ()))


def dot(a, b):
    return jnp.dot(a, b, preferred_element_type=F32)


def dot_nt(a, b):
    return lax.dot_general(a, b, NT, preferred_element_type=F32)


def iota(shape, dim):
    return lax.broadcasted_iota(I32, shape, dim)


def onehot(condition, dtype=BF16):
    return jnp.where(condition, 1.0, 0.0).astype(F32).astype(dtype)


def pairs(tiles):
    lead = 1
    for size in tiles.shape[:-2]:
        lead *= size
    return tiles.reshape(lead // 2, 16, 128).astype(BF16)


def unpairs(tiles, lead):
    return tiles.astype(F32).reshape(*lead, 8, 128)


def body(
    disp_h, force_h, stiff_h, wcell_h, wnorm_h, route_h, tu_h, tv_h, trow_h, tcol_h, trank_h,
    out_u, out_p, out_w,
    disp, force, stiff, wcell, wnorm, route, tu, tv, trow, tcol, trank,
    vol_s, vol_r, rep_s, rep_r, cor_s, cor_r, fvol_s, fvol_r, frep_s, frep_r,
    alone, f_own, c_own, ring_w, ring_once, ring_twice, ring_c, face_w, face_once, face_twice, face_c,
    corner_w, corner_once, corner_c, field, base, scale,
    vdt, ud, ol, rowhot, armask, place, sel_t, diag_m, row_m, sel_at, at_hot, za_hot,
    ra, g, zs, zr, ws, wr,
    load_sem, halo_ss, halo_rs, fhalo_ss, fhalo_rs, ph_ss, ph_rs,
):
    v = lax.axis_index("vol")
    r = lax.axis_index("rep")
    hi, lo = v // NLO, lax.rem(v, NLO)
    x, zh = hi // NZH, lax.rem(hi, NZH)
    y, c = lo // NC, lax.rem(lo, NC)

    def vol_of(x_, zh_, y_, c_):
        return ((x_ * NZH + zh_) * NY + y_) * NC + c_

    hi_peers = [(lax.rem(hi + j, NHI) * NLO + lo, r) for j in range(1, NHI)]
    y_peers = [(vol_of(x, zh, lax.rem(y + j, NY), c), r) for j in range(1, NY)]
    core_peer = (vol_of(x, zh, y, 1 - c), r)
    here = x * NLO + lo

    def plane_peer(j):
        at = lax.rem(here + j, NXY)
        return at, (at // NLO * (NZH * NLO) + zh * NLO + lax.rem(at, NLO), r)

    z_at = [(zh, lax.rem(r + j, NR)) for j in range(1, NR)] + [(1 - zh, lax.rem(r + j, NR)) for j in range(NR)]
    z_peers = [(vol_of(x, zh_, y, c), r_) for zh_, r_ in z_at]
    up_v, down_v = lax.rem(v + 1, NV), lax.rem(v + NV - 1, NV)
    up_r, down_r = lax.rem(r + 1, NR), lax.rem(r + NR - 1, NR)
    halo_peers = [(up_v, r), (down_v, r)] + [(a, b) for a in (up_v, down_v) for b in (up_r, down_r)]

    barrier = pltpu.get_barrier_semaphore()
    greeted = halo_peers + hi_peers + z_peers + y_peers + [core_peer]
    for peer in greeted:
        pl.semaphore_signal(barrier, inc=1, device_id=peer, device_id_type=MESH)

    sources = (disp_h, force_h, stiff_h, wcell_h, wnorm_h, route_h, trow_h, tcol_h, trank_h, tv_h, tu_h)
    targets = (disp, force, stiff, wcell, wnorm, route, trow, tcol, trank, tv, tu)
    loads = [pltpu.make_async_copy(a, b, load_sem.at[i]) for i, (a, b) in enumerate(zip(sources, targets))]
    for load in loads:
        load.start()
    for load in loads[:3]:
        load.wait()

    keep = 1.0 - relax_factor

    def rolled(w, shift, axis):
        shift = shift % (8 if axis == w.ndim - 2 else 128)
        if shift == 0:
            return w
        return pltpu.roll(w.reshape(-1, 8, 128), shift, axis - w.ndim + 3).reshape(w.shape)

    def sides(w, ring):
        row = iota(w.shape, w.ndim - 2)
        axis = w.ndim - 2
        before, after = rolled(ring, 1, axis), rolled(ring, 7, axis)
        return jnp.where(row == 0, before, rolled(w, 1, axis)) + jnp.where(row == 7, after, rolled(w, 7, axis))

    def from_ring(ring):
        row = iota(ring.shape, ring.ndim - 2)
        axis = ring.ndim - 2
        return jnp.where(row == 0, rolled(ring, 1, axis), jnp.where(row == 7, rolled(ring, 7, axis), 0.0))

    def to_ring(w):
        row = iota(w.shape, w.ndim - 2)
        axis = w.ndim - 2
        return jnp.where(row == 0, rolled(w, 1, axis), rolled(w, 7, axis))

    def along_z(w):
        lane = iota(w.shape, w.ndim - 1)
        axis = w.ndim - 1
        return jnp.where(lane == 0, 0.0, rolled(w, 1, axis)) + jnp.where(lane == 127, 0.0, rolled(w, 127, axis))

    row_c = iota((COMP, 8, 128), 1)
    own_inv = relax_factor / (mass_shift + 6.0 * stiff[...])
    own_c = own_inv * stiff[...]
    scale[...] = own_inv
    c_own[...] = own_c
    f_own[...] = force[...] * own_inv[None]
    for p in range(4):
        w = disp[:, p]
        total = sides(w, jnp.zeros_like(w)) + along_z(w)
        if p > 0:
            total = total + disp[:, p - 1]
        if p < 3:
            total = total + disp[:, p + 1]
        alone[:, p] = keep * w + f_own[:, p] + own_c[p][None] * total

    def row_of_planes(plane, row, start):
        out = None
        for p in range(4):
            moved = rolled(plane(p), start + p - row, 1)
            out = moved if out is None else jnp.where(iota(moved.shape, 1) == start + p, moved, out)
        return out

    for side in (0, 1):
        edge, second = (3, 2) if side == 0 else (0, 1)
        w_e, w_2, once = disp[:, edge], disp[:, second], alone[:, edge]
        c_e = own_c[edge]
        vol_s[side, 0:6] = pairs(w_e)
        vol_s[side, 6:12] = pairs(once)
        vol_s[side, 12:18] = pairs(f_own[:, edge] + c_e[None] * alone[:, second])
        vol_s[side, 18:19] = pairs(jnp.stack([c_e, c_e * own_c[second]]))
        up = jnp.where(row_c >= 6, w_e, jnp.where(row_c == 5, rolled(once, 6, 1), rolled(w_2, 5, 1)))
        down = jnp.where(row_c <= 1, w_e, jnp.where(row_c == 2, rolled(once, 2, 1), rolled(w_2, 3, 1)))
        half = row_c[0:6] >= 4
        cor_s[side, 0, 0:3] = pairs(jnp.where(half, up[6:12], rolled(up[0:6], 4, 1)))
        cor_s[side, 1, 0:3] = pairs(jnp.where(half, rolled(down[6:12], 4, 1), down[0:6]))
        for t in (0, 1):
            cor_s[side, t, 3:4] = pairs(jnp.stack([c_e, c_e]))
        row, inner = (7, 1) if side == 0 else (0, 7)
        first = row_of_planes(lambda p: disp[:, p], row, 0)
        then = row_of_planes(lambda p: alone[:, p], row, 4)
        rep_s[side, 0:6] = pairs(jnp.where(row_c < 4, first, then))
        last = [row_of_planes(lambda p: f_own[a:a + 6, p] + own_c[p][None] * rolled(alone[a:a + 6, p], inner, 1), row, start)
                for a, start in ((0, 0), (6, 4))]
        rep_s[side, 6:9] = pairs(jnp.where(half, last[1], last[0]))
        c_rows = row_of_planes(lambda p: own_c[p:p + 1], row, 0)
        cc_rows = row_of_planes(lambda p: own_c[p:p + 1] * rolled(own_c[p:p + 1], inner, 1), row, 4)
        c_rows = jnp.where(row_c[0:1] < 4, c_rows, cc_rows)
        rep_s[side, 9:10] = pairs(jnp.concatenate([c_rows, c_rows], axis=0))

    vol_to = [v < NV - 1, v > 0]
    vol_from = [v > 0, v < NV - 1]
    rep_to = [r < NR - 1, r > 0]
    rep_from = [r > 0, r < NR - 1]
    vol_dev, rep_dev = [up_v, down_v], [up_r, down_r]

    moves = []
    for s in (0, 1):
        moves.append((vol_s.at[s], vol_r.at[s], s, (vol_dev[s], r), vol_to[s], vol_from[s]))
    for s in (0, 1):
        for t in (0, 1):
            moves.append((cor_s.at[s, t], cor_r.at[s, t], 4 + 2 * s + t, (vol_dev[s], rep_dev[t]),
                          jnp.logical_and(vol_to[s], rep_to[t]), jnp.logical_and(vol_from[s], rep_from[t])))
    for t in (0, 1):
        moves.append((rep_s.at[t], rep_r.at[t], 2 + t, (v, rep_dev[t]), rep_to[t], rep_from[t]))

    def remote(src, dst, ss, rs, dev):
        return pltpu.make_async_remote_copy(src_ref=src, dst_ref=dst, send_sem=ss, recv_sem=rs, device_id=dev, device_id_type=MESH)

    for src, dst, at, dev, sends, comes in moves:
        @pl.when(jnp.logical_not(comes))
        def _():
            dst[...] = jnp.zeros(dst.shape, BF16)

    pl.semaphore_wait(barrier, len(greeted))

    for src, dst, at, dev, sends, comes in moves:
        @pl.when(sends)
        def _():
            remote(src, dst, halo_ss.at[at], halo_rs.at[at], dev).start()

    for load in loads[3:]:
        load.wait()
    route_row = route[...]
    route_sq = jnp.broadcast_to(route_row, (SLOTS, SLOTS))
    route_col = jnp.transpose(route_sq.astype(F32)).astype(I32)
    sub = iota((SLOTS, SLOTS), 0)
    lane = iota((SLOTS, SLOTS), 1)
    earlier = jnp.where(jnp.logical_and(route_col == route_sq, sub < lane), 1.0, 0.0)
    arrival = jnp.sum(earlier, axis=0, keepdims=True).astype(I32)
    place[...] = onehot(sub == route_sq)
    armask[...] = jnp.where(iota((8, SLOTS), 0) // 4 == jnp.broadcast_to(arrival, (8, SLOTS)), 1.0, 0.0)
    cell = wcell[...]
    z_one = onehot(sub == jnp.broadcast_to(lax.rem(cell, 128), (SLOTS, SLOTS)))
    ol[0:128] = z_one
    ol[128:256] = z_one
    rowhot[...] = jnp.where(iota((32, SLOTS), 0) == jnp.broadcast_to(cell // 128, (32, SLOTS)), 1.0, 0.0)
    owner_at = route_row // (NZH * NLO) * NLO + lax.rem(route_row, NLO)
    at_t = jnp.where(sub == jnp.broadcast_to(owner_at, (SLOTS, SLOTS)), 1.0, 0.0)
    at_hot[...] = jnp.transpose(at_t).astype(BF16)
    za = lax.rem(route_row // NLO, NZH) * 2 + arrival
    za_t = jnp.where(sub // 4 == jnp.broadcast_to(za, (SLOTS, SLOTS)), 1.0, 0.0)
    za_hot[...] = jnp.transpose(za_t)
    at_row = iota((NXY, NV), 0)
    sel_at[...] = onehot(iota((NXY, NV), 1) == at_row // NLO * (NZH * NLO) + zh * NLO + lax.rem(at_row, NLO))

    spread = onehot(iota((TILES, TQ), 1) // RANK == iota((TILES, TQ), 0))
    lists = jnp.concatenate([jnp.broadcast_to(trank[...], (4, TILES)), jnp.broadcast_to(trow[...], (4, TILES))], axis=0)
    over = dot(lists.astype(F32).astype(BF16), spread)
    rank_l, row_l = over[0:1], over[4:5]
    lane_q = lax.rem(iota((TILES, TQ), 1), RANK).astype(F32)
    diag_m[...] = jnp.where(lane_q < jnp.broadcast_to(rank_l, (TILES, TQ)), spread.astype(F32), 0.0)
    row_m[...] = jnp.where(iota((32, TQ), 0) // 8 == jnp.broadcast_to(row_l, (32, TQ)).astype(I32), 1.0, 0.0)
    col_t = jnp.where(iota((128, TILES), 0) == jnp.broadcast_to(tcol[...], (128, TILES)), 1.0, 0.0)
    col_t = jnp.concatenate([col_t, jnp.zeros((128, 96), F32)], axis=1)
    sel_t[...] = jnp.transpose(col_t)[0:TILES].astype(BF16)

    at_b, at_g = iota((256, 256), 0), iota((256, 256), 1)
    source = lax.rem(at_b, 8) * 32 + lax.rem(at_b // 16, 8) * 4 + at_b // 128 * 2 + lax.rem(at_b // 8, 2)
    perm_v = onehot(at_g == source)
    vdt[...] = dot_nt(perm_v, tv[...].reshape(TQ, 256)).astype(BF16)
    split = at_b == lax.rem(at_g, 128) * 2 + at_g // 128
    ud[...] = dot(tu[...].reshape(TQ, 256), onehot(split)).astype(BF16)

    for src, dst, at, dev, sends, comes in moves:
        @pl.when(comes)
        def _():
            remote(src, dst, halo_ss.at[at], halo_rs.at[at], dev).wait_recv()

    upper_half = row_c <= 3

    def ring_of(low, high, start):
        return [jnp.where(iota(low.shape, 1) <= 3, rolled(high, -start - p, 1), rolled(low, 7 - start - p, 1)) for p in range(4)]

    low_r, high_r = unpairs(rep_r[0, 0:6], (COMP,)), unpairs(rep_r[1, 0:6], (COMP,))
    for p, (w, once) in enumerate(zip(ring_of(low_r, high_r, 0), ring_of(low_r, high_r, 4))):
        ring_w[:, p] = w
        ring_once[:, p] = once
    low_r, high_r = unpairs(rep_r[0, 6:9], (6,)), unpairs(rep_r[1, 6:9], (6,))
    for p, (a, b) in enumerate(zip(ring_of(low_r, high_r, 0), ring_of(low_r, high_r, 4))):
        ring_twice[0:6, p] = a
        ring_twice[6:12, p] = b
    low_r, high_r = unpairs(rep_r[0, 9:10], (2,))[0:1], unpairs(rep_r[1, 9:10], (2,))[0:1]
    ring_cc = ring_of(low_r, high_r, 4)
    for p, part in enumerate(ring_of(low_r, high_r, 0)):
        ring_c[p:p + 1] = part
    for s in (0, 1):
        face_w[:, s] = unpairs(vol_r[s, 0:6], (COMP,))
        face_once[:, s] = unpairs(vol_r[s, 6:12], (COMP,))
        c_s = unpairs(vol_r[s, 18:19], (2,))
        face_c[s] = c_s[0]
        low_t, high_t = unpairs(cor_r[s, 0, 0:3], (6,)), unpairs(cor_r[s, 1, 0:3], (6,))
        low_c = jnp.concatenate([rolled(low_t, 4, 1), low_t], axis=0)
        high_c = jnp.concatenate([high_t, rolled(high_t, 4, 1)], axis=0)
        corner_w[:, s] = jnp.where(upper_half, high_c, low_c)
        corner_once[:, s] = jnp.where(upper_half, rolled(high_c, 6, 1), rolled(low_c, 2, 1))
        c_low, c_high = unpairs(cor_r[s, 0, 3:4], (2,)), unpairs(cor_r[s, 1, 3:4], (2,))
        corner_c[s] = jnp.where(upper_half[0], c_high[0], c_low[0])
        beside = jnp.where(row_c == 0, rolled(low_c, 4, 1), jnp.where(row_c == 7, rolled(high_c, 4, 1), 0.0))
        face_twice[:, s] = unpairs(vol_r[s, 12:18], (COMP,)) + c_s[1][None] * beside
        below = jnp.where(upper_half, rolled(high_c, 7, 1), rolled(low_c, 1, 1))
        ring_twice[:, 3 * s] = ring_twice[:, 3 * s] + ring_cc[3 * s] * below

    def sweeps(i, carry):
        own, ring = disp[i], ring_w[i]
        f, cc, c_r, c_f, c_x = f_own[i], c_own[...], ring_c[...], face_c[...], corner_c[...]
        face, corner = face_w[i], corner_w[i]

        def beside(w, ends):
            wide = jnp.concatenate([ends[0:1], w, ends[1:2]], axis=0)
            return wide[0:4] + wide[2:6]

        def ends_of(w):
            return jnp.concatenate([w[0:1], w[3:4]], axis=0)

        zero = jnp.zeros((2, 8, 128), F32)
        from_faces = jnp.concatenate([face[0:1], zero, face[1:2]], axis=0)
        from_corners = jnp.concatenate([corner[0:1], zero, corner[1:2]], axis=0)
        own_1 = alone[i] + cc * (from_faces + from_ring(ring))
        ring_1 = ring_once[i] + c_r * (to_ring(own) + from_corners)
        face_1 = face_once[i] + c_f * (ends_of(own) + from_ring(corner))
        corner_1 = corner_once[i] + c_x * (ends_of(ring) + to_ring(face))
        own_2 = keep * own_1 + f + cc * (beside(own_1, face_1) + sides(own_1, ring_1) + along_z(own_1))
        ring_2 = ring_twice[i] + keep * ring_1 + c_r * (to_ring(own_1) + beside(ring_1, corner_1) + along_z(ring_1))
        face_2 = face_twice[i] + keep * face_1 + c_f * (ends_of(own_1) + sides(face_1, corner_1) + along_z(face_1))
        field[i] = keep * own_2 + f + cc * (beside(own_2, face_2) + sides(own_2, ring_2) + along_z(own_2))
        return carry

    lax.fori_loop(0, COMP, sweeps, 0, unroll=12)

    flat = field[...].reshape(COMP * 32, 128)
    upper = flat.astype(BF16)
    lower = (flat - upper.astype(F32)).astype(BF16)
    picked = dot(jnp.concatenate([upper, lower], axis=1), ol[...]).reshape(COMP, 32, SLOTS)
    normal = wnorm[...]
    picked = jnp.sum(picked * rowhot[...][None], axis=1)
    traces = normal[0:1] * picked[0:4] + normal[1:2] * picked[4:8] + normal[2:3] * picked[8:12]
    traces = jnp.concatenate([traces, traces], axis=0) * armask[...]
    message = dot_nt(traces.astype(BF16), place[...])

    ra[hi] = message
    for peer in hi_peers:
        remote(ra.at[hi], ra.at[hi], ph_ss.at[0], ph_rs.at[0], peer).start()

    def wait_all(region, at, peer):
        remote(region, region, ph_ss.at[at], ph_rs.at[at], peer).wait_recv()

    wait_all(ra.at[pl.ds(0, NHI - 1)], 0, hi_peers[0])
    for k in range(4):
        g[c, y, k] = jnp.concatenate([ra[:, k], ra[:, 4 + k]], axis=0).astype(BF16)
    for peer in y_peers:
        remote(g.at[c, y], g.at[c, y], ph_ss.at[1], ph_rs.at[1], peer).start()
    row_f = iota((COMP, 8, 128), 1)
    fvol_s[0] = pairs(field[:, 3])
    fvol_s[1] = pairs(field[:, 0])
    for t in (0, 1):
        acc = jnp.zeros((COMP, 8, 128), F32)
        for p in range(4):
            shift = p + 1 if t == 0 else p
            acc = jnp.where(row_f == p, rolled(field[:, p], shift, 1), acc)
        frep_s[t] = pairs(acc)
    fmoves = []
    for s in (0, 1):
        fmoves.append((fvol_s.at[s], fvol_r.at[s], s, (vol_dev[s], r), vol_to[s], vol_from[s]))
        fmoves.append((frep_s.at[s], frep_r.at[s], 2 + s, (v, rep_dev[s]), rep_to[s], rep_from[s]))
    for src, dst, at, dev, sends, comes in fmoves:
        @pl.when(sends)
        def _():
            remote(src, dst, fhalo_ss.at[at], fhalo_rs.at[at], dev).start()

        @pl.when(jnp.logical_not(comes))
        def _():
            dst[...] = jnp.zeros(dst.shape, BF16)


    wait_all(g.at[c, pl.ds(0, NY - 1)], 1, y_peers[0])
    remote(g.at[c], g.at[c], ph_ss.at[2], ph_rs.at[2], core_peer).start()

    wait_all(g.at[c], 2, core_peer)

    pick = sel_t[...]
    chosen = jnp.concatenate([dot_nt(pick, g[:, :, k].reshape(256, 128)) for k in range(4)], axis=0).astype(BF16)
    every = dot(chosen, vdt[...])
    coef = jnp.sum(every.reshape(4, TILES, TQ) * diag_m[...][None], axis=1)
    coef = jnp.concatenate([coef, coef], axis=0)
    spread_c = (jnp.concatenate([coef] * 4, axis=0) * row_m[...]).astype(BF16)
    parts = dot(spread_c, ud[...])
    take = lax.rem(iota((32, 128), 0), 8) < 4
    parts = jnp.where(take, parts[:, 0:128], parts[:, 128:256])
    zs[...] = parts.reshape(4, 8, 128)

    mine_at = zh * NR + r
    for (zh_, r_), peer in zip(z_at, z_peers):
        remote(zs.at[r_], zr.at[mine_at], ph_ss.at[3], ph_rs.at[3], peer).start()
    zr[mine_at] = zs[r]

    wait_all(zr.at[pl.ds(0, 2 * NR - 1)], 3, z_peers[0])
    sums = jnp.sum(zr[...].reshape(NZH, NR, 8, 128), axis=1)
    back = jnp.concatenate([sums.reshape(16, 128), jnp.zeros((112, 128), F32)], axis=0).astype(BF16)
    ws[...] = dot_nt(sel_at[...], back).reshape(NXY, 1, 128)

    def give_back(j, carry):
        at, peer = plane_peer(j)
        remote(ws.at[at], wr.at[here], ph_ss.at[4], ph_rs.at[4], peer).start()
        return carry

    lax.fori_loop(1, NXY, give_back, 0)
    wr[here] = ws[here]
    own = jnp.where(zh == 0, sums[0], sums[1])
    wide = jnp.concatenate([own[0:4], own[4:8]], axis=1)
    join = jnp.where(at_g == lax.rem(at_b, 128) * 2 + at_b // 128, 1.0, 0.0)
    out_p[...] = jnp.dot(wide, join, precision=lax.Precision.HIGHEST, preferred_element_type=F32)

    for src, dst, at, dev, sends, comes in fmoves:
        @pl.when(comes)
        def _():
            remote(src, dst, fhalo_ss.at[at], fhalo_rs.at[at], dev).wait_recv()

    low_f, high_f = unpairs(fvol_r[0], (COMP,)), unpairs(fvol_r[1], (COMP,))
    low_y, high_y = unpairs(frep_r[0], (COMP,)), unpairs(frep_r[1], (COMP,))
    for p in range(4):
        w = field[:, p]
        total = (field[:, p - 1] if p > 0 else low_f) + (field[:, p + 1] if p < 3 else high_f)
        before = pltpu.roll(low_y, 8 - p, 1) if p > 0 else low_y
        after = pltpu.roll(high_y, 7 - p, 1)
        total = total + jnp.where(row_f == 0, before, pltpu.roll(w, 1, 1))
        total = total + jnp.where(row_f == 7, after, pltpu.roll(w, 7, 1))
        lane_f = iota((COMP, 8, 128), 2)
        total = total + jnp.where(lane_f == 0, 0.0, pltpu.roll(w, 1, 2))
        total = total + jnp.where(lane_f == 127, 0.0, pltpu.roll(w, 127, 2))
        base[:, p] = keep * w + f_own[:, p] + c_own[p][None] * total

    wait_all(wr.at[pl.ds(0, NXY - 1)], 4, core_peer)

    got = wr[...].reshape(NXY, 128).astype(BF16)
    got = jnp.concatenate([got, jnp.zeros((128 - NXY, 128), BF16)], axis=0)
    per_slot = (dot(at_hot[...], got) * za_hot[...]).astype(BF16)
    wave = onehot(lax.rem(iota((8, 128), 1), 4) == iota((8, 128), 0))
    wet = dot_nt(wave, per_slot)[0:4]
    out_w[...] = wet

    normal = -wnorm[...]
    load = jnp.concatenate([normal[i:i + 1] * wet for i in range(3)], axis=0)
    rows = (load[:, None, :] * rowhot[...][None]).reshape(COMP * 32, SLOTS)
    upper = rows.astype(BF16)
    lower = (rows - upper.astype(F32)).astype(BF16)
    z_one = ol[0:128]
    placed = dot_nt(jnp.concatenate([upper, lower], axis=1), jnp.concatenate([z_one, z_one], axis=1))
    out_u[...] = base[...] + scale[...][None] * placed.reshape(COMP, 4, 8, 128)

    for src, dst, at, dev, sends, comes in moves:
        @pl.when(sends)
        def _():
            remote(src, dst, halo_ss.at[at], halo_rs.at[at], dev).wait_send()
    for src, dst, at, dev, sends, comes in fmoves:
        @pl.when(sends)
        def _():
            remote(src, dst, fhalo_ss.at[at], fhalo_rs.at[at], dev).wait_send()

    def sent(region, at, peer):
        remote(region, region, ph_ss.at[at], ph_rs.at[at], peer).wait_send()

    sent(ra.at[pl.ds(0, NHI - 1)], 0, hi_peers[0])
    sent(g.at[c, pl.ds(0, NY - 1)], 1, y_peers[0])
    sent(g.at[c], 2, core_peer)
    sent(zr.at[pl.ds(0, 2 * NR - 1)], 3, z_peers[0])
    sent(wr.at[pl.ds(0, NXY - 1)], 4, core_peer)


def hand_out(u, p, w, out_u, out_p, out_w):
    out_u[...] = u[...]
    out_p[...] = p[...]
    out_w[...] = w[...]


def shards(displacement, body_force, stiffness, wet_cell, wet_normal, route, tile_u, tile_v, tile_row, tile_col, tile_rank):
    vmem = pl.BlockSpec(memory_space=pltpu.VMEM)
    hbm = pl.BlockSpec(memory_space=pltpu.HBM)
    V = pltpu.VMEM
    updated, pressure, wet = pl.pallas_call(
        body,
        out_shape=(
            jax.ShapeDtypeStruct((COMP, 4, 8, 128), F32),
            jax.ShapeDtypeStruct((4, 256), F32),
            jax.ShapeDtypeStruct((4, SLOTS), F32),
        ),
        in_specs=[hbm] * 11,
        out_specs=(vmem, vmem, vmem),
        scratch_shapes=[
            V((COMP, 4, 8, 128), F32), V((COMP, 4, 8, 128), F32), V((4, 8, 128), F32),
            V((1, SLOTS), I32), V((3, SLOTS), F32), V((1, SLOTS), I32),
            V((TILES, RANK, 256), BF16), V((TILES, RANK, 256), BF16),
            V((1, TILES), I32), V((1, TILES), I32), V((1, TILES), I32),
            V((2, 19, 16, 128), BF16), V((2, 19, 16, 128), BF16),
            V((2, 10, 16, 128), BF16), V((2, 10, 16, 128), BF16),
            V((2, 2, 4, 16, 128), BF16), V((2, 2, 4, 16, 128), BF16),
            V((2, 6, 16, 128), BF16), V((2, 6, 16, 128), BF16),
            V((2, 6, 16, 128), BF16), V((2, 6, 16, 128), BF16),
            V((COMP, 4, 8, 128), F32), V((COMP, 4, 8, 128), F32), V((4, 8, 128), F32),
            V((COMP, 4, 8, 128), F32), V((COMP, 4, 8, 128), F32), V((COMP, 4, 8, 128), F32), V((4, 8, 128), F32),
            V((COMP, 2, 8, 128), F32), V((COMP, 2, 8, 128), F32), V((COMP, 2, 8, 128), F32), V((2, 8, 128), F32),
            V((COMP, 2, 8, 128), F32), V((COMP, 2, 8, 128), F32), V((2, 8, 128), F32),
            V((COMP, 4, 8, 128), F32), V((COMP, 4, 8, 128), F32), V((4, 8, 128), F32),
            V((256, TQ), BF16), V((TQ, 256), BF16), V((256, SLOTS), BF16), V((32, SLOTS), F32),
            V((8, SLOTS), F32), V((128, SLOTS), BF16), V((TILES, 128), BF16), V((TILES, TQ), F32),
            V((32, TQ), F32), V((NXY, NV), BF16), V((SLOTS, 128), BF16), V((SLOTS, 128), F32),
            V((NHI, 8, 128), F32), V((NC, NY, 4, 16, 128), BF16),
            V((NR, 8, 128), F32), V((NZH * NR, 8, 128), F32),
            V((NXY, 1, 128), F32), V((NXY, 1, 128), F32),
            pltpu.SemaphoreType.DMA((11,)),
            pltpu.SemaphoreType.DMA((8,)), pltpu.SemaphoreType.DMA((8,)),
            pltpu.SemaphoreType.DMA((4,)), pltpu.SemaphoreType.DMA((4,)),
            pltpu.SemaphoreType.DMA((5,)), pltpu.SemaphoreType.DMA((5,)),
        ],
        compiler_params=pltpu.CompilerParams(collective_id=0, has_side_effects=True, vmem_limit_bytes=56 << 20),
    )(
        displacement.reshape(COMP, 4, 8, 128),
        body_force.reshape(COMP, 4, 8, 128),
        stiffness,
        wet_cell,
        wet_normal,
        route.reshape(1, SLOTS),
        tile_u,
        tile_v,
        tile_row.reshape(1, TILES),
        tile_col.reshape(1, TILES),
        tile_rank.reshape(1, TILES),
    )
    updated, pressure, wet = pl.pallas_call(
        hand_out,
        out_shape=(
            jax.ShapeDtypeStruct((COMP, 4, 8, 128), F32),
            jax.ShapeDtypeStruct((4, 256), F32),
            jax.ShapeDtypeStruct((4, SLOTS), F32),
        ),
        in_specs=[vmem] * 3,
        out_specs=(vmem, vmem, vmem),
        compiler_params=pltpu.CompilerParams(vmem_limit_bytes=56 << 20),
    )(updated, pressure, wet)
    return updated.reshape(displacement.shape), pressure, wet


def solution(mesh):
    return jax.shard_map(
        shards,
        mesh=mesh,
        in_specs=(
            P(None, None, "vol", "rep", None),
            P(None, None, "vol", "rep", None),
            P("vol", "rep", None),
            P(("vol", "rep"), None),
            P(None, ("vol", "rep")),
            P(("vol", "rep"), None),
            P(("vol", "rep"), None, None),
            P(("vol", "rep"), None, None),
            P(("vol", "rep")),
            P(("vol", "rep")),
            P(("vol", "rep")),
        ),
        out_specs=(
            P(None, None, "vol", "rep", None),
            P(None, ("vol", "rep")),
            P(None, ("vol", "rep")),
        ),
        check_vma=False,
    )
```

```python
import jax
import jax.numpy as jnp
from jax import lax
from jax.experimental import pallas as pl
from jax.experimental.pallas import tpu as pltpu
from jax.sharding import PartitionSpec as P

MESH = pl.DeviceIdType.MESH
relax_factor = 0.8
mass_shift = 1.0

F32 = jnp.float32
BF16 = jnp.bfloat16
I32 = jnp.int32

NX, NZH, NY, NC = 4, 2, 8, 2
NR = 4
NHI = NX * NZH
NLO = NY * NC
NV = NHI * NLO
NXY = NX * NLO
SLOTS = 128
COMP = 12
TILES, RANK = 32, 32
TQ = TILES * RANK

NT = (((1,), (1,)), ((), ()))


def dot(a, b):
    return jnp.dot(a, b, preferred_element_type=F32)


def dot_nt(a, b):
    return lax.dot_general(a, b, NT, preferred_element_type=F32)


def iota(shape, dim):
    return lax.broadcasted_iota(I32, shape, dim)


def onehot(condition, dtype=BF16):
    return jnp.where(condition, 1.0, 0.0).astype(F32).astype(dtype)


def pairs(tiles):
    lead = 1
    for size in tiles.shape[:-2]:
        lead *= size
    return tiles.reshape(lead // 2, 16, 128).astype(BF16)


def unpairs(tiles, lead):
    return tiles.astype(F32).reshape(*lead, 8, 128)


def body(
    disp_h, force_h, stiff_h, wcell_h, wnorm_h, route_h, tu_h, tv_h, trow_h, tcol_h, trank_h,
    out_u, out_p, out_w,
    disp, force, stiff, wcell, wnorm, route, tu, tv, trow, tcol, trank,
    vol_s, vol_r, rep_s, rep_r, cor_s, cor_r, fvol_s, fvol_r, frep_s, frep_r,
    alone, f_own, c_own, ring_w, ring_once, ring_twice, ring_c, face_w, face_once, face_twice, face_c,
    corner_w, corner_once, corner_c, field, base, scale,
    vdt, ud, ol, rowhot, armask, place, sel_t, diag_m, row_m, sel_at, at_hot, za_hot,
    ra, g, zs, zr, ws, wr,
    load_sem, halo_ss, halo_rs, fhalo_ss, fhalo_rs, ph_ss, ph_rs,
):
    v = lax.axis_index("vol")
    r = lax.axis_index("rep")
    hi, lo = v // NLO, lax.rem(v, NLO)
    x, zh = hi // NZH, lax.rem(hi, NZH)
    y, c = lo // NC, lax.rem(lo, NC)

    def vol_of(x_, zh_, y_, c_):
        return ((x_ * NZH + zh_) * NY + y_) * NC + c_

    ring_x, ring_y = (2, 1, NX - 1), (4, 3, NY - 3, 2, NY - 2, 1, NY - 1)
    flip_peers = [(vol_of(lax.rem(x + j, NX), 1 - zh, y, c), r) for j in ring_x + (0,)]
    x_peers = [(vol_of(lax.rem(x + j, NX), zh, y, c), r) for j in ring_x]
    hi_peers = flip_peers + x_peers
    y_peers = [(vol_of(x, zh, lax.rem(y + j, NY), c), r) for j in ring_y]
    core_peer = (vol_of(x, zh, y, 1 - c), r)
    here = x * NLO + lo

    hops = {}
    for dx in range(NX):
        for dy in range(NY):
            for dc in range(NC):
                hops[dx, dy, dc] = 2 * (min(dx, NX - dx) + min(dy, NY - dy)) + dc
    plane_order = sorted(hops, key=lambda step: -hops[step])[:-1]
    at_x = [lax.rem(x + d, NX) for d in range(NX)]
    at_y = [lax.rem(y + d, NY) for d in range(NY)]
    at_c = [c, 1 - c]

    z_at = [(1 - zh, lax.rem(r + j, NR)) for j in (0, 1, 3)] + [(zh, lax.rem(r + j, NR)) for j in (3, 1, 2)] + [(1 - zh, lax.rem(r + 2, NR))]
    z_peers = [(vol_of(x, zh_, y, c), r_) for zh_, r_ in z_at]
    up_v, down_v = lax.rem(v + 1, NV), lax.rem(v + NV - 1, NV)
    up_r, down_r = lax.rem(r + 1, NR), lax.rem(r + NR - 1, NR)
    halo_peers = [(up_v, r), (down_v, r)] + [(a, b) for a in (up_v, down_v) for b in (up_r, down_r)]

    barrier = pltpu.get_barrier_semaphore()
    greeted = halo_peers + hi_peers + z_peers + y_peers + [core_peer]
    for peer in greeted:
        pl.semaphore_signal(barrier, inc=1, device_id=peer, device_id_type=MESH)

    sources = (disp_h, force_h, stiff_h, wcell_h, wnorm_h, route_h, trow_h, tcol_h, trank_h, tv_h, tu_h)
    targets = (disp, force, stiff, wcell, wnorm, route, trow, tcol, trank, tv, tu)
    loads = [pltpu.make_async_copy(a, b, load_sem.at[i]) for i, (a, b) in enumerate(zip(sources, targets))]
    for load in loads:
        load.start()
    for load in loads[:3]:
        load.wait()

    keep = 1.0 - relax_factor

    def rolled(w, shift, axis):
        shift = shift % (8 if axis == w.ndim - 2 else 128)
        if shift == 0:
            return w
        return pltpu.roll(w.reshape(-1, 8, 128), shift, axis - w.ndim + 3).reshape(w.shape)

    def sides(w, ring):
        row = iota(w.shape, w.ndim - 2)
        axis = w.ndim - 2
        before, after = rolled(ring, 1, axis), rolled(ring, 7, axis)
        return jnp.where(row == 0, before, rolled(w, 1, axis)) + jnp.where(row == 7, after, rolled(w, 7, axis))

    def from_ring(ring):
        row = iota(ring.shape, ring.ndim - 2)
        axis = ring.ndim - 2
        return jnp.where(row == 0, rolled(ring, 1, axis), jnp.where(row == 7, rolled(ring, 7, axis), 0.0))

    def to_ring(w):
        row = iota(w.shape, w.ndim - 2)
        axis = w.ndim - 2
        return jnp.where(row == 0, rolled(w, 1, axis), rolled(w, 7, axis))

    def along_z(w):
        lane = iota(w.shape, w.ndim - 1)
        axis = w.ndim - 1
        return jnp.where(lane == 0, 0.0, rolled(w, 1, axis)) + jnp.where(lane == 127, 0.0, rolled(w, 127, axis))

    row_c = iota((COMP, 8, 128), 1)
    own_inv = relax_factor / (mass_shift + 6.0 * stiff[...])
    own_c = own_inv * stiff[...]
    scale[...] = own_inv
    c_own[...] = own_c
    f_own[...] = force[...] * own_inv[None]
    for p in range(4):
        w = disp[:, p]
        total = sides(w, jnp.zeros_like(w)) + along_z(w)
        if p > 0:
            total = total + disp[:, p - 1]
        if p < 3:
            total = total + disp[:, p + 1]
        alone[:, p] = keep * w + f_own[:, p] + own_c[p][None] * total

    def row_of_planes(plane, row, start):
        out = None
        for p in range(4):
            moved = rolled(plane(p), start + p - row, 1)
            out = moved if out is None else jnp.where(iota(moved.shape, 1) == start + p, moved, out)
        return out

    for side in (0, 1):
        edge, second = (3, 2) if side == 0 else (0, 1)
        w_e, w_2, once = disp[:, edge], disp[:, second], alone[:, edge]
        c_e = own_c[edge]
        vol_s[side, 0:6] = pairs(w_e)
        vol_s[side, 6:12] = pairs(once)
        vol_s[side, 12:18] = pairs(f_own[:, edge] + c_e[None] * alone[:, second])
        vol_s[side, 18:19] = pairs(jnp.stack([c_e, c_e * own_c[second]]))
        up = jnp.where(row_c >= 6, w_e, jnp.where(row_c == 5, rolled(once, 6, 1), rolled(w_2, 5, 1)))
        down = jnp.where(row_c <= 1, w_e, jnp.where(row_c == 2, rolled(once, 2, 1), rolled(w_2, 3, 1)))
        half = row_c[0:6] >= 4
        cor_s[side, 0, 0:3] = pairs(jnp.where(half, up[6:12], rolled(up[0:6], 4, 1)))
        cor_s[side, 1, 0:3] = pairs(jnp.where(half, rolled(down[6:12], 4, 1), down[0:6]))
        for t in (0, 1):
            cor_s[side, t, 3:4] = pairs(jnp.stack([c_e, c_e]))
        row, inner = (7, 1) if side == 0 else (0, 7)
        first = row_of_planes(lambda p: disp[:, p], row, 0)
        then = row_of_planes(lambda p: alone[:, p], row, 4)
        rep_s[side, 0:6] = pairs(jnp.where(row_c < 4, first, then))
        last = [row_of_planes(lambda p: f_own[a:a + 6, p] + own_c[p][None] * rolled(alone[a:a + 6, p], inner, 1), row, start)
                for a, start in ((0, 0), (6, 4))]
        rep_s[side, 6:9] = pairs(jnp.where(half, last[1], last[0]))
        c_rows = row_of_planes(lambda p: own_c[p:p + 1], row, 0)
        cc_rows = row_of_planes(lambda p: own_c[p:p + 1] * rolled(own_c[p:p + 1], inner, 1), row, 4)
        c_rows = jnp.where(row_c[0:1] < 4, c_rows, cc_rows)
        rep_s[side, 9:10] = pairs(jnp.concatenate([c_rows, c_rows], axis=0))

    vol_to = [v < NV - 1, v > 0]
    vol_from = [v > 0, v < NV - 1]
    rep_to = [r < NR - 1, r > 0]
    rep_from = [r > 0, r < NR - 1]
    vol_dev, rep_dev = [up_v, down_v], [up_r, down_r]

    moves = []
    for s in (0, 1):
        moves.append((vol_s.at[s], vol_r.at[s], s, (vol_dev[s], r), vol_to[s], vol_from[s]))
    for s in (0, 1):
        for t in (0, 1):
            moves.append((cor_s.at[s, t], cor_r.at[s, t], 4 + 2 * s + t, (vol_dev[s], rep_dev[t]),
                          jnp.logical_and(vol_to[s], rep_to[t]), jnp.logical_and(vol_from[s], rep_from[t])))
    for t in (0, 1):
        moves.append((rep_s.at[t], rep_r.at[t], 2 + t, (v, rep_dev[t]), rep_to[t], rep_from[t]))

    def remote(src, dst, ss, rs, dev):
        return pltpu.make_async_remote_copy(src_ref=src, dst_ref=dst, send_sem=ss, recv_sem=rs, device_id=dev, device_id_type=MESH)

    for src, dst, at, dev, sends, comes in moves:
        @pl.when(jnp.logical_not(comes))
        def _():
            dst[...] = jnp.zeros(dst.shape, BF16)

    pl.semaphore_wait(barrier, len(greeted))

    for src, dst, at, dev, sends, comes in moves:
        @pl.when(sends)
        def _():
            remote(src, dst, halo_ss.at[at], halo_rs.at[at], dev).start()

    for load in loads[3:]:
        load.wait()
    route_row = route[...]
    route_sq = jnp.broadcast_to(route_row, (SLOTS, SLOTS))
    route_col = jnp.transpose(route_sq.astype(F32)).astype(I32)
    sub = iota((SLOTS, SLOTS), 0)
    lane = iota((SLOTS, SLOTS), 1)
    earlier = jnp.where(jnp.logical_and(route_col == route_sq, sub < lane), 1.0, 0.0)
    arrival = jnp.sum(earlier, axis=0, keepdims=True).astype(I32)
    place[...] = onehot(sub == route_sq)
    armask[...] = jnp.where(iota((8, SLOTS), 0) // 4 == jnp.broadcast_to(arrival, (8, SLOTS)), 1.0, 0.0)
    cell = wcell[...]
    z_one = onehot(sub == jnp.broadcast_to(lax.rem(cell, 128), (SLOTS, SLOTS)))
    ol[0:128] = z_one
    ol[128:256] = z_one
    rowhot[...] = jnp.where(iota((32, SLOTS), 0) == jnp.broadcast_to(cell // 128, (32, SLOTS)), 1.0, 0.0)
    owner_at = route_row // (NZH * NLO) * NLO + lax.rem(route_row, NLO)
    at_t = jnp.where(sub == jnp.broadcast_to(owner_at, (SLOTS, SLOTS)), 1.0, 0.0)
    at_hot[...] = jnp.transpose(at_t).astype(BF16)
    za = lax.rem(route_row // NLO, NZH) * 2 + arrival
    za_t = jnp.where(sub // 4 == jnp.broadcast_to(za, (SLOTS, SLOTS)), 1.0, 0.0)
    za_hot[...] = jnp.transpose(za_t)
    at_row = iota((NXY, NV), 0)
    sel_at[...] = onehot(iota((NXY, NV), 1) == at_row // NLO * (NZH * NLO) + zh * NLO + lax.rem(at_row, NLO))

    spread = onehot(iota((TILES, TQ), 1) // RANK == iota((TILES, TQ), 0))
    lists = jnp.concatenate([jnp.broadcast_to(trank[...], (4, TILES)), jnp.broadcast_to(trow[...], (4, TILES))], axis=0)
    over = dot(lists.astype(F32).astype(BF16), spread)
    rank_l, row_l = over[0:1], over[4:5]
    lane_q = lax.rem(iota((TILES, TQ), 1), RANK).astype(F32)
    diag_m[...] = jnp.where(lane_q < jnp.broadcast_to(rank_l, (TILES, TQ)), spread.astype(F32), 0.0)
    row_m[...] = jnp.where(iota((32, TQ), 0) // 8 == jnp.broadcast_to(row_l, (32, TQ)).astype(I32), 1.0, 0.0)
    col_t = jnp.where(iota((128, TILES), 0) == jnp.broadcast_to(tcol[...], (128, TILES)), 1.0, 0.0)
    col_t = jnp.concatenate([col_t, jnp.zeros((128, 96), F32)], axis=1)
    sel_t[...] = jnp.transpose(col_t)[0:TILES].astype(BF16)

    at_b, at_g = iota((256, 256), 0), iota((256, 256), 1)
    source = lax.rem(at_b, 8) * 32 + lax.rem(at_b // 16, 8) * 4 + at_b // 128 * 2 + lax.rem(at_b // 8, 2)
    perm_v = onehot(at_g == source)
    vdt[...] = dot_nt(perm_v, tv[...].reshape(TQ, 256)).astype(BF16)
    split = at_b == lax.rem(at_g, 128) * 2 + at_g // 128
    ud[...] = dot(tu[...].reshape(TQ, 256), onehot(split)).astype(BF16)

    for src, dst, at, dev, sends, comes in moves:
        @pl.when(comes)
        def _():
            remote(src, dst, halo_ss.at[at], halo_rs.at[at], dev).wait_recv()

    upper_half = row_c <= 3

    def ring_of(low, high, start):
        return [jnp.where(iota(low.shape, 1) <= 3, rolled(high, -start - p, 1), rolled(low, 7 - start - p, 1)) for p in range(4)]

    low_r, high_r = unpairs(rep_r[0, 0:6], (COMP,)), unpairs(rep_r[1, 0:6], (COMP,))
    for p, (w, once) in enumerate(zip(ring_of(low_r, high_r, 0), ring_of(low_r, high_r, 4))):
        ring_w[:, p] = w
        ring_once[:, p] = once
    low_r, high_r = unpairs(rep_r[0, 6:9], (6,)), unpairs(rep_r[1, 6:9], (6,))
    for p, (a, b) in enumerate(zip(ring_of(low_r, high_r, 0), ring_of(low_r, high_r, 4))):
        ring_twice[0:6, p] = a
        ring_twice[6:12, p] = b
    low_r, high_r = unpairs(rep_r[0, 9:10], (2,))[0:1], unpairs(rep_r[1, 9:10], (2,))[0:1]
    ring_cc = ring_of(low_r, high_r, 4)
    for p, part in enumerate(ring_of(low_r, high_r, 0)):
        ring_c[p:p + 1] = part
    for s in (0, 1):
        face_w[:, s] = unpairs(vol_r[s, 0:6], (COMP,))
        face_once[:, s] = unpairs(vol_r[s, 6:12], (COMP,))
        c_s = unpairs(vol_r[s, 18:19], (2,))
        face_c[s] = c_s[0]
        low_t, high_t = unpairs(cor_r[s, 0, 0:3], (6,)), unpairs(cor_r[s, 1, 0:3], (6,))
        low_c = jnp.concatenate([rolled(low_t, 4, 1), low_t], axis=0)
        high_c = jnp.concatenate([high_t, rolled(high_t, 4, 1)], axis=0)
        corner_w[:, s] = jnp.where(upper_half, high_c, low_c)
        corner_once[:, s] = jnp.where(upper_half, rolled(high_c, 6, 1), rolled(low_c, 2, 1))
        c_low, c_high = unpairs(cor_r[s, 0, 3:4], (2,)), unpairs(cor_r[s, 1, 3:4], (2,))
        corner_c[s] = jnp.where(upper_half[0], c_high[0], c_low[0])
        beside = jnp.where(row_c == 0, rolled(low_c, 4, 1), jnp.where(row_c == 7, rolled(high_c, 4, 1), 0.0))
        face_twice[:, s] = unpairs(vol_r[s, 12:18], (COMP,)) + c_s[1][None] * beside
        below = jnp.where(upper_half, rolled(high_c, 7, 1), rolled(low_c, 1, 1))
        ring_twice[:, 3 * s] = ring_twice[:, 3 * s] + ring_cc[3 * s] * below

    def sweeps(i, carry):
        own, ring = disp[i], ring_w[i]
        f, cc, c_r, c_f, c_x = f_own[i], c_own[...], ring_c[...], face_c[...], corner_c[...]
        face, corner = face_w[i], corner_w[i]

        def beside(w, ends):
            wide = jnp.concatenate([ends[0:1], w, ends[1:2]], axis=0)
            return wide[0:4] + wide[2:6]

        def ends_of(w):
            return jnp.concatenate([w[0:1], w[3:4]], axis=0)

        zero = jnp.zeros((2, 8, 128), F32)
        from_faces = jnp.concatenate([face[0:1], zero, face[1:2]], axis=0)
        from_corners = jnp.concatenate([corner[0:1], zero, corner[1:2]], axis=0)
        own_1 = alone[i] + cc * (from_faces + from_ring(ring))
        ring_1 = ring_once[i] + c_r * (to_ring(own) + from_corners)
        face_1 = face_once[i] + c_f * (ends_of(own) + from_ring(corner))
        corner_1 = corner_once[i] + c_x * (ends_of(ring) + to_ring(face))
        own_2 = keep * own_1 + f + cc * (beside(own_1, face_1) + sides(own_1, ring_1) + along_z(own_1))
        ring_2 = ring_twice[i] + keep * ring_1 + c_r * (to_ring(own_1) + beside(ring_1, corner_1) + along_z(ring_1))
        face_2 = face_twice[i] + keep * face_1 + c_f * (ends_of(own_1) + sides(face_1, corner_1) + along_z(face_1))
        field[i] = keep * own_2 + f + cc * (beside(own_2, face_2) + sides(own_2, ring_2) + along_z(own_2))
        return carry

    lax.fori_loop(0, COMP, sweeps, 0, unroll=12)

    flat = field[...].reshape(COMP * 32, 128)
    upper = flat.astype(BF16)
    lower = (flat - upper.astype(F32)).astype(BF16)
    picked = dot(jnp.concatenate([upper, lower], axis=1), ol[...]).reshape(COMP, 32, SLOTS)
    normal = wnorm[...]
    picked = jnp.sum(picked * rowhot[...][None], axis=1)
    traces = normal[0:1] * picked[0:4] + normal[1:2] * picked[4:8] + normal[2:3] * picked[8:12]
    traces = jnp.concatenate([traces, traces], axis=0) * armask[...]
    message = dot_nt(traces.astype(BF16), place[...])

    ra[hi] = message
    for peer in hi_peers:
        remote(ra.at[hi], ra.at[hi], ph_ss.at[0], ph_rs.at[0], peer).start()

    def wait_all(region, at, peer):
        remote(region, region, ph_ss.at[at], ph_rs.at[at], peer).wait_recv()

    wait_all(ra.at[pl.ds(0, NHI - 1)], 0, hi_peers[0])
    for k in range(4):
        g[c, y, k] = jnp.concatenate([ra[:, k], ra[:, 4 + k]], axis=0).astype(BF16)
    for peer in y_peers:
        remote(g.at[c, y], g.at[c, y], ph_ss.at[1], ph_rs.at[1], peer).start()
    row_f = iota((COMP, 8, 128), 1)
    fvol_s[0] = pairs(field[:, 3])
    fvol_s[1] = pairs(field[:, 0])
    for t in (0, 1):
        acc = jnp.zeros((COMP, 8, 128), F32)
        for p in range(4):
            shift = p + 1 if t == 0 else p
            acc = jnp.where(row_f == p, rolled(field[:, p], shift, 1), acc)
        frep_s[t] = pairs(acc)
    fmoves = []
    for s in (0, 1):
        fmoves.append((fvol_s.at[s], fvol_r.at[s], s, (vol_dev[s], r), vol_to[s], vol_from[s]))
        fmoves.append((frep_s.at[s], frep_r.at[s], 2 + s, (v, rep_dev[s]), rep_to[s], rep_from[s]))
    for src, dst, at, dev, sends, comes in fmoves:
        @pl.when(sends)
        def _():
            remote(src, dst, fhalo_ss.at[at], fhalo_rs.at[at], dev).start()

        @pl.when(jnp.logical_not(comes))
        def _():
            dst[...] = jnp.zeros(dst.shape, BF16)


    wait_all(g.at[c, pl.ds(0, NY - 1)], 1, y_peers[0])
    remote(g.at[c], g.at[c], ph_ss.at[2], ph_rs.at[2], core_peer).start()

    wait_all(g.at[c], 2, core_peer)

    pick = sel_t[...]
    chosen = jnp.concatenate([dot_nt(pick, g[:, :, k].reshape(256, 128)) for k in range(4)], axis=0).astype(BF16)
    every = dot(chosen, vdt[...])
    coef = jnp.sum(every.reshape(4, TILES, TQ) * diag_m[...][None], axis=1)
    coef = jnp.concatenate([coef, coef], axis=0)
    spread_c = (jnp.concatenate([coef] * 4, axis=0) * row_m[...]).astype(BF16)
    parts = dot(spread_c, ud[...])
    take = lax.rem(iota((32, 128), 0), 8) < 4
    parts = jnp.where(take, parts[:, 0:128], parts[:, 128:256])
    zs[...] = parts.reshape(4, 8, 128)

    mine_at = zh * NR + r
    for (zh_, r_), peer in zip(z_at, z_peers):
        remote(zs.at[r_], zr.at[mine_at], ph_ss.at[3], ph_rs.at[3], peer).start()
    zr[mine_at] = zs[r]

    wait_all(zr.at[pl.ds(0, 2 * NR - 1)], 3, z_peers[0])
    sums = jnp.sum(zr[...].reshape(NZH, NR, 8, 128), axis=1)
    back = jnp.concatenate([sums.reshape(16, 128), jnp.zeros((112, 128), F32)], axis=0).astype(BF16)
    ws[...] = dot_nt(sel_at[...], back).reshape(NXY, 1, 128)

    for dx, dy, dc in plane_order:
        at = at_x[dx] * NLO + at_y[dy] * NC + at_c[dc]
        remote(ws.at[at], wr.at[here], ph_ss.at[4], ph_rs.at[4], (vol_of(at_x[dx], zh, at_y[dy], at_c[dc]), r)).start()
    wr[here] = ws[here]
    own = jnp.where(zh == 0, sums[0], sums[1])
    wide = jnp.concatenate([own[0:4], own[4:8]], axis=1)
    join = jnp.where(at_g == lax.rem(at_b, 128) * 2 + at_b // 128, 1.0, 0.0)
    out_p[...] = jnp.dot(wide, join, precision=lax.Precision.HIGHEST, preferred_element_type=F32)

    for src, dst, at, dev, sends, comes in fmoves:
        @pl.when(comes)
        def _():
            remote(src, dst, fhalo_ss.at[at], fhalo_rs.at[at], dev).wait_recv()

    low_f, high_f = unpairs(fvol_r[0], (COMP,)), unpairs(fvol_r[1], (COMP,))
    low_y, high_y = unpairs(frep_r[0], (COMP,)), unpairs(frep_r[1], (COMP,))
    for p in range(4):
        w = field[:, p]
        total = (field[:, p - 1] if p > 0 else low_f) + (field[:, p + 1] if p < 3 else high_f)
        before = pltpu.roll(low_y, 8 - p, 1) if p > 0 else low_y
        after = pltpu.roll(high_y, 7 - p, 1)
        total = total + jnp.where(row_f == 0, before, pltpu.roll(w, 1, 1))
        total = total + jnp.where(row_f == 7, after, pltpu.roll(w, 7, 1))
        lane_f = iota((COMP, 8, 128), 2)
        total = total + jnp.where(lane_f == 0, 0.0, pltpu.roll(w, 1, 2))
        total = total + jnp.where(lane_f == 127, 0.0, pltpu.roll(w, 127, 2))
        base[:, p] = keep * w + f_own[:, p] + c_own[p][None] * total

    wait_all(wr.at[pl.ds(0, NXY - 1)], 4, core_peer)

    got = wr[...].reshape(NXY, 128).astype(BF16)
    got = jnp.concatenate([got, jnp.zeros((128 - NXY, 128), BF16)], axis=0)
    per_slot = (dot(at_hot[...], got) * za_hot[...]).astype(BF16)
    wave = onehot(lax.rem(iota((8, 128), 1), 4) == iota((8, 128), 0))
    wet = dot_nt(wave, per_slot)[0:4]
    out_w[...] = wet

    normal = -wnorm[...]
    load = jnp.concatenate([normal[i:i + 1] * wet for i in range(3)], axis=0)
    rows = (load[:, None, :] * rowhot[...][None]).reshape(COMP * 32, SLOTS)
    upper = rows.astype(BF16)
    lower = (rows - upper.astype(F32)).astype(BF16)
    z_one = ol[0:128]
    placed = dot_nt(jnp.concatenate([upper, lower], axis=1), jnp.concatenate([z_one, z_one], axis=1))
    out_u[...] = base[...] + scale[...][None] * placed.reshape(COMP, 4, 8, 128)

    for src, dst, at, dev, sends, comes in moves:
        @pl.when(sends)
        def _():
            remote(src, dst, halo_ss.at[at], halo_rs.at[at], dev).wait_send()
    for src, dst, at, dev, sends, comes in fmoves:
        @pl.when(sends)
        def _():
            remote(src, dst, fhalo_ss.at[at], fhalo_rs.at[at], dev).wait_send()

    def sent(region, at, peer):
        remote(region, region, ph_ss.at[at], ph_rs.at[at], peer).wait_send()

    sent(ra.at[pl.ds(0, NHI - 1)], 0, hi_peers[0])
    sent(g.at[c, pl.ds(0, NY - 1)], 1, y_peers[0])
    sent(g.at[c], 2, core_peer)
    sent(zr.at[pl.ds(0, 2 * NR - 1)], 3, z_peers[0])
    sent(wr.at[pl.ds(0, NXY - 1)], 4, core_peer)


def hand_out(u, p, w, out_u, out_p, out_w):
    out_u[...] = u[...]
    out_p[...] = p[...]
    out_w[...] = w[...]


def shards(displacement, body_force, stiffness, wet_cell, wet_normal, route, tile_u, tile_v, tile_row, tile_col, tile_rank):
    vmem = pl.BlockSpec(memory_space=pltpu.VMEM)
    hbm = pl.BlockSpec(memory_space=pltpu.HBM)
    V = pltpu.VMEM
    updated, pressure, wet = pl.pallas_call(
        body,
        out_shape=(
            jax.ShapeDtypeStruct((COMP, 4, 8, 128), F32),
            jax.ShapeDtypeStruct((4, 256), F32),
            jax.ShapeDtypeStruct((4, SLOTS), F32),
        ),
        in_specs=[hbm] * 11,
        out_specs=(vmem, vmem, vmem),
        scratch_shapes=[
            V((COMP, 4, 8, 128), F32), V((COMP, 4, 8, 128), F32), V((4, 8, 128), F32),
            V((1, SLOTS), I32), V((3, SLOTS), F32), V((1, SLOTS), I32),
            V((TILES, RANK, 256), BF16), V((TILES, RANK, 256), BF16),
            V((1, TILES), I32), V((1, TILES), I32), V((1, TILES), I32),
            V((2, 19, 16, 128), BF16), V((2, 19, 16, 128), BF16),
            V((2, 10, 16, 128), BF16), V((2, 10, 16, 128), BF16),
            V((2, 2, 4, 16, 128), BF16), V((2, 2, 4, 16, 128), BF16),
            V((2, 6, 16, 128), BF16), V((2, 6, 16, 128), BF16),
            V((2, 6, 16, 128), BF16), V((2, 6, 16, 128), BF16),
            V((COMP, 4, 8, 128), F32), V((COMP, 4, 8, 128), F32), V((4, 8, 128), F32),
            V((COMP, 4, 8, 128), F32), V((COMP, 4, 8, 128), F32), V((COMP, 4, 8, 128), F32), V((4, 8, 128), F32),
            V((COMP, 2, 8, 128), F32), V((COMP, 2, 8, 128), F32), V((COMP, 2, 8, 128), F32), V((2, 8, 128), F32),
            V((COMP, 2, 8, 128), F32), V((COMP, 2, 8, 128), F32), V((2, 8, 128), F32),
            V((COMP, 4, 8, 128), F32), V((COMP, 4, 8, 128), F32), V((4, 8, 128), F32),
            V((256, TQ), BF16), V((TQ, 256), BF16), V((256, SLOTS), BF16), V((32, SLOTS), F32),
            V((8, SLOTS), F32), V((128, SLOTS), BF16), V((TILES, 128), BF16), V((TILES, TQ), F32),
            V((32, TQ), F32), V((NXY, NV), BF16), V((SLOTS, 128), BF16), V((SLOTS, 128), F32),
            V((NHI, 8, 128), F32), V((NC, NY, 4, 16, 128), BF16),
            V((NR, 8, 128), F32), V((NZH * NR, 8, 128), F32),
            V((NXY, 1, 128), F32), V((NXY, 1, 128), F32),
            pltpu.SemaphoreType.DMA((11,)),
            pltpu.SemaphoreType.DMA((8,)), pltpu.SemaphoreType.DMA((8,)),
            pltpu.SemaphoreType.DMA((4,)), pltpu.SemaphoreType.DMA((4,)),
            pltpu.SemaphoreType.DMA((5,)), pltpu.SemaphoreType.DMA((5,)),
        ],
        compiler_params=pltpu.CompilerParams(collective_id=0, has_side_effects=True, vmem_limit_bytes=56 << 20),
    )(
        displacement.reshape(COMP, 4, 8, 128),
        body_force.reshape(COMP, 4, 8, 128),
        stiffness,
        wet_cell,
        wet_normal,
        route.reshape(1, SLOTS),
        tile_u,
        tile_v,
        tile_row.reshape(1, TILES),
        tile_col.reshape(1, TILES),
        tile_rank.reshape(1, TILES),
    )
    updated, pressure, wet = pl.pallas_call(
        hand_out,
        out_shape=(
            jax.ShapeDtypeStruct((COMP, 4, 8, 128), F32),
            jax.ShapeDtypeStruct((4, 256), F32),
            jax.ShapeDtypeStruct((4, SLOTS), F32),
        ),
        in_specs=[vmem] * 3,
        out_specs=(vmem, vmem, vmem),
        compiler_params=pltpu.CompilerParams(vmem_limit_bytes=56 << 20),
    )(updated, pressure, wet)
    return updated.reshape(displacement.shape), pressure, wet


def solution(mesh):
    return jax.shard_map(
        shards,
        mesh=mesh,
        in_specs=(
            P(None, None, "vol", "rep", None),
            P(None, None, "vol", "rep", None),
            P("vol", "rep", None),
            P(("vol", "rep"), None),
            P(None, ("vol", "rep")),
            P(("vol", "rep"), None),
            P(("vol", "rep"), None, None),
            P(("vol", "rep"), None, None),
            P(("vol", "rep")),
            P(("vol", "rep")),
            P(("vol", "rep")),
        ),
        out_specs=(
            P(None, None, "vol", "rep", None),
            P(None, ("vol", "rep")),
            P(None, ("vol", "rep")),
        ),
        check_vma=False,
    )
```

```python
import jax
import jax.numpy as jnp
from jax import lax
from jax.experimental import pallas as pl
from jax.experimental.pallas import tpu as pltpu
from jax.sharding import PartitionSpec as P

MESH = pl.DeviceIdType.MESH
relax_factor = 0.8
mass_shift = 1.0

F32 = jnp.float32
BF16 = jnp.bfloat16
I32 = jnp.int32

NX, NZH, NY, NC = 4, 2, 8, 2
NR = 4
NHI = NX * NZH
NLO = NY * NC
NV = NHI * NLO
NXY = NX * NLO
SLOTS = 128
COMP = 12
TILES, RANK = 32, 32
TQ = TILES * RANK

NT = (((1,), (1,)), ((), ()))


def dot(a, b):
    return jnp.dot(a, b, preferred_element_type=F32)


def dot_nt(a, b):
    return lax.dot_general(a, b, NT, preferred_element_type=F32)


def iota(shape, dim):
    return lax.broadcasted_iota(I32, shape, dim)


def onehot(condition, dtype=BF16):
    return jnp.where(condition, 1.0, 0.0).astype(F32).astype(dtype)


def pairs(tiles):
    lead = 1
    for size in tiles.shape[:-2]:
        lead *= size
    return tiles.reshape(lead // 2, 16, 128).astype(BF16)


def unpairs(tiles, lead):
    return tiles.astype(F32).reshape(*lead, 8, 128)


def body(
    disp_h, force_h, stiff_h, wcell_h, wnorm_h, route_h, tu_h, tv_h, trow_h, tcol_h, trank_h,
    out_u, out_p, out_w,
    disp, force, stiff, wcell, wnorm, route, tu, tv, trow, tcol, trank,
    vol_s, vol_r, rep_s, rep_r, cor_s, cor_r, fvol_s, fvol_r, frep_s, frep_r,
    alone, f_own, c_own, ring_w, ring_once, ring_twice, ring_c, face_w, face_once, face_twice, face_c,
    corner_w, corner_once, corner_c, field, base, scale,
    vdt, ud, ol, rowhot, armask, place, sel_t, diag_m, row_m, sel_at, at_hot, za_hot,
    ra, g, zs, zr, ws, wr,
    load_sem, halo_ss, halo_rs, fhalo_ss, fhalo_rs, ph_ss, ph_rs,
):
    v = lax.axis_index("vol")
    r = lax.axis_index("rep")
    hi, lo = v // NLO, lax.rem(v, NLO)
    x, zh = hi // NZH, lax.rem(hi, NZH)
    y, c = lo // NC, lax.rem(lo, NC)

    def vol_of(x_, zh_, y_, c_):
        return ((x_ * NZH + zh_) * NY + y_) * NC + c_

    ring_x, ring_y = (2, 1, NX - 1), (4, 3, NY - 3, 2, NY - 2, 1, NY - 1)
    flip_peers = [(vol_of(lax.rem(x + j, NX), 1 - zh, y, c), r) for j in ring_x + (0,)]
    x_peers = [(vol_of(lax.rem(x + j, NX), zh, y, c), r) for j in ring_x]
    hi_peers = flip_peers + x_peers
    y_peers = [(vol_of(x, zh, lax.rem(y + j, NY), c), r) for j in ring_y]
    core_peer = (vol_of(x, zh, y, 1 - c), r)
    here = x * NLO + lo

    hops = {}
    for dx in range(NX):
        for dy in range(NY):
            for dc in range(NC):
                hops[dx, dy, dc] = 2 * (min(dx, NX - dx) + min(dy, NY - dy)) + dc
    plane_order = sorted(hops, key=lambda step: -hops[step])[:-1]
    at_x = [lax.rem(x + d, NX) for d in range(NX)]
    at_y = [lax.rem(y + d, NY) for d in range(NY)]
    at_c = [c, 1 - c]

    z_at = [(1 - zh, lax.rem(r + j, NR)) for j in (0, 1, 3)] + [(zh, lax.rem(r + j, NR)) for j in (3, 1, 2)] + [(1 - zh, lax.rem(r + 2, NR))]
    z_peers = [(vol_of(x, zh_, y, c), r_) for zh_, r_ in z_at]
    up_v, down_v = lax.rem(v + 1, NV), lax.rem(v + NV - 1, NV)
    up_r, down_r = lax.rem(r + 1, NR), lax.rem(r + NR - 1, NR)
    halo_peers = [(up_v, r), (down_v, r)] + [(a, b) for a in (up_v, down_v) for b in (up_r, down_r)]

    barrier = pltpu.get_barrier_semaphore()
    greeted = halo_peers + hi_peers + z_peers + y_peers + [core_peer]
    for peer in greeted:
        pl.semaphore_signal(barrier, inc=1, device_id=peer, device_id_type=MESH)

    sources = (disp_h, force_h, stiff_h, wcell_h, wnorm_h, route_h, trow_h, tcol_h, trank_h, tv_h, tu_h)
    targets = (disp, force, stiff, wcell, wnorm, route, trow, tcol, trank, tv, tu)
    loads = [pltpu.make_async_copy(a, b, load_sem.at[i]) for i, (a, b) in enumerate(zip(sources, targets))]
    for load in loads:
        load.start()
    for load in loads[:3]:
        load.wait()

    keep = 1.0 - relax_factor

    def rolled(w, shift, axis):
        shift = shift % (8 if axis == w.ndim - 2 else 128)
        if shift == 0:
            return w
        return pltpu.roll(w.reshape(-1, 8, 128), shift, axis - w.ndim + 3).reshape(w.shape)

    def sides(w, ring):
        row = iota(w.shape, w.ndim - 2)
        axis = w.ndim - 2
        before, after = rolled(ring, 1, axis), rolled(ring, 7, axis)
        return jnp.where(row == 0, before, rolled(w, 1, axis)) + jnp.where(row == 7, after, rolled(w, 7, axis))

    def from_ring(ring):
        row = iota(ring.shape, ring.ndim - 2)
        axis = ring.ndim - 2
        return jnp.where(row == 0, rolled(ring, 1, axis), jnp.where(row == 7, rolled(ring, 7, axis), 0.0))

    def to_ring(w):
        row = iota(w.shape, w.ndim - 2)
        axis = w.ndim - 2
        return jnp.where(row == 0, rolled(w, 1, axis), rolled(w, 7, axis))

    def along_z(w):
        lane = iota(w.shape, w.ndim - 1)
        axis = w.ndim - 1
        return jnp.where(lane == 0, 0.0, rolled(w, 1, axis)) + jnp.where(lane == 127, 0.0, rolled(w, 127, axis))

    row_c = iota((COMP, 8, 128), 1)
    own_inv = relax_factor / (mass_shift + 6.0 * stiff[...])
    own_c = own_inv * stiff[...]
    scale[...] = own_inv
    c_own[...] = own_c
    f_own[...] = force[...] * own_inv[None]
    for p in range(4):
        w = disp[:, p]
        total = sides(w, jnp.zeros_like(w)) + along_z(w)
        if p > 0:
            total = total + disp[:, p - 1]
        if p < 3:
            total = total + disp[:, p + 1]
        alone[:, p] = keep * w + f_own[:, p] + own_c[p][None] * total

    def row_of_planes(plane, row, start):
        out = None
        for p in range(4):
            moved = rolled(plane(p), start + p - row, 1)
            out = moved if out is None else jnp.where(iota(moved.shape, 1) == start + p, moved, out)
        return out

    for side in (0, 1):
        edge, second = (3, 2) if side == 0 else (0, 1)
        w_e, w_2, once = disp[:, edge], disp[:, second], alone[:, edge]
        c_e = own_c[edge]
        vol_s[side, 0:6] = pairs(w_e)
        vol_s[side, 6:12] = pairs(once)
        vol_s[side, 12:18] = pairs(f_own[:, edge] + c_e[None] * alone[:, second])
        vol_s[side, 18:19] = pairs(jnp.stack([c_e, c_e * own_c[second]]))
        up = jnp.where(row_c >= 6, w_e, jnp.where(row_c == 5, rolled(once, 6, 1), rolled(w_2, 5, 1)))
        down = jnp.where(row_c <= 1, w_e, jnp.where(row_c == 2, rolled(once, 2, 1), rolled(w_2, 3, 1)))
        half = row_c[0:6] >= 4
        cor_s[side, 0, 0:3] = pairs(jnp.where(half, up[6:12], rolled(up[0:6], 4, 1)))
        cor_s[side, 1, 0:3] = pairs(jnp.where(half, rolled(down[6:12], 4, 1), down[0:6]))
        for t in (0, 1):
            cor_s[side, t, 3:4] = pairs(jnp.stack([c_e, c_e]))
        row, inner = (7, 1) if side == 0 else (0, 7)
        first = row_of_planes(lambda p: disp[:, p], row, 0)
        then = row_of_planes(lambda p: alone[:, p], row, 4)
        rep_s[side, 0:6] = pairs(jnp.where(row_c < 4, first, then))
        last = [row_of_planes(lambda p: f_own[a:a + 6, p] + own_c[p][None] * rolled(alone[a:a + 6, p], inner, 1), row, start)
                for a, start in ((0, 0), (6, 4))]
        rep_s[side, 6:9] = pairs(jnp.where(half, last[1], last[0]))
        c_rows = row_of_planes(lambda p: own_c[p:p + 1], row, 0)
        cc_rows = row_of_planes(lambda p: own_c[p:p + 1] * rolled(own_c[p:p + 1], inner, 1), row, 4)
        c_rows = jnp.where(row_c[0:1] < 4, c_rows, cc_rows)
        rep_s[side, 9:10] = pairs(jnp.concatenate([c_rows, c_rows], axis=0))

    vol_to = [v < NV - 1, v > 0]
    vol_from = [v > 0, v < NV - 1]
    rep_to = [r < NR - 1, r > 0]
    rep_from = [r > 0, r < NR - 1]
    vol_dev, rep_dev = [up_v, down_v], [up_r, down_r]

    moves = []
    for s in (0, 1):
        moves.append((vol_s.at[s], vol_r.at[s], s, (vol_dev[s], r), vol_to[s], vol_from[s]))
    for s in (0, 1):
        for t in (0, 1):
            moves.append((cor_s.at[s, t], cor_r.at[s, t], 4 + 2 * s + t, (vol_dev[s], rep_dev[t]),
                          jnp.logical_and(vol_to[s], rep_to[t]), jnp.logical_and(vol_from[s], rep_from[t])))
    for t in (0, 1):
        moves.append((rep_s.at[t], rep_r.at[t], 2 + t, (v, rep_dev[t]), rep_to[t], rep_from[t]))

    def remote(src, dst, ss, rs, dev):
        return pltpu.make_async_remote_copy(src_ref=src, dst_ref=dst, send_sem=ss, recv_sem=rs, device_id=dev, device_id_type=MESH)

    for src, dst, at, dev, sends, comes in moves:
        @pl.when(jnp.logical_not(comes))
        def _():
            dst[...] = jnp.zeros(dst.shape, BF16)

    pl.semaphore_wait(barrier, len(greeted))

    for src, dst, at, dev, sends, comes in moves:
        @pl.when(sends)
        def _():
            remote(src, dst, halo_ss.at[at], halo_rs.at[at], dev).start()

    for load in loads[3:]:
        load.wait()
    route_row = route[...]
    route_sq = jnp.broadcast_to(route_row, (SLOTS, SLOTS))
    route_col = jnp.transpose(route_sq.astype(F32)).astype(I32)
    sub = iota((SLOTS, SLOTS), 0)
    lane = iota((SLOTS, SLOTS), 1)
    earlier = jnp.where(jnp.logical_and(route_col == route_sq, sub < lane), 1.0, 0.0)
    arrival = jnp.sum(earlier, axis=0, keepdims=True).astype(I32)
    place[...] = onehot(sub == route_sq)
    armask[...] = jnp.where(iota((8, SLOTS), 0) // 4 == jnp.broadcast_to(arrival, (8, SLOTS)), 1.0, 0.0)
    cell = wcell[...]
    z_one = onehot(sub == jnp.broadcast_to(lax.rem(cell, 128), (SLOTS, SLOTS)))
    ol[0:128] = z_one
    ol[128:256] = z_one
    rowhot[...] = jnp.where(iota((32, SLOTS), 0) == jnp.broadcast_to(cell // 128, (32, SLOTS)), 1.0, 0.0)
    owner_at = route_row // (NZH * NLO) * NLO + lax.rem(route_row, NLO)
    at_t = jnp.where(sub == jnp.broadcast_to(owner_at, (SLOTS, SLOTS)), 1.0, 0.0)
    at_hot[...] = jnp.transpose(at_t).astype(BF16)
    za = lax.rem(route_row // NLO, NZH) * 2 + arrival
    za_t = jnp.where(sub // 4 == jnp.broadcast_to(za, (SLOTS, SLOTS)), 1.0, 0.0)
    za_hot[...] = jnp.transpose(za_t)
    at_row = iota((NXY, NV), 0)
    sel_at[...] = onehot(iota((NXY, NV), 1) == at_row // NLO * (NZH * NLO) + zh * NLO + lax.rem(at_row, NLO))

    spread = onehot(iota((TILES, TQ), 1) // RANK == iota((TILES, TQ), 0))
    lists = jnp.concatenate([jnp.broadcast_to(trank[...], (4, TILES)), jnp.broadcast_to(trow[...], (4, TILES))], axis=0)
    over = dot(lists.astype(F32).astype(BF16), spread)
    rank_l, row_l = over[0:1], over[4:5]
    lane_q = lax.rem(iota((TILES, TQ), 1), RANK).astype(F32)
    diag_m[...] = jnp.where(lane_q < jnp.broadcast_to(rank_l, (TILES, TQ)), spread.astype(F32), 0.0)
    row_m[...] = jnp.where(iota((32, TQ), 0) // 8 == jnp.broadcast_to(row_l, (32, TQ)).astype(I32), 1.0, 0.0)
    col_t = jnp.where(iota((128, TILES), 0) == jnp.broadcast_to(tcol[...], (128, TILES)), 1.0, 0.0)
    col_t = jnp.concatenate([col_t, jnp.zeros((128, 96), F32)], axis=1)
    sel_t[...] = jnp.transpose(col_t)[0:TILES].astype(BF16)

    at_b, at_g = iota((256, 256), 0), iota((256, 256), 1)
    source = lax.rem(at_b, 8) * 32 + lax.rem(at_b // 16, 8) * 4 + at_b // 128 * 2 + lax.rem(at_b // 8, 2)
    perm_v = onehot(at_g == source)
    vdt[...] = dot_nt(perm_v, tv[...].reshape(TQ, 256)).astype(BF16)
    split = at_b == lax.rem(at_g, 128) * 2 + at_g // 128
    ud[...] = dot(tu[...].reshape(TQ, 256), onehot(split)).astype(BF16)

    for src, dst, at, dev, sends, comes in moves:
        @pl.when(comes)
        def _():
            remote(src, dst, halo_ss.at[at], halo_rs.at[at], dev).wait_recv()

    upper_half = row_c <= 3

    def ring_of(low, high, start):
        return [jnp.where(iota(low.shape, 1) <= 3, rolled(high, -start - p, 1), rolled(low, 7 - start - p, 1)) for p in range(4)]

    low_r, high_r = unpairs(rep_r[0, 0:6], (COMP,)), unpairs(rep_r[1, 0:6], (COMP,))
    for p, (w, once) in enumerate(zip(ring_of(low_r, high_r, 0), ring_of(low_r, high_r, 4))):
        ring_w[:, p] = w
        ring_once[:, p] = once
    low_r, high_r = unpairs(rep_r[0, 6:9], (6,)), unpairs(rep_r[1, 6:9], (6,))
    for p, (a, b) in enumerate(zip(ring_of(low_r, high_r, 0), ring_of(low_r, high_r, 4))):
        ring_twice[0:6, p] = a
        ring_twice[6:12, p] = b
    low_r, high_r = unpairs(rep_r[0, 9:10], (2,))[0:1], unpairs(rep_r[1, 9:10], (2,))[0:1]
    ring_cc = ring_of(low_r, high_r, 4)
    for p, part in enumerate(ring_of(low_r, high_r, 0)):
        ring_c[p:p + 1] = part
    for s in (0, 1):
        face_w[:, s] = unpairs(vol_r[s, 0:6], (COMP,))
        face_once[:, s] = unpairs(vol_r[s, 6:12], (COMP,))
        c_s = unpairs(vol_r[s, 18:19], (2,))
        face_c[s] = c_s[0]
        low_t, high_t = unpairs(cor_r[s, 0, 0:3], (6,)), unpairs(cor_r[s, 1, 0:3], (6,))
        low_c = jnp.concatenate([rolled(low_t, 4, 1), low_t], axis=0)
        high_c = jnp.concatenate([high_t, rolled(high_t, 4, 1)], axis=0)
        corner_w[:, s] = jnp.where(upper_half, high_c, low_c)
        corner_once[:, s] = jnp.where(upper_half, rolled(high_c, 6, 1), rolled(low_c, 2, 1))
        c_low, c_high = unpairs(cor_r[s, 0, 3:4], (2,)), unpairs(cor_r[s, 1, 3:4], (2,))
        corner_c[s] = jnp.where(upper_half[0], c_high[0], c_low[0])
        beside = jnp.where(row_c == 0, rolled(low_c, 4, 1), jnp.where(row_c == 7, rolled(high_c, 4, 1), 0.0))
        face_twice[:, s] = unpairs(vol_r[s, 12:18], (COMP,)) + c_s[1][None] * beside
        below = jnp.where(upper_half, rolled(high_c, 7, 1), rolled(low_c, 1, 1))
        ring_twice[:, 3 * s] = ring_twice[:, 3 * s] + ring_cc[3 * s] * below

    def sweeps(i, carry):
        own, ring = disp[i], ring_w[i]
        f, cc, c_r, c_f, c_x = f_own[i], c_own[...], ring_c[...], face_c[...], corner_c[...]
        face, corner = face_w[i], corner_w[i]

        def beside(w, ends):
            wide = jnp.concatenate([ends[0:1], w, ends[1:2]], axis=0)
            return wide[0:4] + wide[2:6]

        def ends_of(w):
            return jnp.concatenate([w[0:1], w[3:4]], axis=0)

        zero = jnp.zeros((2, 8, 128), F32)
        from_faces = jnp.concatenate([face[0:1], zero, face[1:2]], axis=0)
        from_corners = jnp.concatenate([corner[0:1], zero, corner[1:2]], axis=0)
        own_1 = alone[i] + cc * (from_faces + from_ring(ring))
        ring_1 = ring_once[i] + c_r * (to_ring(own) + from_corners)
        face_1 = face_once[i] + c_f * (ends_of(own) + from_ring(corner))
        corner_1 = corner_once[i] + c_x * (ends_of(ring) + to_ring(face))
        own_2 = keep * own_1 + f + cc * (beside(own_1, face_1) + sides(own_1, ring_1) + along_z(own_1))
        ring_2 = ring_twice[i] + keep * ring_1 + c_r * (to_ring(own_1) + beside(ring_1, corner_1) + along_z(ring_1))
        face_2 = face_twice[i] + keep * face_1 + c_f * (ends_of(own_1) + sides(face_1, corner_1) + along_z(face_1))
        field[i] = keep * own_2 + f + cc * (beside(own_2, face_2) + sides(own_2, ring_2) + along_z(own_2))
        return carry

    lax.fori_loop(0, COMP, sweeps, 0, unroll=12)

    flat = field[...].reshape(COMP * 32, 128)
    upper = flat.astype(BF16)
    lower = (flat - upper.astype(F32)).astype(BF16)
    picked = dot(jnp.concatenate([upper, lower], axis=1), ol[...]).reshape(COMP, 32, SLOTS)
    normal = wnorm[...]
    picked = jnp.sum(picked * rowhot[...][None], axis=1)
    traces = normal[0:1] * picked[0:4] + normal[1:2] * picked[4:8] + normal[2:3] * picked[8:12]
    traces = jnp.concatenate([traces, traces], axis=0) * armask[...]
    message = dot_nt(traces.astype(BF16), place[...])

    ra[hi] = message
    for peer in hi_peers:
        remote(ra.at[hi], ra.at[hi], ph_ss.at[0], ph_rs.at[0], peer).start()

    def wait_all(region, at, peer):
        remote(region, region, ph_ss.at[at], ph_rs.at[at], peer).wait_recv()

    wait_all(ra.at[pl.ds(0, NHI - 1)], 0, hi_peers[0])
    for k in range(4):
        g[c, y, k] = jnp.concatenate([ra[:, k], ra[:, 4 + k]], axis=0).astype(BF16)
    for peer in y_peers:
        remote(g.at[c, y], g.at[c, y], ph_ss.at[1], ph_rs.at[1], peer).start()
    row_f = iota((COMP, 8, 128), 1)
    fvol_s[0] = pairs(field[:, 3])
    fvol_s[1] = pairs(field[:, 0])
    for t in (0, 1):
        acc = jnp.zeros((COMP, 8, 128), F32)
        for p in range(4):
            shift = p + 1 if t == 0 else p
            acc = jnp.where(row_f == p, rolled(field[:, p], shift, 1), acc)
        frep_s[t] = pairs(acc)
    fmoves = []
    for s in (0, 1):
        fmoves.append((fvol_s.at[s], fvol_r.at[s], s, (vol_dev[s], r), vol_to[s], vol_from[s]))
        fmoves.append((frep_s.at[s], frep_r.at[s], 2 + s, (v, rep_dev[s]), rep_to[s], rep_from[s]))
    for src, dst, at, dev, sends, comes in fmoves:
        @pl.when(sends)
        def _():
            remote(src, dst, fhalo_ss.at[at], fhalo_rs.at[at], dev).start()

        @pl.when(jnp.logical_not(comes))
        def _():
            dst[...] = jnp.zeros(dst.shape, BF16)


    wait_all(g.at[c, pl.ds(0, NY - 1)], 1, y_peers[0])
    remote(g.at[c], g.at[c], ph_ss.at[2], ph_rs.at[2], core_peer).start()

    wait_all(g.at[c], 2, core_peer)

    pick = sel_t[...]
    chosen = jnp.concatenate([dot_nt(pick, g[:, :, k].reshape(256, 128)) for k in range(4)], axis=0).astype(BF16)
    every = dot(chosen, vdt[...])
    coef = jnp.sum(every.reshape(4, TILES, TQ) * diag_m[...][None], axis=1)
    coef = jnp.concatenate([coef, coef], axis=0)
    spread_c = (jnp.concatenate([coef] * 4, axis=0) * row_m[...]).astype(BF16)
    parts = dot(spread_c, ud[...])
    take = lax.rem(iota((32, 128), 0), 8) < 4
    parts = jnp.where(take, parts[:, 0:128], parts[:, 128:256])
    zs[...] = parts.reshape(4, 8, 128)

    mine_at = zh * NR + r
    for (zh_, r_), peer in zip(z_at, z_peers):
        remote(zs.at[r_], zr.at[mine_at], ph_ss.at[3], ph_rs.at[3], peer).start()
    zr[mine_at] = zs[r]

    wait_all(zr.at[pl.ds(0, 2 * NR - 1)], 3, z_peers[0])
    sums = jnp.sum(zr[...].reshape(NZH, NR, 8, 128), axis=1)
    back = jnp.concatenate([sums.reshape(16, 128), jnp.zeros((112, 128), F32)], axis=0).astype(BF16)
    ws[...] = dot_nt(sel_at[...], back).reshape(NXY, 1, 128)

    for dx, dy, dc in plane_order:
        at = at_x[dx] * NLO + at_y[dy] * NC + at_c[dc]
        remote(ws.at[at], wr.at[here], ph_ss.at[4], ph_rs.at[4], (vol_of(at_x[dx], zh, at_y[dy], at_c[dc]), r)).start()
    wr[here] = ws[here]
    own = jnp.where(zh == 0, sums[0], sums[1])
    wide = jnp.concatenate([own[0:4], own[4:8]], axis=1)
    join = jnp.where(at_g == lax.rem(at_b, 128) * 2 + at_b // 128, 1.0, 0.0)
    out_p[...] = jnp.dot(wide, join, precision=lax.Precision.HIGHEST, preferred_element_type=F32)

    for src, dst, at, dev, sends, comes in fmoves:
        @pl.when(comes)
        def _():
            remote(src, dst, fhalo_ss.at[at], fhalo_rs.at[at], dev).wait_recv()

    low_f, high_f = unpairs(fvol_r[0], (COMP,)), unpairs(fvol_r[1], (COMP,))
    low_y, high_y = unpairs(frep_r[0], (COMP,)), unpairs(frep_r[1], (COMP,))
    for p in range(4):
        w = field[:, p]
        total = (field[:, p - 1] if p > 0 else low_f) + (field[:, p + 1] if p < 3 else high_f)
        before = pltpu.roll(low_y, 8 - p, 1) if p > 0 else low_y
        after = pltpu.roll(high_y, 7 - p, 1)
        total = total + jnp.where(row_f == 0, before, pltpu.roll(w, 1, 1))
        total = total + jnp.where(row_f == 7, after, pltpu.roll(w, 7, 1))
        lane_f = iota((COMP, 8, 128), 2)
        total = total + jnp.where(lane_f == 0, 0.0, pltpu.roll(w, 1, 2))
        total = total + jnp.where(lane_f == 127, 0.0, pltpu.roll(w, 127, 2))
        base[:, p] = keep * w + f_own[:, p] + c_own[p][None] * total

    wait_all(wr.at[pl.ds(0, NXY - 1)], 4, core_peer)

    got = wr[...].reshape(NXY, 128).astype(BF16)
    got = jnp.concatenate([got, jnp.zeros((128 - NXY, 128), BF16)], axis=0)
    per_slot = (dot(at_hot[...], got) * za_hot[...]).astype(BF16)
    wave = onehot(lax.rem(iota((8, 128), 1), 4) == iota((8, 128), 0))
    wet = dot_nt(wave, per_slot)[0:4]
    out_w[...] = wet

    normal = -wnorm[...]
    load = jnp.concatenate([normal[i:i + 1] * wet for i in range(3)], axis=0)
    rows = (load[:, None, :] * rowhot[...][None]).reshape(COMP * 32, SLOTS)
    upper = rows.astype(BF16)
    lower = (rows - upper.astype(F32)).astype(BF16)
    z_one = ol[0:128]
    placed = dot_nt(jnp.concatenate([upper, lower], axis=1), jnp.concatenate([z_one, z_one], axis=1))
    out_u[...] = base[...] + scale[...][None] * placed.reshape(COMP, 4, 8, 128)

    for src, dst, at, dev, sends, comes in moves:
        @pl.when(sends)
        def _():
            remote(src, dst, halo_ss.at[at], halo_rs.at[at], dev).wait_send()
    for src, dst, at, dev, sends, comes in fmoves:
        @pl.when(sends)
        def _():
            remote(src, dst, fhalo_ss.at[at], fhalo_rs.at[at], dev).wait_send()

    def sent(region, at, peer):
        remote(region, region, ph_ss.at[at], ph_rs.at[at], peer).wait_send()

    sent(ra.at[pl.ds(0, NHI - 1)], 0, hi_peers[0])
    sent(g.at[c, pl.ds(0, NY - 1)], 1, y_peers[0])
    sent(g.at[c], 2, core_peer)
    sent(zr.at[pl.ds(0, 2 * NR - 1)], 3, z_peers[0])
    sent(wr.at[pl.ds(0, NXY - 1)], 4, core_peer)


def hand_out(u, p, w, out_u, out_p, out_w):
    out_u[...] = u[...]
    out_p[...] = p[...]
    out_w[...] = w[...]


def shards(displacement, body_force, stiffness, wet_cell, wet_normal, route, tile_u, tile_v, tile_row, tile_col, tile_rank):
    vmem = pl.BlockSpec(memory_space=pltpu.VMEM)
    hbm = pl.BlockSpec(memory_space=pltpu.HBM)
    V = pltpu.VMEM
    updated, pressure, wet = pl.pallas_call(
        body,
        out_shape=(
            jax.ShapeDtypeStruct((COMP, 4, 8, 128), F32),
            jax.ShapeDtypeStruct((4, 256), F32),
            jax.ShapeDtypeStruct((4, SLOTS), F32),
        ),
        in_specs=[hbm] * 11,
        out_specs=(vmem, vmem, vmem),
        scratch_shapes=[
            V((COMP, 4, 8, 128), F32), V((COMP, 4, 8, 128), F32), V((4, 8, 128), F32),
            V((1, SLOTS), I32), V((3, SLOTS), F32), V((1, SLOTS), I32),
            V((TILES, RANK, 256), BF16), V((TILES, RANK, 256), BF16),
            V((1, TILES), I32), V((1, TILES), I32), V((1, TILES), I32),
            V((2, 19, 16, 128), BF16), V((2, 19, 16, 128), BF16),
            V((2, 10, 16, 128), BF16), V((2, 10, 16, 128), BF16),
            V((2, 2, 4, 16, 128), BF16), V((2, 2, 4, 16, 128), BF16),
            V((2, 6, 16, 128), BF16), V((2, 6, 16, 128), BF16),
            V((2, 6, 16, 128), BF16), V((2, 6, 16, 128), BF16),
            V((COMP, 4, 8, 128), F32), V((COMP, 4, 8, 128), F32), V((4, 8, 128), F32),
            V((COMP, 4, 8, 128), F32), V((COMP, 4, 8, 128), F32), V((COMP, 4, 8, 128), F32), V((4, 8, 128), F32),
            V((COMP, 2, 8, 128), F32), V((COMP, 2, 8, 128), F32), V((COMP, 2, 8, 128), F32), V((2, 8, 128), F32),
            V((COMP, 2, 8, 128), F32), V((COMP, 2, 8, 128), F32), V((2, 8, 128), F32),
            V((COMP, 4, 8, 128), F32), V((COMP, 4, 8, 128), F32), V((4, 8, 128), F32),
            V((256, TQ), BF16), V((TQ, 256), BF16), V((256, SLOTS), BF16), V((32, SLOTS), F32),
            V((8, SLOTS), F32), V((128, SLOTS), BF16), V((TILES, 128), BF16), V((TILES, TQ), F32),
            V((32, TQ), F32), V((NXY, NV), BF16), V((SLOTS, 128), BF16), V((SLOTS, 128), F32),
            V((NHI, 8, 128), F32), V((NC, NY, 4, 16, 128), BF16),
            V((NR, 8, 128), F32), V((NZH * NR, 8, 128), F32),
            V((NXY, 1, 128), F32), V((NXY, 1, 128), F32),
            pltpu.SemaphoreType.DMA((11,)),
            pltpu.SemaphoreType.DMA((8,)), pltpu.SemaphoreType.DMA((8,)),
            pltpu.SemaphoreType.DMA((4,)), pltpu.SemaphoreType.DMA((4,)),
            pltpu.SemaphoreType.DMA((5,)), pltpu.SemaphoreType.DMA((5,)),
        ],
        compiler_params=pltpu.CompilerParams(collective_id=0, has_side_effects=True, vmem_limit_bytes=40 << 20),
    )(
        *(
            pltpu.with_memory_space_constraint(array, pltpu.HBM)
            for array in (
                displacement.reshape(COMP, 4, 8, 128),
                body_force.reshape(COMP, 4, 8, 128),
                stiffness,
                wet_cell,
                wet_normal,
                route.reshape(1, SLOTS),
                tile_u,
                tile_v,
                tile_row.reshape(1, TILES),
                tile_col.reshape(1, TILES),
                tile_rank.reshape(1, TILES),
            )
        )
    )
    updated, pressure, wet = pl.pallas_call(
        hand_out,
        out_shape=(
            jax.ShapeDtypeStruct((COMP, 4, 8, 128), F32),
            jax.ShapeDtypeStruct((4, 256), F32),
            jax.ShapeDtypeStruct((4, SLOTS), F32),
        ),
        in_specs=[vmem] * 3,
        out_specs=(vmem, vmem, vmem),
        compiler_params=pltpu.CompilerParams(vmem_limit_bytes=16 << 20),
    )(updated, pressure, wet)
    return updated.reshape(displacement.shape), pressure, wet


def solution(mesh):
    return jax.shard_map(
        shards,
        mesh=mesh,
        in_specs=(
            P(None, None, "vol", "rep", None),
            P(None, None, "vol", "rep", None),
            P("vol", "rep", None),
            P(("vol", "rep"), None),
            P(None, ("vol", "rep")),
            P(("vol", "rep"), None),
            P(("vol", "rep"), None, None),
            P(("vol", "rep"), None, None),
            P(("vol", "rep")),
            P(("vol", "rep")),
            P(("vol", "rep")),
        ),
        out_specs=(
            P(None, None, "vol", "rep", None),
            P(None, ("vol", "rep")),
            P(None, ("vol", "rep")),
        ),
        check_vma=False,
    )
```

```python
import jax
import jax.numpy as jnp
from jax import lax
from jax.experimental import pallas as pl
from jax.experimental.pallas import tpu as pltpu
from jax.sharding import PartitionSpec as P

MESH = pl.DeviceIdType.MESH
relax_factor = 0.8
mass_shift = 1.0

F32 = jnp.float32
BF16 = jnp.bfloat16
I32 = jnp.int32

NX, NZH, NY, NC = 4, 2, 8, 2
NR = 4
NHI = NX * NZH
NLO = NY * NC
NV = NHI * NLO
NXY = NX * NLO
SLOTS = 128
COMP = 12
TILES, RANK = 32, 32
TQ = TILES * RANK

NT = (((1,), (1,)), ((), ()))


def dot(a, b):
    return jnp.dot(a, b, preferred_element_type=F32)


def dot_nt(a, b):
    return lax.dot_general(a, b, NT, preferred_element_type=F32)


def iota(shape, dim):
    return lax.broadcasted_iota(I32, shape, dim)


def onehot(condition, dtype=BF16):
    return jnp.where(condition, 1.0, 0.0).astype(F32).astype(dtype)


def pairs(tiles):
    lead = 1
    for size in tiles.shape[:-2]:
        lead *= size
    return tiles.reshape(lead // 2, 16, 128).astype(BF16)


def unpairs(tiles, lead):
    return tiles.astype(F32).reshape(*lead, 8, 128)


def body(
    disp_h, force_h, stiff_h, wcell_h, wnorm_h, route_h, tu_h, tv_h, trow_h, tcol_h, trank_h,
    out_u, out_p, out_w,
    disp, force, stiff, wcell, wnorm, route, tu, tv, trow, tcol, trank,
    vol_s, vol_r, rep_s, rep_r, cor_s, cor_r, fvol_s, fvol_r, frep_s, frep_r,
    alone, f_own, c_own, ring_w, ring_once, ring_twice, ring_c, face_w, face_once, face_twice, face_c,
    corner_w, corner_once, corner_c, field, base, scale,
    vdt, ud, ol, rowhot, armask, place, sel_t, diag_m, row_m, sel_at, at_hot, za_hot,
    ra, g, zs, zr, ws, wr,
    load_sem, halo_ss, halo_rs, fhalo_ss, fhalo_rs, ph_ss, ph_rs,
):
    v = lax.axis_index("vol")
    r = lax.axis_index("rep")
    hi, lo = v // NLO, lax.rem(v, NLO)
    x, zh = hi // NZH, lax.rem(hi, NZH)
    y, c = lo // NC, lax.rem(lo, NC)

    def vol_of(x_, zh_, y_, c_):
        return ((x_ * NZH + zh_) * NY + y_) * NC + c_

    ring_x, ring_y = (2, 1, NX - 1), (4, 3, NY - 3, 2, NY - 2, 1, NY - 1)
    flip_peers = [(vol_of(lax.rem(x + j, NX), 1 - zh, y, c), r) for j in ring_x + (0,)]
    x_peers = [(vol_of(lax.rem(x + j, NX), zh, y, c), r) for j in ring_x]
    hi_peers = flip_peers + x_peers
    y_peers = [(vol_of(x, zh, lax.rem(y + j, NY), c), r) for j in ring_y]
    core_peer = (vol_of(x, zh, y, 1 - c), r)
    here = x * NLO + lo

    hops = {}
    for dx in range(NX):
        for dy in range(NY):
            for dc in range(NC):
                hops[dx, dy, dc] = 2 * (min(dx, NX - dx) + min(dy, NY - dy)) + dc
    plane_order = sorted(hops, key=lambda step: -hops[step])[:-1]
    at_x = [lax.rem(x + d, NX) for d in range(NX)]
    at_y = [lax.rem(y + d, NY) for d in range(NY)]
    at_c = [c, 1 - c]

    z_at = [(1 - zh, lax.rem(r + j, NR)) for j in (0, 1, 3)] + [(zh, lax.rem(r + j, NR)) for j in (3, 1, 2)] + [(1 - zh, lax.rem(r + 2, NR))]
    z_peers = [(vol_of(x, zh_, y, c), r_) for zh_, r_ in z_at]
    up_v, down_v = lax.rem(v + 1, NV), lax.rem(v + NV - 1, NV)
    up_r, down_r = lax.rem(r + 1, NR), lax.rem(r + NR - 1, NR)
    halo_peers = [(up_v, r), (down_v, r)] + [(a, b) for a in (up_v, down_v) for b in (up_r, down_r)]

    barrier = pltpu.get_barrier_semaphore()
    greeted = halo_peers + hi_peers + z_peers + y_peers + [core_peer]
    for peer in greeted:
        pl.semaphore_signal(barrier, inc=1, device_id=peer, device_id_type=MESH)

    sources = (disp_h, force_h, stiff_h, wcell_h, wnorm_h, route_h, trow_h, tcol_h, trank_h, tv_h, tu_h)
    targets = (disp, force, stiff, wcell, wnorm, route, trow, tcol, trank, tv, tu)
    loads = [pltpu.make_async_copy(a, b, load_sem.at[i]) for i, (a, b) in enumerate(zip(sources, targets))]
    for load in loads:
        load.start()
    for load in loads[:3]:
        load.wait()

    keep = 1.0 - relax_factor

    def rolled(w, shift, axis):
        shift = shift % (8 if axis == w.ndim - 2 else 128)
        if shift == 0:
            return w
        return pltpu.roll(w.reshape(-1, 8, 128), shift, axis - w.ndim + 3).reshape(w.shape)

    def sides(w, ring):
        row = iota(w.shape, w.ndim - 2)
        axis = w.ndim - 2
        before, after = rolled(ring, 1, axis), rolled(ring, 7, axis)
        return jnp.where(row == 0, before, rolled(w, 1, axis)) + jnp.where(row == 7, after, rolled(w, 7, axis))

    def from_ring(ring):
        row = iota(ring.shape, ring.ndim - 2)
        axis = ring.ndim - 2
        return jnp.where(row == 0, rolled(ring, 1, axis), jnp.where(row == 7, rolled(ring, 7, axis), 0.0))

    def to_ring(w):
        row = iota(w.shape, w.ndim - 2)
        axis = w.ndim - 2
        return jnp.where(row == 0, rolled(w, 1, axis), rolled(w, 7, axis))

    def along_z(w):
        lane = iota(w.shape, w.ndim - 1)
        axis = w.ndim - 1
        return jnp.where(lane == 0, 0.0, rolled(w, 1, axis)) + jnp.where(lane == 127, 0.0, rolled(w, 127, axis))

    row_c = iota((COMP, 8, 128), 1)
    own_inv = relax_factor / (mass_shift + 6.0 * stiff[...])
    own_c = own_inv * stiff[...]
    scale[...] = own_inv
    c_own[...] = own_c
    f_own[...] = force[...] * own_inv[None]
    for p in range(4):
        w = disp[:, p]
        total = sides(w, jnp.zeros_like(w)) + along_z(w)
        if p > 0:
            total = total + disp[:, p - 1]
        if p < 3:
            total = total + disp[:, p + 1]
        alone[:, p] = keep * w + f_own[:, p] + own_c[p][None] * total

    def row_of_planes(plane, row, start):
        out = None
        for p in range(4):
            moved = rolled(plane(p), start + p - row, 1)
            out = moved if out is None else jnp.where(iota(moved.shape, 1) == start + p, moved, out)
        return out

    for side in (0, 1):
        edge, second = (3, 2) if side == 0 else (0, 1)
        w_e, w_2, once = disp[:, edge], disp[:, second], alone[:, edge]
        c_e = own_c[edge]
        vol_s[side, 0:6] = pairs(w_e)
        vol_s[side, 6:12] = pairs(once)
        vol_s[side, 12:18] = pairs(f_own[:, edge] + c_e[None] * alone[:, second])
        vol_s[side, 18:19] = pairs(jnp.stack([c_e, c_e * own_c[second]]))
        up = jnp.where(row_c >= 6, w_e, jnp.where(row_c == 5, rolled(once, 6, 1), rolled(w_2, 5, 1)))
        down = jnp.where(row_c <= 1, w_e, jnp.where(row_c == 2, rolled(once, 2, 1), rolled(w_2, 3, 1)))
        half = row_c[0:6] >= 4
        cor_s[side, 0, 0:3] = pairs(jnp.where(half, up[6:12], rolled(up[0:6], 4, 1)))
        cor_s[side, 1, 0:3] = pairs(jnp.where(half, rolled(down[6:12], 4, 1), down[0:6]))
        for t in (0, 1):
            cor_s[side, t, 3:4] = pairs(jnp.stack([c_e, c_e]))
        row, inner = (7, 1) if side == 0 else (0, 7)
        first = row_of_planes(lambda p: disp[:, p], row, 0)
        then = row_of_planes(lambda p: alone[:, p], row, 4)
        rep_s[side, 0:6] = pairs(jnp.where(row_c < 4, first, then))
        last = [row_of_planes(lambda p: f_own[a:a + 6, p] + own_c[p][None] * rolled(alone[a:a + 6, p], inner, 1), row, start)
                for a, start in ((0, 0), (6, 4))]
        rep_s[side, 6:9] = pairs(jnp.where(half, last[1], last[0]))
        c_rows = row_of_planes(lambda p: own_c[p:p + 1], row, 0)
        cc_rows = row_of_planes(lambda p: own_c[p:p + 1] * rolled(own_c[p:p + 1], inner, 1), row, 4)
        c_rows = jnp.where(row_c[0:1] < 4, c_rows, cc_rows)
        rep_s[side, 9:10] = pairs(jnp.concatenate([c_rows, c_rows], axis=0))

    vol_to = [v < NV - 1, v > 0]
    vol_from = [v > 0, v < NV - 1]
    rep_to = [r < NR - 1, r > 0]
    rep_from = [r > 0, r < NR - 1]
    vol_dev, rep_dev = [up_v, down_v], [up_r, down_r]

    moves = []
    for s in (0, 1):
        moves.append((vol_s.at[s], vol_r.at[s], s, (vol_dev[s], r), vol_to[s], vol_from[s]))
    for s in (0, 1):
        for t in (0, 1):
            moves.append((cor_s.at[s, t], cor_r.at[s, t], 4 + 2 * s + t, (vol_dev[s], rep_dev[t]),
                          jnp.logical_and(vol_to[s], rep_to[t]), jnp.logical_and(vol_from[s], rep_from[t])))
    for t in (0, 1):
        moves.append((rep_s.at[t], rep_r.at[t], 2 + t, (v, rep_dev[t]), rep_to[t], rep_from[t]))

    def remote(src, dst, ss, rs, dev):
        return pltpu.make_async_remote_copy(src_ref=src, dst_ref=dst, send_sem=ss, recv_sem=rs, device_id=dev, device_id_type=MESH)

    for src, dst, at, dev, sends, comes in moves:
        @pl.when(jnp.logical_not(comes))
        def _():
            dst[...] = jnp.zeros(dst.shape, BF16)

    pl.semaphore_wait(barrier, len(greeted))

    for src, dst, at, dev, sends, comes in moves:
        @pl.when(sends)
        def _():
            remote(src, dst, halo_ss.at[at], halo_rs.at[at], dev).start()

    for load in loads[3:]:
        load.wait()
    route_row = route[...]
    route_sq = jnp.broadcast_to(route_row, (SLOTS, SLOTS))
    route_col = jnp.transpose(route_sq.astype(F32)).astype(I32)
    sub = iota((SLOTS, SLOTS), 0)
    lane = iota((SLOTS, SLOTS), 1)
    earlier = jnp.where(jnp.logical_and(route_col == route_sq, sub < lane), 1.0, 0.0)
    arrival = jnp.sum(earlier, axis=0, keepdims=True).astype(I32)
    place[...] = onehot(sub == route_sq)
    armask[...] = jnp.where(iota((8, SLOTS), 0) // 4 == jnp.broadcast_to(arrival, (8, SLOTS)), 1.0, 0.0)
    cell = wcell[...]
    z_one = onehot(sub == jnp.broadcast_to(lax.rem(cell, 128), (SLOTS, SLOTS)))
    ol[0:128] = z_one
    ol[128:256] = z_one
    rowhot[...] = jnp.where(iota((32, SLOTS), 0) == jnp.broadcast_to(cell // 128, (32, SLOTS)), 1.0, 0.0)
    owner_at = route_row // (NZH * NLO) * NLO + lax.rem(route_row, NLO)
    at_t = jnp.where(sub == jnp.broadcast_to(owner_at, (SLOTS, SLOTS)), 1.0, 0.0)
    at_hot[...] = jnp.transpose(at_t).astype(BF16)
    za = lax.rem(route_row // NLO, NZH) * 2 + arrival
    za_t = jnp.where(sub // 4 == jnp.broadcast_to(za, (SLOTS, SLOTS)), 1.0, 0.0)
    za_hot[...] = jnp.transpose(za_t)
    at_row = iota((NXY, NV), 0)
    sel_at[...] = onehot(iota((NXY, NV), 1) == at_row // NLO * (NZH * NLO) + zh * NLO + lax.rem(at_row, NLO))

    spread = onehot(iota((TILES, TQ), 1) // RANK == iota((TILES, TQ), 0))
    lists = jnp.concatenate([jnp.broadcast_to(trank[...], (4, TILES)), jnp.broadcast_to(trow[...], (4, TILES))], axis=0)
    over = dot(lists.astype(F32).astype(BF16), spread)
    rank_l, row_l = over[0:1], over[4:5]
    lane_q = lax.rem(iota((TILES, TQ), 1), RANK).astype(F32)
    diag_m[...] = jnp.where(lane_q < jnp.broadcast_to(rank_l, (TILES, TQ)), spread.astype(F32), 0.0)
    row_m[...] = jnp.where(iota((32, TQ), 0) // 8 == jnp.broadcast_to(row_l, (32, TQ)).astype(I32), 1.0, 0.0)
    col_t = jnp.where(iota((128, TILES), 0) == jnp.broadcast_to(tcol[...], (128, TILES)), 1.0, 0.0)
    col_t = jnp.concatenate([col_t, jnp.zeros((128, 96), F32)], axis=1)
    sel_t[...] = jnp.transpose(col_t)[0:TILES].astype(BF16)

    at_b, at_g = iota((256, 256), 0), iota((256, 256), 1)
    source = lax.rem(at_b, 4) * 64 + lax.rem(at_b // 64, 2) * 32 + lax.rem(at_b // 8, 8) * 4 + at_b // 128 * 2 + lax.rem(at_b // 4, 2)
    perm_v = onehot(at_g == source)
    vdt[...] = dot_nt(perm_v, tv[...].reshape(TQ, 256)).astype(BF16)
    split = at_b == lax.rem(at_g, 128) * 2 + at_g // 128
    ud[...] = dot(tu[...].reshape(TQ, 256), onehot(split)).astype(BF16)

    for src, dst, at, dev, sends, comes in moves:
        @pl.when(comes)
        def _():
            remote(src, dst, halo_ss.at[at], halo_rs.at[at], dev).wait_recv()

    upper_half = row_c <= 3

    def ring_of(low, high, start):
        return [jnp.where(iota(low.shape, 1) <= 3, rolled(high, -start - p, 1), rolled(low, 7 - start - p, 1)) for p in range(4)]

    low_r, high_r = unpairs(rep_r[0, 0:6], (COMP,)), unpairs(rep_r[1, 0:6], (COMP,))
    for p, (w, once) in enumerate(zip(ring_of(low_r, high_r, 0), ring_of(low_r, high_r, 4))):
        ring_w[:, p] = w
        ring_once[:, p] = once
    low_r, high_r = unpairs(rep_r[0, 6:9], (6,)), unpairs(rep_r[1, 6:9], (6,))
    for p, (a, b) in enumerate(zip(ring_of(low_r, high_r, 0), ring_of(low_r, high_r, 4))):
        ring_twice[0:6, p] = a
        ring_twice[6:12, p] = b
    low_r, high_r = unpairs(rep_r[0, 9:10], (2,))[0:1], unpairs(rep_r[1, 9:10], (2,))[0:1]
    ring_cc = ring_of(low_r, high_r, 4)
    for p, part in enumerate(ring_of(low_r, high_r, 0)):
        ring_c[p:p + 1] = part
    for s in (0, 1):
        face_w[:, s] = unpairs(vol_r[s, 0:6], (COMP,))
        face_once[:, s] = unpairs(vol_r[s, 6:12], (COMP,))
        c_s = unpairs(vol_r[s, 18:19], (2,))
        face_c[s] = c_s[0]
        low_t, high_t = unpairs(cor_r[s, 0, 0:3], (6,)), unpairs(cor_r[s, 1, 0:3], (6,))
        low_c = jnp.concatenate([rolled(low_t, 4, 1), low_t], axis=0)
        high_c = jnp.concatenate([high_t, rolled(high_t, 4, 1)], axis=0)
        corner_w[:, s] = jnp.where(upper_half, high_c, low_c)
        corner_once[:, s] = jnp.where(upper_half, rolled(high_c, 6, 1), rolled(low_c, 2, 1))
        c_low, c_high = unpairs(cor_r[s, 0, 3:4], (2,)), unpairs(cor_r[s, 1, 3:4], (2,))
        corner_c[s] = jnp.where(upper_half[0], c_high[0], c_low[0])
        beside = jnp.where(row_c == 0, rolled(low_c, 4, 1), jnp.where(row_c == 7, rolled(high_c, 4, 1), 0.0))
        face_twice[:, s] = unpairs(vol_r[s, 12:18], (COMP,)) + c_s[1][None] * beside
        below = jnp.where(upper_half, rolled(high_c, 7, 1), rolled(low_c, 1, 1))
        ring_twice[:, 3 * s] = ring_twice[:, 3 * s] + ring_cc[3 * s] * below

    def sweeps(i, carry):
        own, ring = disp[i], ring_w[i]
        f, cc, c_r, c_f, c_x = f_own[i], c_own[...], ring_c[...], face_c[...], corner_c[...]
        face, corner = face_w[i], corner_w[i]

        def beside(w, ends):
            wide = jnp.concatenate([ends[0:1], w, ends[1:2]], axis=0)
            return wide[0:4] + wide[2:6]

        def ends_of(w):
            return jnp.concatenate([w[0:1], w[3:4]], axis=0)

        zero = jnp.zeros((2, 8, 128), F32)
        from_faces = jnp.concatenate([face[0:1], zero, face[1:2]], axis=0)
        from_corners = jnp.concatenate([corner[0:1], zero, corner[1:2]], axis=0)
        own_1 = alone[i] + cc * (from_faces + from_ring(ring))
        ring_1 = ring_once[i] + c_r * (to_ring(own) + from_corners)
        face_1 = face_once[i] + c_f * (ends_of(own) + from_ring(corner))
        corner_1 = corner_once[i] + c_x * (ends_of(ring) + to_ring(face))
        own_2 = keep * own_1 + f + cc * (beside(own_1, face_1) + sides(own_1, ring_1) + along_z(own_1))
        ring_2 = ring_twice[i] + keep * ring_1 + c_r * (to_ring(own_1) + beside(ring_1, corner_1) + along_z(ring_1))
        face_2 = face_twice[i] + keep * face_1 + c_f * (ends_of(own_1) + sides(face_1, corner_1) + along_z(face_1))
        field[i] = keep * own_2 + f + cc * (beside(own_2, face_2) + sides(own_2, ring_2) + along_z(own_2))
        return carry

    lax.fori_loop(0, COMP, sweeps, 0, unroll=12)

    flat = field[...].reshape(COMP * 32, 128)
    upper = flat.astype(BF16)
    lower = (flat - upper.astype(F32)).astype(BF16)
    picked = dot(jnp.concatenate([upper, lower], axis=1), ol[...]).reshape(COMP, 32, SLOTS)
    normal = wnorm[...]
    picked = jnp.sum(picked * rowhot[...][None], axis=1)
    traces = normal[0:1] * picked[0:4] + normal[1:2] * picked[4:8] + normal[2:3] * picked[8:12]
    traces = jnp.concatenate([traces, traces], axis=0) * armask[...]
    message = dot_nt(traces.astype(BF16), place[...])

    ra[zh, x] = message
    for peer in flip_peers:
        remote(ra.at[zh, x], ra.at[zh, x], ph_ss.at[0], ph_rs.at[0], peer).start()
    for peer in x_peers:
        remote(ra.at[zh, x], ra.at[zh, x], ph_ss.at[5], ph_rs.at[5], peer).start()

    def wait_all(region, at, peer):
        remote(region, region, ph_ss.at[at], ph_rs.at[at], peer).wait_recv()

    def gather_y(z, at):
        rows = []
        for k in range(4):
            rows += [ra[z, :, k], ra[z, :, 4 + k]]
        g[c, z, y] = jnp.concatenate(rows, axis=0).astype(BF16).reshape(2, 16, 128)
        for peer in y_peers:
            remote(g.at[c, z, y], g.at[c, z, y], ph_ss.at[at], ph_rs.at[at], peer).start()

    wait_all(ra.at[zh, pl.ds(0, NX - 1)], 5, core_peer)
    gather_y(zh, 1)
    wait_all(ra.at[1 - zh], 0, core_peer)
    gather_y(1 - zh, 6)

    wait_all(g.at[c, zh, pl.ds(0, NY - 1)], 1, core_peer)
    remote(g.at[c, zh], g.at[c, zh], ph_ss.at[2], ph_rs.at[2], core_peer).start()
    wait_all(g.at[c, 1 - zh, pl.ds(0, NY - 1)], 6, core_peer)
    remote(g.at[c, 1 - zh], g.at[c, 1 - zh], ph_ss.at[7], ph_rs.at[7], core_peer).start()

    wait_all(g.at[c, zh], 2, core_peer)
    wait_all(g.at[c, 1 - zh], 7, core_peer)

    pick = sel_t[...]
    waves = g[...].astype(F32).reshape(NC, NZH, NY, 4, 8, 128)
    waves = [waves[:, :, :, k].reshape(256, 128).astype(BF16) for k in range(4)]
    chosen = jnp.concatenate([dot_nt(pick, wave) for wave in waves], axis=0).astype(BF16)
    every = dot(chosen, vdt[...])
    coef = jnp.sum(every.reshape(4, TILES, TQ) * diag_m[...][None], axis=1)
    coef = jnp.concatenate([coef, coef], axis=0)
    spread_c = (jnp.concatenate([coef] * 4, axis=0) * row_m[...]).astype(BF16)
    parts = dot(spread_c, ud[...])
    take = lax.rem(iota((32, 128), 0), 8) < 4
    parts = jnp.where(take, parts[:, 0:128], parts[:, 128:256])
    zs[...] = parts.reshape(4, 8, 128)

    mine_at = zh * NR + r
    for (zh_, r_), peer in zip(z_at, z_peers):
        remote(zs.at[r_], zr.at[mine_at], ph_ss.at[3], ph_rs.at[3], peer).start()
    zr[mine_at] = zs[r]
    row_f = iota((COMP, 8, 128), 1)
    fvol_s[0] = pairs(field[:, 3])
    fvol_s[1] = pairs(field[:, 0])
    for t in (0, 1):
        acc = jnp.zeros((COMP, 8, 128), F32)
        for p in range(4):
            shift = p + 1 if t == 0 else p
            acc = jnp.where(row_f == p, rolled(field[:, p], shift, 1), acc)
        frep_s[t] = pairs(acc)
    fmoves = []
    for s in (0, 1):
        fmoves.append((fvol_s.at[s], fvol_r.at[s], s, (vol_dev[s], r), vol_to[s], vol_from[s]))
        fmoves.append((frep_s.at[s], frep_r.at[s], 2 + s, (v, rep_dev[s]), rep_to[s], rep_from[s]))
    for src, dst, at, dev, sends, comes in fmoves:
        @pl.when(sends)
        def _():
            remote(src, dst, fhalo_ss.at[at], fhalo_rs.at[at], dev).start()

        @pl.when(jnp.logical_not(comes))
        def _():
            dst[...] = jnp.zeros(dst.shape, BF16)


    wait_all(zr.at[pl.ds(0, 2 * NR - 1)], 3, z_peers[0])
    sums = jnp.sum(zr[...].reshape(NZH, NR, 8, 128), axis=1)
    back = jnp.concatenate([sums.reshape(16, 128), jnp.zeros((112, 128), F32)], axis=0).astype(BF16)
    ws[...] = dot_nt(sel_at[...], back).reshape(NXY, 1, 128)

    for dx, dy, dc in plane_order:
        at = at_x[dx] * NLO + at_y[dy] * NC + at_c[dc]
        remote(ws.at[at], wr.at[here], ph_ss.at[4], ph_rs.at[4], (vol_of(at_x[dx], zh, at_y[dy], at_c[dc]), r)).start()
    wr[here] = ws[here]
    own = jnp.where(zh == 0, sums[0], sums[1])
    wide = jnp.concatenate([own[0:4], own[4:8]], axis=1)
    join = jnp.where(at_g == lax.rem(at_b, 128) * 2 + at_b // 128, 1.0, 0.0)
    out_p[...] = jnp.dot(wide, join, precision=lax.Precision.HIGHEST, preferred_element_type=F32)

    for src, dst, at, dev, sends, comes in fmoves:
        @pl.when(comes)
        def _():
            remote(src, dst, fhalo_ss.at[at], fhalo_rs.at[at], dev).wait_recv()

    low_f, high_f = unpairs(fvol_r[0], (COMP,)), unpairs(fvol_r[1], (COMP,))
    low_y, high_y = unpairs(frep_r[0], (COMP,)), unpairs(frep_r[1], (COMP,))
    for p in range(4):
        w = field[:, p]
        total = (field[:, p - 1] if p > 0 else low_f) + (field[:, p + 1] if p < 3 else high_f)
        before = pltpu.roll(low_y, 8 - p, 1) if p > 0 else low_y
        after = pltpu.roll(high_y, 7 - p, 1)
        total = total + jnp.where(row_f == 0, before, pltpu.roll(w, 1, 1))
        total = total + jnp.where(row_f == 7, after, pltpu.roll(w, 7, 1))
        lane_f = iota((COMP, 8, 128), 2)
        total = total + jnp.where(lane_f == 0, 0.0, pltpu.roll(w, 1, 2))
        total = total + jnp.where(lane_f == 127, 0.0, pltpu.roll(w, 127, 2))
        base[:, p] = keep * w + f_own[:, p] + c_own[p][None] * total

    wait_all(wr.at[pl.ds(0, NXY - 1)], 4, core_peer)

    got = wr[...].reshape(NXY, 128).astype(BF16)
    got = jnp.concatenate([got, jnp.zeros((128 - NXY, 128), BF16)], axis=0)
    per_slot = (dot(at_hot[...], got) * za_hot[...]).astype(BF16)
    wave = onehot(lax.rem(iota((8, 128), 1), 4) == iota((8, 128), 0))
    wet = dot_nt(wave, per_slot)[0:4]
    out_w[...] = wet

    normal = -wnorm[...]
    load = jnp.concatenate([normal[i:i + 1] * wet for i in range(3)], axis=0)
    rows = (load[:, None, :] * rowhot[...][None]).reshape(COMP * 32, SLOTS)
    upper = rows.astype(BF16)
    lower = (rows - upper.astype(F32)).astype(BF16)
    z_one = ol[0:128]
    placed = dot_nt(jnp.concatenate([upper, lower], axis=1), jnp.concatenate([z_one, z_one], axis=1))
    out_u[...] = base[...] + scale[...][None] * placed.reshape(COMP, 4, 8, 128)

    for src, dst, at, dev, sends, comes in moves:
        @pl.when(sends)
        def _():
            remote(src, dst, halo_ss.at[at], halo_rs.at[at], dev).wait_send()
    for src, dst, at, dev, sends, comes in fmoves:
        @pl.when(sends)
        def _():
            remote(src, dst, fhalo_ss.at[at], fhalo_rs.at[at], dev).wait_send()

    def sent(region, at, peer):
        remote(region, region, ph_ss.at[at], ph_rs.at[at], peer).wait_send()

    sent(ra.at[1 - zh], 0, core_peer)
    sent(ra.at[zh, pl.ds(0, NX - 1)], 5, core_peer)
    for z, at in ((zh, 1), (1 - zh, 6)):
        sent(g.at[c, z, pl.ds(0, NY - 1)], at, core_peer)
    sent(g.at[c, zh], 2, core_peer)
    sent(g.at[c, 1 - zh], 7, core_peer)
    sent(zr.at[pl.ds(0, 2 * NR - 1)], 3, z_peers[0])
    sent(wr.at[pl.ds(0, NXY - 1)], 4, core_peer)


def hand_out(u, p, w, out_u, out_p, out_w):
    out_u[...] = u[...]
    out_p[...] = p[...]
    out_w[...] = w[...]


def shards(displacement, body_force, stiffness, wet_cell, wet_normal, route, tile_u, tile_v, tile_row, tile_col, tile_rank):
    vmem = pl.BlockSpec(memory_space=pltpu.VMEM)
    hbm = pl.BlockSpec(memory_space=pltpu.HBM)
    V = pltpu.VMEM
    updated, pressure, wet = pl.pallas_call(
        body,
        out_shape=(
            jax.ShapeDtypeStruct((COMP, 4, 8, 128), F32),
            jax.ShapeDtypeStruct((4, 256), F32),
            jax.ShapeDtypeStruct((4, SLOTS), F32),
        ),
        in_specs=[hbm] * 11,
        out_specs=(vmem, vmem, vmem),
        scratch_shapes=[
            V((COMP, 4, 8, 128), F32), V((COMP, 4, 8, 128), F32), V((4, 8, 128), F32),
            V((1, SLOTS), I32), V((3, SLOTS), F32), V((1, SLOTS), I32),
            V((TILES, RANK, 256), BF16), V((TILES, RANK, 256), BF16),
            V((1, TILES), I32), V((1, TILES), I32), V((1, TILES), I32),
            V((2, 19, 16, 128), BF16), V((2, 19, 16, 128), BF16),
            V((2, 10, 16, 128), BF16), V((2, 10, 16, 128), BF16),
            V((2, 2, 4, 16, 128), BF16), V((2, 2, 4, 16, 128), BF16),
            V((2, 6, 16, 128), BF16), V((2, 6, 16, 128), BF16),
            V((2, 6, 16, 128), BF16), V((2, 6, 16, 128), BF16),
            V((COMP, 4, 8, 128), F32), V((COMP, 4, 8, 128), F32), V((4, 8, 128), F32),
            V((COMP, 4, 8, 128), F32), V((COMP, 4, 8, 128), F32), V((COMP, 4, 8, 128), F32), V((4, 8, 128), F32),
            V((COMP, 2, 8, 128), F32), V((COMP, 2, 8, 128), F32), V((COMP, 2, 8, 128), F32), V((2, 8, 128), F32),
            V((COMP, 2, 8, 128), F32), V((COMP, 2, 8, 128), F32), V((2, 8, 128), F32),
            V((COMP, 4, 8, 128), F32), V((COMP, 4, 8, 128), F32), V((4, 8, 128), F32),
            V((256, TQ), BF16), V((TQ, 256), BF16), V((256, SLOTS), BF16), V((32, SLOTS), F32),
            V((8, SLOTS), F32), V((128, SLOTS), BF16), V((TILES, 128), BF16), V((TILES, TQ), F32),
            V((32, TQ), F32), V((NXY, NV), BF16), V((SLOTS, 128), BF16), V((SLOTS, 128), F32),
            V((NZH, NX, 8, 128), F32), V((NC, NZH, NY, 2, 16, 128), BF16),
            V((NR, 8, 128), F32), V((NZH * NR, 8, 128), F32),
            V((NXY, 1, 128), F32), V((NXY, 1, 128), F32),
            pltpu.SemaphoreType.DMA((11,)),
            pltpu.SemaphoreType.DMA((8,)), pltpu.SemaphoreType.DMA((8,)),
            pltpu.SemaphoreType.DMA((4,)), pltpu.SemaphoreType.DMA((4,)),
            pltpu.SemaphoreType.DMA((8,)), pltpu.SemaphoreType.DMA((8,)),
        ],
        compiler_params=pltpu.CompilerParams(collective_id=0, has_side_effects=True, vmem_limit_bytes=40 << 20),
    )(
        *(
            pltpu.with_memory_space_constraint(array, pltpu.HBM)
            for array in (
                displacement.reshape(COMP, 4, 8, 128),
                body_force.reshape(COMP, 4, 8, 128),
                stiffness,
                wet_cell,
                wet_normal,
                route.reshape(1, SLOTS),
                tile_u,
                tile_v,
                tile_row.reshape(1, TILES),
                tile_col.reshape(1, TILES),
                tile_rank.reshape(1, TILES),
            )
        )
    )
    updated, pressure, wet = pl.pallas_call(
        hand_out,
        out_shape=(
            jax.ShapeDtypeStruct((COMP, 4, 8, 128), F32),
            jax.ShapeDtypeStruct((4, 256), F32),
            jax.ShapeDtypeStruct((4, SLOTS), F32),
        ),
        in_specs=[vmem] * 3,
        out_specs=(vmem, vmem, vmem),
        compiler_params=pltpu.CompilerParams(vmem_limit_bytes=16 << 20),
    )(updated, pressure, wet)
    return updated.reshape(displacement.shape), pressure, wet


def solution(mesh):
    return jax.shard_map(
        shards,
        mesh=mesh,
        in_specs=(
            P(None, None, "vol", "rep", None),
            P(None, None, "vol", "rep", None),
            P("vol", "rep", None),
            P(("vol", "rep"), None),
            P(None, ("vol", "rep")),
            P(("vol", "rep"), None),
            P(("vol", "rep"), None, None),
            P(("vol", "rep"), None, None),
            P(("vol", "rep")),
            P(("vol", "rep")),
            P(("vol", "rep")),
        ),
        out_specs=(
            P(None, None, "vol", "rep", None),
            P(None, ("vol", "rep")),
            P(None, ("vol", "rep")),
        ),
        check_vma=False,
    )
```

```python
import jax
import jax.numpy as jnp
from jax import lax
from jax.experimental import pallas as pl
from jax.experimental.pallas import tpu as pltpu
from jax.sharding import PartitionSpec as P

MESH = pl.DeviceIdType.MESH
relax_factor = 0.8
mass_shift = 1.0

F32 = jnp.float32
BF16 = jnp.bfloat16
I32 = jnp.int32

NX, NZH, NY, NC = 4, 2, 8, 2
NR = 4
NHI = NX * NZH
NLO = NY * NC
NV = NHI * NLO
NXY = NX * NLO
SLOTS = 128
COMP = 12
TILES, RANK = 32, 32
TQ = TILES * RANK

NT = (((1,), (1,)), ((), ()))


def dot(a, b):
    return jnp.dot(a, b, preferred_element_type=F32)


def dot_nt(a, b):
    return lax.dot_general(a, b, NT, preferred_element_type=F32)


def iota(shape, dim):
    return lax.broadcasted_iota(I32, shape, dim)


def onehot(condition, dtype=BF16):
    return jnp.where(condition, 1.0, 0.0).astype(F32).astype(dtype)


def pairs(tiles):
    lead = 1
    for size in tiles.shape[:-2]:
        lead *= size
    return tiles.reshape(lead // 2, 16, 128).astype(BF16)


def unpairs(tiles, lead):
    return tiles.astype(F32).reshape(*lead, 8, 128)


def body(
    disp_h, force_h, stiff_h, wcell_h, wnorm_h, route_h, tu_h, tv_h, trow_h, tcol_h, trank_h,
    out_u, out_p, out_w,
    disp, force, stiff, wcell, wnorm, route, tu, tv, trow, tcol, trank,
    vol_s, vol_r, rep_s, rep_r, cor_s, cor_r, fvol_s, fvol_r, frep_s, frep_r,
    alone, f_own, c_own, ring_w, ring_once, ring_twice, ring_c, face_w, face_once, face_twice, face_c,
    corner_w, corner_once, corner_c, field, base, scale,
    vdt, ud, ol, rowhot, armask, place, sel_t, diag_m, row_m, sel_at, at_hot, za_hot,
    ra, g, zs, zr, ws, wr,
    load_sem, halo_ss, halo_rs, fhalo_ss, fhalo_rs, ph_ss, ph_rs,
):
    v = lax.axis_index("vol")
    r = lax.axis_index("rep")
    hi, lo = v // NLO, lax.rem(v, NLO)
    x, zh = hi // NZH, lax.rem(hi, NZH)
    y, c = lo // NC, lax.rem(lo, NC)

    def vol_of(x_, zh_, y_, c_):
        return ((x_ * NZH + zh_) * NY + y_) * NC + c_

    ring_x, ring_y = (2, 1, NX - 1), (4, 3, NY - 3, 2, NY - 2, 1, NY - 1)
    flip_peers = [(vol_of(lax.rem(x + j, NX), 1 - zh, y, c), r) for j in ring_x + (0,)]
    x_peers = [(vol_of(lax.rem(x + j, NX), zh, y, c), r) for j in ring_x]
    hi_peers = flip_peers + x_peers
    y_peers = [(vol_of(x, zh, lax.rem(y + j, NY), c), r) for j in ring_y]
    core_peer = (vol_of(x, zh, y, 1 - c), r)
    here = x * NLO + lo

    hops = {}
    for dx in range(NX):
        for dy in range(NY):
            for dc in range(NC):
                hops[dx, dy, dc] = 2 * (min(dx, NX - dx) + min(dy, NY - dy)) + dc
    plane_order = sorted(hops, key=lambda step: -hops[step])[:-1]
    at_x = [lax.rem(x + d, NX) for d in range(NX)]
    at_y = [lax.rem(y + d, NY) for d in range(NY)]
    at_c = [c, 1 - c]

    z_at = [(1 - zh, lax.rem(r + j, NR)) for j in (0, 1, 3)] + [(zh, lax.rem(r + j, NR)) for j in (3, 1, 2)] + [(1 - zh, lax.rem(r + 2, NR))]
    z_peers = [(vol_of(x, zh_, y, c), r_) for zh_, r_ in z_at]
    up_v, down_v = lax.rem(v + 1, NV), lax.rem(v + NV - 1, NV)
    up_r, down_r = lax.rem(r + 1, NR), lax.rem(r + NR - 1, NR)
    halo_peers = [(up_v, r), (down_v, r)] + [(a, b) for a in (up_v, down_v) for b in (up_r, down_r)]

    barrier = pltpu.get_barrier_semaphore()
    greeted = halo_peers + hi_peers + z_peers + y_peers + [core_peer]
    for peer in greeted:
        pl.semaphore_signal(barrier, inc=1, device_id=peer, device_id_type=MESH)

    sources = (disp_h, force_h, stiff_h, wcell_h, wnorm_h, route_h, trow_h, tcol_h, trank_h, tv_h, tu_h)
    targets = (disp, force, stiff, wcell, wnorm, route, trow, tcol, trank, tv, tu)
    loads = [pltpu.make_async_copy(a, b, load_sem.at[i]) for i, (a, b) in enumerate(zip(sources, targets))]
    for load in loads:
        load.start()
    for load in loads[:3]:
        load.wait()

    keep = 1.0 - relax_factor

    def rolled(w, shift, axis):
        shift = shift % (8 if axis == w.ndim - 2 else 128)
        if shift == 0:
            return w
        return pltpu.roll(w.reshape(-1, 8, 128), shift, axis - w.ndim + 3).reshape(w.shape)

    def sides(w, ring):
        row = iota(w.shape, w.ndim - 2)
        axis = w.ndim - 2
        before, after = rolled(ring, 1, axis), rolled(ring, 7, axis)
        return jnp.where(row == 0, before, rolled(w, 1, axis)) + jnp.where(row == 7, after, rolled(w, 7, axis))

    def from_ring(ring):
        row = iota(ring.shape, ring.ndim - 2)
        axis = ring.ndim - 2
        return jnp.where(row == 0, rolled(ring, 1, axis), jnp.where(row == 7, rolled(ring, 7, axis), 0.0))

    def to_ring(w):
        row = iota(w.shape, w.ndim - 2)
        axis = w.ndim - 2
        return jnp.where(row == 0, rolled(w, 1, axis), rolled(w, 7, axis))

    def along_z(w):
        lane = iota(w.shape, w.ndim - 1)
        axis = w.ndim - 1
        return jnp.where(lane == 0, 0.0, rolled(w, 1, axis)) + jnp.where(lane == 127, 0.0, rolled(w, 127, axis))

    row_c = iota((COMP, 8, 128), 1)
    own_inv = relax_factor / (mass_shift + 6.0 * stiff[...])
    own_c = own_inv * stiff[...]
    scale[...] = own_inv
    c_own[...] = own_c
    f_own[...] = force[...] * own_inv[None]
    for p in range(4):
        w = disp[:, p]
        total = sides(w, jnp.zeros_like(w)) + along_z(w)
        if p > 0:
            total = total + disp[:, p - 1]
        if p < 3:
            total = total + disp[:, p + 1]
        alone[:, p] = keep * w + f_own[:, p] + own_c[p][None] * total

    def row_of_planes(plane, row, start):
        out = None
        for p in range(4):
            moved = rolled(plane(p), start + p - row, 1)
            out = moved if out is None else jnp.where(iota(moved.shape, 1) == start + p, moved, out)
        return out

    for side in (0, 1):
        edge, second = (3, 2) if side == 0 else (0, 1)
        w_e, w_2, once = disp[:, edge], disp[:, second], alone[:, edge]
        c_e = own_c[edge]
        vol_s[side, 0:6] = pairs(w_e)
        vol_s[side, 6:12] = pairs(once)
        vol_s[side, 12:18] = pairs(f_own[:, edge] + c_e[None] * alone[:, second])
        vol_s[side, 18:19] = pairs(jnp.stack([c_e, c_e * own_c[second]]))
        up = jnp.where(row_c >= 6, w_e, jnp.where(row_c == 5, rolled(once, 6, 1), rolled(w_2, 5, 1)))
        down = jnp.where(row_c <= 1, w_e, jnp.where(row_c == 2, rolled(once, 2, 1), rolled(w_2, 3, 1)))
        half = row_c[0:6] >= 4
        cor_s[side, 0, 0:3] = pairs(jnp.where(half, up[6:12], rolled(up[0:6], 4, 1)))
        cor_s[side, 1, 0:3] = pairs(jnp.where(half, rolled(down[6:12], 4, 1), down[0:6]))
        for t in (0, 1):
            cor_s[side, t, 3:4] = pairs(jnp.stack([c_e, c_e]))
        row, inner = (7, 1) if side == 0 else (0, 7)
        first = row_of_planes(lambda p: disp[:, p], row, 0)
        then = row_of_planes(lambda p: alone[:, p], row, 4)
        rep_s[side, 0:6] = pairs(jnp.where(row_c < 4, first, then))
        last = [row_of_planes(lambda p: f_own[a:a + 6, p] + own_c[p][None] * rolled(alone[a:a + 6, p], inner, 1), row, start)
                for a, start in ((0, 0), (6, 4))]
        rep_s[side, 6:9] = pairs(jnp.where(half, last[1], last[0]))
        c_rows = row_of_planes(lambda p: own_c[p:p + 1], row, 0)
        cc_rows = row_of_planes(lambda p: own_c[p:p + 1] * rolled(own_c[p:p + 1], inner, 1), row, 4)
        c_rows = jnp.where(row_c[0:1] < 4, c_rows, cc_rows)
        rep_s[side, 9:10] = pairs(jnp.concatenate([c_rows, c_rows], axis=0))

    vol_to = [v < NV - 1, v > 0]
    vol_from = [v > 0, v < NV - 1]
    rep_to = [r < NR - 1, r > 0]
    rep_from = [r > 0, r < NR - 1]
    vol_dev, rep_dev = [up_v, down_v], [up_r, down_r]

    moves = []
    for s in (0, 1):
        moves.append((vol_s.at[s], vol_r.at[s], s, (vol_dev[s], r), vol_to[s], vol_from[s]))
    for s in (0, 1):
        for t in (0, 1):
            moves.append((cor_s.at[s, t], cor_r.at[s, t], 4 + 2 * s + t, (vol_dev[s], rep_dev[t]),
                          jnp.logical_and(vol_to[s], rep_to[t]), jnp.logical_and(vol_from[s], rep_from[t])))
    for t in (0, 1):
        moves.append((rep_s.at[t], rep_r.at[t], 2 + t, (v, rep_dev[t]), rep_to[t], rep_from[t]))

    def remote(src, dst, ss, rs, dev):
        return pltpu.make_async_remote_copy(src_ref=src, dst_ref=dst, send_sem=ss, recv_sem=rs, device_id=dev, device_id_type=MESH)

    for src, dst, at, dev, sends, comes in moves:
        @pl.when(jnp.logical_not(comes))
        def _():
            dst[...] = jnp.zeros(dst.shape, BF16)

    pl.semaphore_wait(barrier, len(greeted))

    for src, dst, at, dev, sends, comes in moves[:6]:
        @pl.when(sends)
        def _():
            remote(src, dst, halo_ss.at[at], halo_rs.at[at], dev).start()

    for load in loads[3:]:
        load.wait()
    route_row = route[...]
    route_sq = jnp.broadcast_to(route_row, (SLOTS, SLOTS))
    route_col = jnp.transpose(route_sq.astype(F32)).astype(I32)
    sub = iota((SLOTS, SLOTS), 0)
    lane = iota((SLOTS, SLOTS), 1)
    earlier = jnp.where(jnp.logical_and(route_col == route_sq, sub < lane), 1.0, 0.0)
    arrival = jnp.sum(earlier, axis=0, keepdims=True).astype(I32)
    place[...] = onehot(sub == route_sq)
    armask[...] = jnp.where(iota((8, SLOTS), 0) // 4 == jnp.broadcast_to(arrival, (8, SLOTS)), 1.0, 0.0)
    cell = wcell[...]
    z_one = onehot(sub == jnp.broadcast_to(lax.rem(cell, 128), (SLOTS, SLOTS)))
    ol[0:128] = z_one
    ol[128:256] = z_one
    rowhot[...] = jnp.where(iota((32, SLOTS), 0) == jnp.broadcast_to(cell // 128, (32, SLOTS)), 1.0, 0.0)
    owner_at = route_row // (NZH * NLO) * NLO + lax.rem(route_row, NLO)
    at_t = jnp.where(sub == jnp.broadcast_to(owner_at, (SLOTS, SLOTS)), 1.0, 0.0)
    at_hot[...] = jnp.transpose(at_t).astype(BF16)
    za = lax.rem(route_row // NLO, NZH) * 2 + arrival
    za_t = jnp.where(sub // 4 == jnp.broadcast_to(za, (SLOTS, SLOTS)), 1.0, 0.0)
    za_hot[...] = jnp.transpose(za_t)
    at_row = iota((NXY, NV), 0)
    sel_at[...] = onehot(iota((NXY, NV), 1) == at_row // NLO * (NZH * NLO) + zh * NLO + lax.rem(at_row, NLO))

    for src, dst, at, dev, sends, comes in moves[6:]:
        @pl.when(sends)
        def _():
            remote(src, dst, halo_ss.at[at], halo_rs.at[at], dev).start()

    spread = onehot(iota((TILES, TQ), 1) // RANK == iota((TILES, TQ), 0))
    lists = jnp.concatenate([jnp.broadcast_to(trank[...], (4, TILES)), jnp.broadcast_to(trow[...], (4, TILES))], axis=0)
    over = dot(lists.astype(F32).astype(BF16), spread)
    rank_l, row_l = over[0:1], over[4:5]
    lane_q = lax.rem(iota((TILES, TQ), 1), RANK).astype(F32)
    diag_m[...] = jnp.where(lane_q < jnp.broadcast_to(rank_l, (TILES, TQ)), spread.astype(F32), 0.0)
    row_m[...] = jnp.where(iota((32, TQ), 0) // 8 == jnp.broadcast_to(row_l, (32, TQ)).astype(I32), 1.0, 0.0)
    col_t = jnp.where(iota((128, TILES), 0) == jnp.broadcast_to(tcol[...], (128, TILES)), 1.0, 0.0)
    col_t = jnp.concatenate([col_t, jnp.zeros((128, 96), F32)], axis=1)
    sel_t[...] = jnp.transpose(col_t)[0:TILES].astype(BF16)

    at_b, at_g = iota((256, 256), 0), iota((256, 256), 1)
    source = lax.rem(at_b, 8) * 32 + lax.rem(at_b // 16, 8) * 4 + at_b // 128 * 2 + lax.rem(at_b // 8, 2)
    perm_v = onehot(at_g == source)
    vdt[...] = dot_nt(perm_v, tv[...].reshape(TQ, 256)).astype(BF16)
    split = at_b == lax.rem(at_g, 128) * 2 + at_g // 128
    ud[...] = dot(tu[...].reshape(TQ, 256), onehot(split)).astype(BF16)

    for src, dst, at, dev, sends, comes in moves:
        @pl.when(comes)
        def _():
            remote(src, dst, halo_ss.at[at], halo_rs.at[at], dev).wait_recv()

    upper_half = row_c <= 3

    def ring_of(low, high, start):
        return [jnp.where(iota(low.shape, 1) <= 3, rolled(high, -start - p, 1), rolled(low, 7 - start - p, 1)) for p in range(4)]

    low_r, high_r = unpairs(rep_r[0, 0:6], (COMP,)), unpairs(rep_r[1, 0:6], (COMP,))
    for p, (w, once) in enumerate(zip(ring_of(low_r, high_r, 0), ring_of(low_r, high_r, 4))):
        ring_w[:, p] = w
        ring_once[:, p] = once
    low_r, high_r = unpairs(rep_r[0, 6:9], (6,)), unpairs(rep_r[1, 6:9], (6,))
    for p, (a, b) in enumerate(zip(ring_of(low_r, high_r, 0), ring_of(low_r, high_r, 4))):
        ring_twice[0:6, p] = a
        ring_twice[6:12, p] = b
    low_r, high_r = unpairs(rep_r[0, 9:10], (2,))[0:1], unpairs(rep_r[1, 9:10], (2,))[0:1]
    ring_cc = ring_of(low_r, high_r, 4)
    for p, part in enumerate(ring_of(low_r, high_r, 0)):
        ring_c[p:p + 1] = part
    for s in (0, 1):
        face_w[:, s] = unpairs(vol_r[s, 0:6], (COMP,))
        face_once[:, s] = unpairs(vol_r[s, 6:12], (COMP,))
        c_s = unpairs(vol_r[s, 18:19], (2,))
        face_c[s] = c_s[0]
        low_t, high_t = unpairs(cor_r[s, 0, 0:3], (6,)), unpairs(cor_r[s, 1, 0:3], (6,))
        low_c = jnp.concatenate([rolled(low_t, 4, 1), low_t], axis=0)
        high_c = jnp.concatenate([high_t, rolled(high_t, 4, 1)], axis=0)
        corner_w[:, s] = jnp.where(upper_half, high_c, low_c)
        corner_once[:, s] = jnp.where(upper_half, rolled(high_c, 6, 1), rolled(low_c, 2, 1))
        c_low, c_high = unpairs(cor_r[s, 0, 3:4], (2,)), unpairs(cor_r[s, 1, 3:4], (2,))
        corner_c[s] = jnp.where(upper_half[0], c_high[0], c_low[0])
        beside = jnp.where(row_c == 0, rolled(low_c, 4, 1), jnp.where(row_c == 7, rolled(high_c, 4, 1), 0.0))
        face_twice[:, s] = unpairs(vol_r[s, 12:18], (COMP,)) + c_s[1][None] * beside
        below = jnp.where(upper_half, rolled(high_c, 7, 1), rolled(low_c, 1, 1))
        ring_twice[:, 3 * s] = ring_twice[:, 3 * s] + ring_cc[3 * s] * below

    def sweeps(i, carry):
        own, ring = disp[i], ring_w[i]
        f, cc, c_r, c_f, c_x = f_own[i], c_own[...], ring_c[...], face_c[...], corner_c[...]
        face, corner = face_w[i], corner_w[i]

        def beside(w, ends):
            wide = jnp.concatenate([ends[0:1], w, ends[1:2]], axis=0)
            return wide[0:4] + wide[2:6]

        def ends_of(w):
            return jnp.concatenate([w[0:1], w[3:4]], axis=0)

        zero = jnp.zeros((2, 8, 128), F32)
        from_faces = jnp.concatenate([face[0:1], zero, face[1:2]], axis=0)
        from_corners = jnp.concatenate([corner[0:1], zero, corner[1:2]], axis=0)
        own_1 = alone[i] + cc * (from_faces + from_ring(ring))
        ring_1 = ring_once[i] + c_r * (to_ring(own) + from_corners)
        face_1 = face_once[i] + c_f * (ends_of(own) + from_ring(corner))
        corner_1 = corner_once[i] + c_x * (ends_of(ring) + to_ring(face))
        own_2 = keep * own_1 + f + cc * (beside(own_1, face_1) + sides(own_1, ring_1) + along_z(own_1))
        ring_2 = ring_twice[i] + keep * ring_1 + c_r * (to_ring(own_1) + beside(ring_1, corner_1) + along_z(ring_1))
        face_2 = face_twice[i] + keep * face_1 + c_f * (ends_of(own_1) + sides(face_1, corner_1) + along_z(face_1))
        field[i] = keep * own_2 + f + cc * (beside(own_2, face_2) + sides(own_2, ring_2) + along_z(own_2))
        return carry

    lax.fori_loop(0, COMP, sweeps, 0, unroll=12)

    flat = field[...].reshape(COMP * 32, 128)
    upper = flat.astype(BF16)
    lower = (flat - upper.astype(F32)).astype(BF16)
    picked = dot(jnp.concatenate([upper, lower], axis=1), ol[...]).reshape(COMP, 32, SLOTS)
    normal = wnorm[...]
    picked = jnp.sum(picked * rowhot[...][None], axis=1)
    traces = normal[0:1] * picked[0:4] + normal[1:2] * picked[4:8] + normal[2:3] * picked[8:12]
    traces = jnp.concatenate([traces, traces], axis=0) * armask[...]
    message = dot_nt(traces.astype(BF16), place[...])

    ra[hi] = message
    for peer in hi_peers:
        remote(ra.at[hi], ra.at[hi], ph_ss.at[0], ph_rs.at[0], peer).start()

    def wait_all(region, at, peer):
        remote(region, region, ph_ss.at[at], ph_rs.at[at], peer).wait_recv()

    wait_all(ra.at[pl.ds(0, NHI - 1)], 0, hi_peers[0])
    for k in range(4):
        g[c, y, k] = jnp.concatenate([ra[:, k], ra[:, 4 + k]], axis=0).astype(BF16)
    for peer in y_peers:
        remote(g.at[c, y], g.at[c, y], ph_ss.at[1], ph_rs.at[1], peer).start()
    row_f = iota((COMP, 8, 128), 1)
    fvol_s[0] = pairs(field[:, 3])
    fvol_s[1] = pairs(field[:, 0])
    for t in (0, 1):
        acc = jnp.zeros((COMP, 8, 128), F32)
        for p in range(4):
            shift = p + 1 if t == 0 else p
            acc = jnp.where(row_f == p, rolled(field[:, p], shift, 1), acc)
        frep_s[t] = pairs(acc)
    fmoves = []
    for s in (0, 1):
        fmoves.append((fvol_s.at[s], fvol_r.at[s], s, (vol_dev[s], r), vol_to[s], vol_from[s]))
        fmoves.append((frep_s.at[s], frep_r.at[s], 2 + s, (v, rep_dev[s]), rep_to[s], rep_from[s]))
    for src, dst, at, dev, sends, comes in fmoves:
        @pl.when(sends)
        def _():
            remote(src, dst, fhalo_ss.at[at], fhalo_rs.at[at], dev).start()

        @pl.when(jnp.logical_not(comes))
        def _():
            dst[...] = jnp.zeros(dst.shape, BF16)


    wait_all(g.at[c, pl.ds(0, NY - 1)], 1, y_peers[0])
    remote(g.at[c], g.at[c], ph_ss.at[2], ph_rs.at[2], core_peer).start()

    wait_all(g.at[c], 2, core_peer)

    pick = sel_t[...]
    chosen = jnp.concatenate([dot_nt(pick, g[:, :, k].reshape(256, 128)) for k in range(4)], axis=0).astype(BF16)
    every = dot(chosen, vdt[...])
    coef = jnp.sum(every.reshape(4, TILES, TQ) * diag_m[...][None], axis=1)
    coef = jnp.concatenate([coef, coef], axis=0)
    spread_c = (jnp.concatenate([coef] * 4, axis=0) * row_m[...]).astype(BF16)
    parts = dot(spread_c, ud[...])
    take = lax.rem(iota((32, 128), 0), 8) < 4
    parts = jnp.where(take, parts[:, 0:128], parts[:, 128:256])
    zs[...] = parts.reshape(4, 8, 128)

    mine_at = zh * NR + r
    for (zh_, r_), peer in zip(z_at, z_peers):
        remote(zs.at[r_], zr.at[mine_at], ph_ss.at[3], ph_rs.at[3], peer).start()
    zr[mine_at] = zs[r]

    wait_all(zr.at[pl.ds(0, 2 * NR - 1)], 3, z_peers[0])
    sums = jnp.sum(zr[...].reshape(NZH, NR, 8, 128), axis=1)
    back = jnp.concatenate([sums.reshape(16, 128), jnp.zeros((112, 128), F32)], axis=0).astype(BF16)
    ws[...] = dot_nt(sel_at[...], back).reshape(NXY, 1, 128)

    for dx, dy, dc in plane_order:
        at = at_x[dx] * NLO + at_y[dy] * NC + at_c[dc]
        remote(ws.at[at], wr.at[here], ph_ss.at[4], ph_rs.at[4], (vol_of(at_x[dx], zh, at_y[dy], at_c[dc]), r)).start()
    wr[here] = ws[here]
    own = jnp.where(zh == 0, sums[0], sums[1])
    wide = jnp.concatenate([own[0:4], own[4:8]], axis=1)
    join = jnp.where(at_g == lax.rem(at_b, 128) * 2 + at_b // 128, 1.0, 0.0)
    out_p[...] = jnp.dot(wide, join, precision=lax.Precision.HIGHEST, preferred_element_type=F32)

    for src, dst, at, dev, sends, comes in fmoves:
        @pl.when(comes)
        def _():
            remote(src, dst, fhalo_ss.at[at], fhalo_rs.at[at], dev).wait_recv()

    low_f, high_f = unpairs(fvol_r[0], (COMP,)), unpairs(fvol_r[1], (COMP,))
    low_y, high_y = unpairs(frep_r[0], (COMP,)), unpairs(frep_r[1], (COMP,))
    for p in range(4):
        w = field[:, p]
        total = (field[:, p - 1] if p > 0 else low_f) + (field[:, p + 1] if p < 3 else high_f)
        before = pltpu.roll(low_y, 8 - p, 1) if p > 0 else low_y
        after = pltpu.roll(high_y, 7 - p, 1)
        total = total + jnp.where(row_f == 0, before, pltpu.roll(w, 1, 1))
        total = total + jnp.where(row_f == 7, after, pltpu.roll(w, 7, 1))
        lane_f = iota((COMP, 8, 128), 2)
        total = total + jnp.where(lane_f == 0, 0.0, pltpu.roll(w, 1, 2))
        total = total + jnp.where(lane_f == 127, 0.0, pltpu.roll(w, 127, 2))
        base[:, p] = keep * w + f_own[:, p] + c_own[p][None] * total

    wait_all(wr.at[pl.ds(0, NXY - 1)], 4, core_peer)

    got = wr[...].reshape(NXY, 128).astype(BF16)
    got = jnp.concatenate([got, jnp.zeros((128 - NXY, 128), BF16)], axis=0)
    per_slot = (dot(at_hot[...], got) * za_hot[...]).astype(BF16)
    wave = onehot(lax.rem(iota((8, 128), 1), 4) == iota((8, 128), 0))
    wet = dot_nt(wave, per_slot)[0:4]
    out_w[...] = wet

    normal = -wnorm[...]
    load = jnp.concatenate([normal[i:i + 1] * wet for i in range(3)], axis=0)
    rows = (load[:, None, :] * rowhot[...][None]).reshape(COMP * 32, SLOTS)
    upper = rows.astype(BF16)
    lower = (rows - upper.astype(F32)).astype(BF16)
    z_one = ol[0:128]
    placed = dot_nt(jnp.concatenate([upper, lower], axis=1), jnp.concatenate([z_one, z_one], axis=1))
    out_u[...] = base[...] + scale[...][None] * placed.reshape(COMP, 4, 8, 128)

    for src, dst, at, dev, sends, comes in moves:
        @pl.when(sends)
        def _():
            remote(src, dst, halo_ss.at[at], halo_rs.at[at], dev).wait_send()
    for src, dst, at, dev, sends, comes in fmoves:
        @pl.when(sends)
        def _():
            remote(src, dst, fhalo_ss.at[at], fhalo_rs.at[at], dev).wait_send()

    def sent(region, at, peer):
        remote(region, region, ph_ss.at[at], ph_rs.at[at], peer).wait_send()

    sent(ra.at[pl.ds(0, NHI - 1)], 0, hi_peers[0])
    sent(g.at[c, pl.ds(0, NY - 1)], 1, y_peers[0])
    sent(g.at[c], 2, core_peer)
    sent(zr.at[pl.ds(0, 2 * NR - 1)], 3, z_peers[0])
    sent(wr.at[pl.ds(0, NXY - 1)], 4, core_peer)


def hand_out(u, p, w, out_u, out_p, out_w):
    out_u[...] = u[...]
    out_p[...] = p[...]
    out_w[...] = w[...]


def shards(displacement, body_force, stiffness, wet_cell, wet_normal, route, tile_u, tile_v, tile_row, tile_col, tile_rank):
    vmem = pl.BlockSpec(memory_space=pltpu.VMEM)
    hbm = pl.BlockSpec(memory_space=pltpu.HBM)
    V = pltpu.VMEM
    updated, pressure, wet = pl.pallas_call(
        body,
        out_shape=(
            jax.ShapeDtypeStruct((COMP, 4, 8, 128), F32),
            jax.ShapeDtypeStruct((4, 256), F32),
            jax.ShapeDtypeStruct((4, SLOTS), F32),
        ),
        in_specs=[hbm] * 11,
        out_specs=(vmem, vmem, vmem),
        scratch_shapes=[
            V((COMP, 4, 8, 128), F32), V((COMP, 4, 8, 128), F32), V((4, 8, 128), F32),
            V((1, SLOTS), I32), V((3, SLOTS), F32), V((1, SLOTS), I32),
            V((TILES, RANK, 256), BF16), V((TILES, RANK, 256), BF16),
            V((1, TILES), I32), V((1, TILES), I32), V((1, TILES), I32),
            V((2, 19, 16, 128), BF16), V((2, 19, 16, 128), BF16),
            V((2, 10, 16, 128), BF16), V((2, 10, 16, 128), BF16),
            V((2, 2, 4, 16, 128), BF16), V((2, 2, 4, 16, 128), BF16),
            V((2, 6, 16, 128), BF16), V((2, 6, 16, 128), BF16),
            V((2, 6, 16, 128), BF16), V((2, 6, 16, 128), BF16),
            V((COMP, 4, 8, 128), F32), V((COMP, 4, 8, 128), F32), V((4, 8, 128), F32),
            V((COMP, 4, 8, 128), F32), V((COMP, 4, 8, 128), F32), V((COMP, 4, 8, 128), F32), V((4, 8, 128), F32),
            V((COMP, 2, 8, 128), F32), V((COMP, 2, 8, 128), F32), V((COMP, 2, 8, 128), F32), V((2, 8, 128), F32),
            V((COMP, 2, 8, 128), F32), V((COMP, 2, 8, 128), F32), V((2, 8, 128), F32),
            V((COMP, 4, 8, 128), F32), V((COMP, 4, 8, 128), F32), V((4, 8, 128), F32),
            V((256, TQ), BF16), V((TQ, 256), BF16), V((256, SLOTS), BF16), V((32, SLOTS), F32),
            V((8, SLOTS), F32), V((128, SLOTS), BF16), V((TILES, 128), BF16), V((TILES, TQ), F32),
            V((32, TQ), F32), V((NXY, NV), BF16), V((SLOTS, 128), BF16), V((SLOTS, 128), F32),
            V((NHI, 8, 128), F32), V((NC, NY, 4, 16, 128), BF16),
            V((NR, 8, 128), F32), V((NZH * NR, 8, 128), F32),
            V((NXY, 1, 128), F32), V((NXY, 1, 128), F32),
            pltpu.SemaphoreType.DMA((11,)),
            pltpu.SemaphoreType.DMA((8,)), pltpu.SemaphoreType.DMA((8,)),
            pltpu.SemaphoreType.DMA((4,)), pltpu.SemaphoreType.DMA((4,)),
            pltpu.SemaphoreType.DMA((5,)), pltpu.SemaphoreType.DMA((5,)),
        ],
        compiler_params=pltpu.CompilerParams(collective_id=0, has_side_effects=True, vmem_limit_bytes=40 << 20),
    )(
        *(
            pltpu.with_memory_space_constraint(array, pltpu.HBM)
            for array in (
                displacement.reshape(COMP, 4, 8, 128),
                body_force.reshape(COMP, 4, 8, 128),
                stiffness,
                wet_cell,
                wet_normal,
                route.reshape(1, SLOTS),
                tile_u,
                tile_v,
                tile_row.reshape(1, TILES),
                tile_col.reshape(1, TILES),
                tile_rank.reshape(1, TILES),
            )
        )
    )
    updated, pressure, wet = pl.pallas_call(
        hand_out,
        out_shape=(
            jax.ShapeDtypeStruct((COMP, 4, 8, 128), F32),
            jax.ShapeDtypeStruct((4, 256), F32),
            jax.ShapeDtypeStruct((4, SLOTS), F32),
        ),
        in_specs=[vmem] * 3,
        out_specs=(vmem, vmem, vmem),
        compiler_params=pltpu.CompilerParams(vmem_limit_bytes=16 << 20),
    )(updated, pressure, wet)
    return updated.reshape(displacement.shape), pressure, wet


def solution(mesh):
    return jax.shard_map(
        shards,
        mesh=mesh,
        in_specs=(
            P(None, None, "vol", "rep", None),
            P(None, None, "vol", "rep", None),
            P("vol", "rep", None),
            P(("vol", "rep"), None),
            P(None, ("vol", "rep")),
            P(("vol", "rep"), None),
            P(("vol", "rep"), None, None),
            P(("vol", "rep"), None, None),
            P(("vol", "rep")),
            P(("vol", "rep")),
            P(("vol", "rep")),
        ),
        out_specs=(
            P(None, None, "vol", "rep", None),
            P(None, ("vol", "rep")),
            P(None, ("vol", "rep")),
        ),
        check_vma=False,
    )
```
